32 devices in a mesh: ctx: 8 (over y, x, core), fsdp: 4 (over z).
Axes of the slice: x: 2, y: 2, z: 4, core: 2. Of those that a mesh axis runs over, the one named last changes fastest.
Arguments:
- hidden_in: bfloat16 [4, 1536, 2048], P('fsdp', 'ctx'), may hold values from -6 to 6
- cotangent: bfloat16 [4, 1536, 2048], P('fsdp', 'ctx'), may hold values from -6 to 6
- routes: int32 [4, 1536, 8], P('fsdp', 'ctx'), may hold values from 0 to 31, all different within a row; in each aligned block of 192 rows (0 to 191, 192 to 383, ..., all dimensions but the last counted through in order) at most 64 rows name the same one
- attn_gain: bfloat16 [2048], P(('ctx', 'fsdp')), may hold values from 0.25 to 1.75
- query_gain: bfloat16 [2048], P(('ctx', 'fsdp')), may hold values from 0.25 to 1.75
- key_gain: bfloat16 [2048], P(('ctx', 'fsdp')), may hold values from 0.25 to 1.75
- ffn_gain: bfloat16 [2048], P(('ctx', 'fsdp')), may hold values from 0.25 to 1.75
- w_query: bfloat16 [2048, 2048], P(('ctx', 'fsdp')), may hold values from -0.125 to 0.125
- w_key: bfloat16 [2048, 2048], P(('ctx', 'fsdp')), may hold values from -0.125 to 0.125
- w_value: bfloat16 [2048, 2048], P(('ctx', 'fsdp')), may hold values from -0.125 to 0.125
- w_out: bfloat16 [2048, 2048], P(('ctx', 'fsdp')), may hold values from -0.5 to 0.5
- w_router: bfloat16 [2048, 32], P(('ctx', 'fsdp')), may hold values from -0.0625 to 0.0625
- w_gate: bfloat16 [32, 2048, 1024], P('ctx', 'fsdp'), may hold values from -0.125 to 0.125
- w_up: bfloat16 [32, 2048, 1024], P('ctx', 'fsdp'), may hold values from -0.125 to 0.125
- w_down: bfloat16 [32, 1024, 2048], P('ctx', 'fsdp'), may hold values from -0.75 to 0.75
Outputs:
- out_hidden: bfloat16 [4, 1536, 2048], P('fsdp', 'ctx')
- grad_hidden: float32 [4, 1536, 2048], P('fsdp', 'ctx')
- grad_attn_gain: float32 [2048], P(('ctx', 'fsdp'))
- grad_query_gain: float32 [2048], P(('ctx', 'fsdp'))
- grad_key_gain: float32 [2048], P(('ctx', 'fsdp'))
- grad_ffn_gain: float32 [2048], P(('ctx', 'fsdp'))
- grad_query: float32 [2048, 2048], P(('ctx', 'fsdp'))
- grad_key: float32 [2048, 2048], P(('ctx', 'fsdp'))
- grad_value: float32 [2048, 2048], P(('ctx', 'fsdp'))
- grad_out: float32 [2048, 2048], P(('ctx', 'fsdp'))
- grad_router: float32 [2048, 32], P(('ctx', 'fsdp'))
- grad_gate: float32 [32, 2048, 1024], P('ctx', 'fsdp')
- grad_up: float32 [32, 2048, 1024], P('ctx', 'fsdp')
- grad_down: float32 [32, 1024, 2048], P('ctx', 'fsdp')
The draws below stay inside these ranges and needn't reach their ends.
Inputs may be any that keep to these rules, and one draw needn't show every extreme that they name: `routes`: each row names 8 different experts. In each aligned block of 192 tokens (the tokens of one device), no expert is named by more than 64 tokens, a bound that some block reaches.
All inputs are finite; a program needn't handle non-finite values.
Results may differ from the reference program's by a relative error of at most 0.018.
Values may be sent and summed in bfloat16 or wider, within the bound.
A program may use at most 384 MiB of HBM per device.

```python
import math
import jax
import jax.numpy as jnp
import numpy as np
from jax import lax

D = 2048
HEADS = 16
HD = 128
F = 1024
TOP = 8
TOK_DEV = 192
EXPERTS = 32
LEN = 1536
SEQS = 4
CAP = 64
N_CTX = 8


def block_scale(own_key, dims, pieces, smallest, top_value):
    loudness, own = 1.0, jax.random.fold_in(own_key, 6)
    for dim, blocks in pieces:
        steps = jnp.exp(jax.random.uniform(jax.random.fold_in(own, dim), (blocks,), jnp.float32, smallest / len(pieces), top_value / len(pieces)))
        loudness = loudness * jnp.repeat(steps, dims[dim] // blocks).reshape([-1 if axis == dim else 1 for axis in range(len(dims))])
    return loudness


def assign_block(stream_key, own, number, rows, number_of, top, bound, skew):
    order = jax.random.permutation(stream_key, number_of)
    heavy_load, common = portions_of(number_of, rows * top, bound, skew, True), portions_of(number_of, rows * top, bound, skew, False)
    places = jnp.arange(number_of)

    def named(sizes, turn):
        used = int((sizes > 0).sum())
        fixed = max(1, used // 4)
        moved = fixed + (places - fixed + turn * (used - fixed)) % max(1, number_of - fixed)
        return jnp.zeros((number_of,), jnp.int32).at[order[jnp.where(places < fixed, places, moved)]].set(jnp.asarray(sizes, jnp.int32))

    sizes = jnp.where(number % 4 == 0, named(heavy_load, number // 4), named(common, number - number // 4 - 1))
    mixed = jax.random.permutation(jax.random.fold_in(own, 3), number_of)
    giver, taker = mixed[0:number_of // 2 * 2:2], mixed[1:number_of // 2 * 2:2]
    slack = jnp.minimum(sizes[giver] - 1, bound - sizes[taker]) // 2
    slack = jnp.where((giver == order[0]) | (taker == order[0]) | (sizes[taker] == 0), 0, jnp.maximum(slack, 0))
    moved = jax.random.randint(jax.random.fold_in(own, 4), (number_of // 2,), 0, 1 << 20) % (slack + 1)
    sizes = sizes.at[giver].add(-moved).at[taker].add(moved)
    labels = jnp.searchsorted(jnp.cumsum(sizes), jnp.arange(rows * top), side="right").astype(jnp.int32)
    listing = labels.reshape(top, rows).T
    listing = listing[jax.random.permutation(jax.random.fold_in(own, 1), rows)]
    turn = jax.random.randint(jax.random.fold_in(own, 2), (rows, 1), 0, top)
    return jnp.take_along_axis(listing, (jnp.arange(top)[None, :] + turn) % top, axis=1)


def portions_of(number_of, total, bound, skew, full):
    portions = [(1 << 20) // math.isqrt(standing ** skew) + 1 for standing in range(1, number_of + 1)]
    largest = bound if full else min(bound, max(-(-total // number_of), total * portions[0] // sum(portions)))
    least = 1 if total - largest >= number_of - 1 else 0
    given, rest = [largest] + [least] * (number_of - 1), total - largest - least * (number_of - 1)
    while rest > 0:
        candidates = [i for i in range(1, number_of) if given[i] < largest] or [i for i in range(1, number_of) if given[i] < bound]
        mass, budget = sum([portions[i] for i in candidates]), rest
        for i in candidates:
            addition = min(bound - given[i], max(1, budget * portions[i] // mass), rest)
            given[i] = given[i] + addition
            rest = rest - addition
    return np.array(given)


def normal_values(own_key, dims, deviation, limit, cuts=(), kind=jnp.bfloat16):
    values = jax.random.normal(own_key, dims, jnp.float32) * deviation
    if len(cuts) > 0:
        values = block_scale(own_key, dims, cuts, -0.22, 0.18) * values
    return jnp.clip(values, min=-limit, max=limit).astype(kind)


def setup_inputs(seed: int = 0) -> dict:
    arg_keys = jax.random.split(jax.random.key(seed), 16)
    hidden_in = normal_values(arg_keys[0], (SEQS, LEN, D), 1.0, 6.0, ((0, 4), (1, 8)))
    cotangent = normal_values(arg_keys[1], (SEQS, LEN, D), 1.0, 6.0, ((0, 4), (1, 8)))
    routes_keys = jax.random.split(jax.random.fold_in(arg_keys[2], 1), SEQS * LEN // TOK_DEV)
    routes_turns = jax.random.permutation(jax.random.fold_in(arg_keys[2], 3), SEQS * LEN // TOK_DEV)
    routes = jax.vmap(lambda own, number: assign_block(jax.random.fold_in(arg_keys[2], 2), own, number, TOK_DEV, EXPERTS, TOP, CAP, 2))(routes_keys, routes_turns).reshape((SEQS, LEN, TOP))
    attn_gain = jnp.clip(1.0 + 0.15 * jax.random.normal(arg_keys[3], (D,), jnp.float32), 0.25, 1.75).astype(jnp.bfloat16)
    query_gain = jnp.clip(1.0 + 0.15 * jax.random.normal(arg_keys[4], (D,), jnp.float32), 0.25, 1.75).astype(jnp.bfloat16)
    key_gain = jnp.clip(1.0 + 0.15 * jax.random.normal(arg_keys[5], (D,), jnp.float32), 0.25, 1.75).astype(jnp.bfloat16)
    ffn_gain = jnp.clip(1.0 + 0.15 * jax.random.normal(arg_keys[6], (D,), jnp.float32), 0.25, 1.75).astype(jnp.bfloat16)
    w_query = normal_values(arg_keys[7], (D, D), D ** -0.5, 0.125, ((0, 32),))
    w_key = normal_values(arg_keys[8], (D, D), D ** -0.5, 0.125, ((0, 32),))
    w_value = normal_values(arg_keys[9], (D, D), D ** -0.5, 0.125, ((0, 32),))
    w_out = normal_values(arg_keys[10], (D, D), (D // 16) ** -0.5, 0.5, ((0, 32),))
    w_router = normal_values(arg_keys[11], (D, EXPERTS), (4 * D) ** -0.5, 0.0625, ((0, 32),))
    w_gate = normal_values(arg_keys[12], (EXPERTS, D, F), D ** -0.5, 0.125, ((0, 8), (1, 4)))
    w_up = normal_values(arg_keys[13], (EXPERTS, D, F), D ** -0.5, 0.125, ((0, 8), (1, 4)))
    w_down = normal_values(arg_keys[14], (EXPERTS, F, D), (F // 16) ** -0.5, 0.75, ((0, 8), (1, 4)))
    return dict(hidden_in=hidden_in, cotangent=cotangent, routes=routes, attn_gain=attn_gain, query_gain=query_gain, key_gain=key_gain, ffn_gain=ffn_gain, w_query=w_query, w_key=w_key, w_value=w_value, w_out=w_out, w_router=w_router, w_gate=w_gate, w_up=w_up, w_down=w_down)


@jax.custom_vjp
def low(v):
    return lax.optimization_barrier(v.astype(jnp.bfloat16)).astype(jnp.float32)

@jax.custom_vjp
def low_back(v):
    return v

def low_keep(v):
    return (low(v), None)

def low_pass(kept, grad):
    return (grad,)

def back_keep(v):
    return (v, None)

def back_low(kept, grad):
    return (low(grad),)
low.defvjp(low_keep, low_pass)
low_back.defvjp(back_keep, back_low)
highest = lax.Precision.HIGHEST
epsilon = 1e-05

def normalize(vector):
    return vector * lax.rsqrt(lax.optimization_barrier(jnp.mean(vector * vector, axis=-1, keepdims=True)) + epsilon)

def token_position(index):
    half = TOK_DEV // 2
    device = index // TOK_DEV
    local = index % TOK_DEV
    return jnp.where(local < half, device * half + local, (2 * N_CTX - 1 - device) * half + local - half).astype(jnp.int32)

def rotation(positions):
    half = HD // 2
    freq = 10000.0 ** (-jnp.arange(half, dtype=jnp.float32) * (2.0 / HD))
    angle = positions[:, None] * freq[None, :]
    return (jnp.cos(angle)[:, None, :], jnp.sin(angle)[:, None, :])

def rotate(vector, cosine, sine):
    half = vector.shape[-1] // 2
    first = vector[..., :half]
    second = vector[..., half:]
    return jnp.concatenate([first * cosine - second * sine, second * cosine + first * sine], axis=-1)

def matmul(left, right):
    return jnp.dot(left, right, precision=highest, preferred_element_type=jnp.float32)

def attend_block(query_block, start, keys, values):
    block_rows = query_block.shape[0]
    scores = jnp.einsum('qhd,khd->hqk', query_block, keys, precision=highest) * HD ** (-0.5)
    scores = low_back(scores)
    query_pos = token_position(start + jnp.arange(block_rows, dtype=jnp.int32))
    key_pos = token_position(jnp.arange(keys.shape[0], dtype=jnp.int32))
    allowed = key_pos[None, :] <= query_pos[:, None]
    scores = jnp.where(allowed[None], scores, -1e+30)
    probs = low(jax.nn.softmax(scores, axis=-1))
    return jnp.einsum('hqk,khd->qhd', probs, values, precision=highest)

def attend_sequence(inputs):
    queries, keys, values = inputs
    block = math.gcd(LEN, 512)
    starts = jnp.arange(LEN // block, dtype=jnp.int32) * block
    blocks = queries.reshape(LEN // block, block, HEADS, HD)

    def one_block(pair):
        return attend_block(pair[0], pair[1], keys, values)
    return lax.map(jax.checkpoint(one_block), (blocks, starts)).reshape(LEN, HEADS, HD)

def expert_apply(inputs):
    rows, gate_weight, up_weight, down_weight = inputs
    gate_pre = low_back(matmul(rows, gate_weight))
    up_pre = low_back(matmul(rows, up_weight))
    inner = low(jax.nn.silu(gate_pre) * up_pre)
    return low(low_back(matmul(inner, down_weight)))

def reference(hidden_in, cotangent, routes, attn_gain, query_gain, key_gain, ffn_gain, w_query, w_key, w_value, w_out, w_router, w_gate, w_up, w_down):
    total_rows = SEQS * LEN
    route_rows = routes.reshape(total_rows, TOP).astype(jnp.int32)
    blocks = total_rows // TOK_DEV
    ident = route_rows.reshape(blocks, TOK_DEV * TOP)
    onehot = (ident[..., None] == jnp.arange(EXPERTS, dtype=jnp.int32)).astype(jnp.int32)
    rank = lax.optimization_barrier(jnp.sum(jnp.cumsum(onehot, axis=1) * onehot, axis=-1)) - 1
    slot = ((jnp.arange(blocks, dtype=jnp.int32)[:, None] * EXPERTS + ident) * CAP + rank).reshape(-1).astype(jnp.int32)
    entries = total_rows * TOP
    slot_entry = jnp.full((blocks * EXPERTS * CAP,), entries, jnp.int32).at[slot].set(jnp.arange(entries, dtype=jnp.int32))
    slot_token = (slot_entry // TOP).astype(jnp.int32)

    def forward(rows, params):
        gain_attn, gain_query, gain_key, gain_ffn, query_weight, key_weight, value_weight, out_weight, router_weight, gate_weight, up_weight, down_weight = params
        normed = low(normalize(rows) * gain_attn)
        queries = low_back(matmul(normed, query_weight))
        keys = low_back(matmul(normed, key_weight))
        values = low_back(matmul(normed, value_weight))
        positions = jnp.tile(token_position(jnp.arange(LEN, dtype=jnp.int32)).astype(jnp.float32), SEQS)
        cosine, sine = rotation(positions)
        q_rot = low(rotate((normalize(queries) * gain_query).reshape(total_rows, HEADS, HD), cosine, sine))
        k_rot = low(rotate((normalize(keys) * gain_key).reshape(total_rows, HEADS, HD), cosine, sine))
        v_low = low(values).reshape(total_rows, HEADS, HD)
        mixed = lax.map(jax.checkpoint(attend_sequence), (q_rot.reshape(SEQS, LEN, HEADS, HD), k_rot.reshape(SEQS, LEN, HEADS, HD), v_low.reshape(SEQS, LEN, HEADS, HD)))
        attended = low(low_back(mixed.reshape(total_rows, D)))
        resid = rows + low_back(matmul(attended, out_weight))
        ffn_in = low(normalize(resid) * gain_ffn)
        logits = low_back(matmul(ffn_in, router_weight))
        chosen = jnp.take_along_axis(logits, route_rows, axis=1)
        gates = jax.nn.softmax(chosen, axis=-1)
        padded = jnp.concatenate([ffn_in, jnp.zeros((1, D), ffn_in.dtype)], axis=0)
        dispatched = low_back(padded[slot_token])
        per_expert = dispatched.reshape(blocks, EXPERTS, CAP, D).transpose(1, 0, 2, 3).reshape(EXPERTS, blocks * CAP, D)
        produced = lax.map(jax.checkpoint(expert_apply), (per_expert, gate_weight, up_weight, down_weight))
        returned = produced.reshape(EXPERTS, blocks, CAP, D).transpose(1, 0, 2, 3).reshape(-1, D)
        picked = returned[slot].reshape(total_rows, TOP, D)
        return resid + lax.optimization_barrier(jnp.sum(gates[:, :, None] * picked, axis=1))
    params = tuple((weight.astype(jnp.float32) for weight in (attn_gain, query_gain, key_gain, ffn_gain, w_query, w_key, w_value, w_out, w_router, w_gate, w_up, w_down)))
    rows = hidden_in.astype(jnp.float32).reshape(total_rows, D)
    result, pullback = jax.vjp(forward, rows, params)
    grad_rows, grads = pullback(cotangent.astype(jnp.float32).reshape(total_rows, D))
    return (result.astype(jnp.bfloat16).reshape(SEQS, LEN, D), grad_rows.reshape(SEQS, LEN, D), grads[0], grads[1], grads[2], grads[3], grads[4], grads[5], grads[6], grads[7], grads[8], grads[9], grads[10], grads[11])
```

```python
import jax
import jax.numpy as jnp
from jax import lax
from jax.sharding import PartitionSpec as P

HEADS = 16


epsilon = 1e-05
neg_large = -1e30
low = jnp.bfloat16
exact = jnp.float32


def swap(x, axis, bit):
    length = lax.axis_size(axis)
    return lax.ppermute(x, axis, [(i, i ^ bit) for i in range(length)])


def bits_of(axis):
    length = lax.axis_size(axis)
    return [1 << i for i in range(length.bit_length() - 1)]


def doubled(x, axis, bits):
    index = lax.axis_index(axis)
    for bit in bits:
        other = swap(x, axis, bit)
        high = (index & bit) != 0
        x = jnp.stack([jnp.where(high, other, x), jnp.where(high, x, other)])
    count = len(bits)
    order = sorted(range(count), key=lambda i: -bits[count - 1 - i])
    x = x.transpose(order + list(range(count, x.ndim)))
    return x.reshape((1 << count,) + x.shape[count:])


def gather_ctx(x):
    bits = bits_of("ctx")
    half = x.shape[-1] // 2
    far = bits[1:]
    one = doubled(x[..., :half], "ctx", far + bits[:1])
    two = doubled(x[..., half:], "ctx", far[::-1] + bits[:1])
    return jnp.concatenate([one, two], axis=-1)


def halved(x, axis, bits):
    index = lax.axis_index(axis)
    count = len(bits)
    x = x.reshape((2,) * count + x.shape[1:])
    left = sorted(bits, reverse=True)
    for bit in bits:
        at = left.index(bit)
        left.remove(bit)
        zero = lax.index_in_dim(x, 0, at, keepdims=False)
        one = lax.index_in_dim(x, 1, at, keepdims=False)
        high = (index & bit) != 0
        got = swap(jnp.where(high, zero, one).astype(low), axis, bit)
        x = jnp.where(high, one, zero).astype(exact) + got.astype(exact)
    return x


def scatter_ctx(x):
    bits = bits_of("ctx")
    half = x.shape[-1] // 2
    far = bits[1:]
    one = halved(x[..., :half], "ctx", bits[:1] + far)
    two = halved(x[..., half:], "ctx", bits[:1] + far[::-1])
    return jnp.concatenate([one, two], axis=-1)


def near_first(x):
    blocks = {0: x}
    for bit in bits_of("fsdp")[::-1]:
        for key in sorted(blocks):
            blocks[key | bit] = swap(blocks[key], "fsdp", bit)
    return [blocks[key] for key in sorted(blocks)]


def back_home(parts):
    parts = [part.astype(exact) for part in parts]
    for bit in bits_of("fsdp"):
        for key in range(len(parts)):
            if key & bit and not key & (bit - 1):
                got = swap(parts[key].astype(low), "fsdp", bit)
                parts[key ^ bit] = parts[key ^ bit] + got.astype(exact)
    return parts[0]


def exchange(x, axis):
    return lax.all_to_all(x, axis, split_axis=0, concat_axis=0, tiled=True)


def rms_apply(vector, gain):
    scale = lax.rsqrt(jnp.mean(vector * vector, axis=-1, keepdims=True) + epsilon)
    normed = vector * scale
    return (normed * gain, normed, scale)


def rms_back(grad, normed, scale, gain):
    dnormed = grad * gain
    gain_grad = jnp.sum(grad * normed, axis=0)
    inner = jnp.mean(dnormed * normed, axis=-1, keepdims=True)
    return (scale * (dnormed - normed * inner), gain_grad)


def rotation(positions, head_size):
    half = head_size // 2
    freq = 10000.0 ** (-jnp.arange(half, dtype=jnp.float32) * (2.0 / head_size))
    angle = positions.astype(jnp.float32)[:, None] * freq[None, :]
    return (jnp.cos(angle)[:, None, :], jnp.sin(angle)[:, None, :])


def rotate(vector, cosine, sine):
    half = vector.shape[-1] // 2
    first = vector[..., :half]
    second = vector[..., half:]
    return jnp.concatenate(
        [first * cosine - second * sine, second * cosine + first * sine], axis=-1
    )


def dot(left, right):
    return jnp.dot(left, right, preferred_element_type=exact)


def contract_rows(left, right):
    return lax.dot_general(
        left, right, (((0,), (0,)), ((), ())), preferred_element_type=exact
    )


def contract_cols(left, right):
    return lax.dot_general(
        left, right, (((1,), (1,)), ((), ())), preferred_element_type=exact
    )


def ordered(x, ctx_count):
    x = x.reshape((ctx_count, 2, -1) + x.shape[1:])
    x = jnp.concatenate([x[:, 0], x[::-1, 1]], axis=0)
    return x.reshape((-1,) + x.shape[2:])


def placed(x, ctx_count):
    x = x.reshape((2 * ctx_count, -1) + x.shape[1:])
    x = jnp.stack([x[:ctx_count], x[ctx_count:][::-1]], axis=1)
    return x.reshape((-1,) + x.shape[3:])


def body(
    hidden_in,
    cotangent,
    routes,
    attn_gain,
    query_gain,
    key_gain,
    ffn_gain,
    w_query,
    w_key,
    w_value,
    w_out,
    w_router,
    w_gate,
    w_up,
    w_down,
):
    tokens = hidden_in.shape[1]
    width = hidden_in.shape[2]
    head_size = width // HEADS
    ctx_count = lax.axis_size("ctx")
    z_count = lax.axis_size("fsdp")
    both = ("ctx", "fsdp")
    top = routes.shape[2]
    exp_local = w_gate.shape[0]
    split = z_count // exp_local
    hidden = w_gate.shape[2]
    part = hidden // split
    experts = exp_local * ctx_count
    capacity = tokens * top * 4 // (3 * experts)
    heads = HEADS // ctx_count
    cols = heads * head_size
    length = tokens * ctx_count
    scale = head_size ** (-0.5)
    c_index = lax.axis_index("ctx")
    z_index = lax.axis_index("fsdp")
    rows_w = w_query.shape[0]

    qkv = jnp.stack([w_query, w_key, w_value], axis=1).reshape(rows_w, 3, ctx_count, cols)
    qkv = exchange(qkv.transpose(2, 0, 1, 3), "ctx")
    qkv = doubled(qkv, "fsdp", bits_of("fsdp")[::-1])
    qkv = qkv.transpose(1, 0, 2, 3, 4).reshape(width, 3 * cols)
    gains = jnp.stack([attn_gain, query_gain, key_gain, ffn_gain])
    small = jnp.concatenate([gains.reshape(-1), w_router.reshape(-1)])
    small = exchange(
        jnp.broadcast_to(small[None], (ctx_count * z_count, small.shape[0])), both
    )
    gains = small[:, : 4 * rows_w].reshape(-1, 4, rows_w).transpose(1, 0, 2).reshape(4, width)
    router_full = small[:, 4 * rows_w :].reshape(width, experts)
    gains = gains.astype(exact)
    attn_scale, query_scale, key_scale, ffn_scale = gains[0], gains[1], gains[2], gains[3]
    query_scale = lax.dynamic_slice_in_dim(query_scale, c_index * cols, cols)
    key_scale = lax.dynamic_slice_in_dim(key_scale, c_index * cols, cols)

    x_all = gather_ctx(hidden_in[0]).reshape(length, width)
    attn_all = rms_apply(x_all.astype(exact), attn_scale)[0].astype(low)

    routes_all = lax.all_gather(routes[0], both, axis=0)
    multi_all = jnp.sum(
        (routes_all[..., None] == jnp.arange(experts, dtype=jnp.int32)).astype(exact), axis=2
    ).reshape(ctx_count, z_count, tokens, experts)
    own_expert = c_index * exp_local + z_index // split
    lower = (
        jnp.arange(tokens)[:, None] >= jnp.arange(tokens)[None, :]
    ).astype(low)

    def slots(mask):
        rank = jnp.einsum("ts,bs->bt", lower, mask.astype(low), preferred_element_type=exact)
        rank = rank.astype(jnp.int32) - 1
        hit = rank[:, None, :] == jnp.arange(capacity, dtype=jnp.int32)[None, :, None]
        return (hit & (mask[:, None, :] > 0)).astype(low)

    multi_own = lax.dynamic_index_in_dim(multi_all, c_index, 0, False)
    sends = []
    metas = []
    for step in range(z_count):
        source = z_index ^ step
        multi = lax.dynamic_index_in_dim(multi_own, source, 0, False)
        plane = multi.reshape(tokens, ctx_count, exp_local)
        plane = lax.dynamic_index_in_dim(plane, z_index // split, 2, False)
        sends.append(slots(plane.T))
        there = lax.dynamic_index_in_dim(multi_all, source, 1, False)
        mine = lax.dynamic_index_in_dim(there, own_expert, 2, False)
        metas.append(
            jnp.einsum(
                "crt,cte->cre", slots(mine), there.astype(low), preferred_element_type=exact
            )
        )
    meta = jnp.stack(metas).reshape(-1, experts)

    def pick(hot, block):
        rows = jnp.einsum("crt,td->crd", hot, block, preferred_element_type=exact)
        return rows.astype(low)

    cot_near = near_first(cotangent[0])
    cot_sent = [pick(hot, block) for hot, block in zip(sends, cot_near)]
    cot_rows = jnp.stack([exchange(rows, "ctx") for rows in cot_sent]).reshape(-1, width)

    def whole_in(weight):
        rows = weight.shape[1]
        weight = weight.reshape(exp_local, rows, z_count, split, part // z_count)
        weight = weight.transpose(0, 3, 1, 2, 4).reshape(z_count, rows, part)
        return exchange(weight, "fsdp").reshape(z_count * rows, part)

    gate_full = whole_in(w_gate)
    up_full = whole_in(w_up)
    rows_d = w_down.shape[1]
    down_full = exchange(
        w_down.reshape(z_count, rows_d // split, width), "fsdp"
    ).reshape(part, width)

    projected = dot(attn_all, qkv)
    queries, keys, values = (
        projected[:, :cols],
        projected[:, cols : 2 * cols],
        projected[:, 2 * cols :],
    )

    def total_over_ctx(one, two):
        both_sums = jnp.stack([one, two])
        return jnp.sum(lax.all_gather(both_sums, "ctx", axis=0), axis=0)

    squares = total_over_ctx(jnp.sum(queries * queries, -1), jnp.sum(keys * keys, -1))
    rms_two = lax.rsqrt(squares / width + epsilon)
    query_rms, key_rms = rms_two[0][:, None], rms_two[1][:, None]
    query_normed, key_normed = queries * query_rms, keys * key_rms
    half = tokens // 2
    row = jnp.arange(length, dtype=jnp.int32)
    device, local = row // tokens, row % tokens
    positions = jnp.where(
        local < half, device * half + local, (2 * ctx_count - 1 - device) * half + local - half
    )
    cosine, sine = rotation(positions, head_size)

    def by_head(x):
        return x.reshape(length, heads, head_size)

    query_rot = ordered(rotate(by_head(query_normed * query_scale), cosine, sine).astype(low), ctx_count)
    key_rot = ordered(rotate(by_head(key_normed * key_scale), cosine, sine).astype(low), ctx_count)
    value_low = ordered(by_head(values.astype(low)), ctx_count)
    allowed = (row[None, :] <= row[:, None])[None]
    scores = (
        jnp.einsum("qhd,khd->hqk", query_rot, key_rot, preferred_element_type=exact) * scale
    )
    scores = jnp.where(allowed, scores, neg_large)
    log_total = jax.nn.logsumexp(scores, axis=-1, keepdims=True)
    probs = jnp.exp(scores - log_total)
    probs_low = probs.astype(low)
    mixed = jnp.einsum("hqk,khd->qhd", probs_low, value_low, preferred_element_type=exact)
    out_heads = placed(mixed.astype(low).reshape(length, cols), ctx_count)
    out_low = exchange(out_heads.reshape(ctx_count, tokens, cols), "ctx")
    out_low = out_low.transpose(1, 0, 2).reshape(tokens, width)
    out_full = doubled(w_out, "fsdp", bits_of("fsdp")[::-1]).reshape(cols, width)
    out_full = gather_ctx(out_full).reshape(width, width)
    rows_in = hidden_in[0].astype(exact)
    resid_one = rows_in + dot(out_low, out_full)
    hidden_two, normed_two, scale_two = rms_apply(resid_one, ffn_scale)
    ffn_input = hidden_two.astype(low)

    input_near = near_first(ffn_input)
    input_rows = jnp.stack(
        [exchange(pick(hot, block), "ctx") for hot, block in zip(sends, input_near)]
    ).reshape(-1, width)

    def routed_softmax(rows, multi):
        logits = jnp.where(multi > 0, dot(rows, router_full), neg_large)
        top_value = jnp.max(logits, axis=-1, keepdims=True)
        weight = jnp.exp(logits - top_value)
        return weight / jnp.sum(weight, axis=-1, keepdims=True)

    row_gates = routed_softmax(input_rows, meta)
    row_gate = lax.dynamic_slice_in_dim(row_gates, own_expert, 1, 1)
    deout = (row_gate * cot_rows.astype(exact)).astype(low)
    gate_pre = dot(input_rows, gate_full)
    up_pre = dot(input_rows, up_full)
    sigmoid_gate = jax.nn.sigmoid(gate_pre)
    activated = gate_pre * sigmoid_gate
    inner_low = (activated * up_pre).astype(low)
    produced = dot(inner_low, down_full).astype(low)
    inner_grad = contract_cols(deout, down_full)
    gate_pre_grad = (
        inner_grad * up_pre * sigmoid_gate * (1.0 + gate_pre * (1.0 - sigmoid_gate))
    ).astype(low)
    up_pre_grad = (inner_grad * activated).astype(low)
    droute = (
        contract_cols(gate_pre_grad, gate_full) + contract_cols(up_pre_grad, up_full)
    ).astype(low)
    down_grad = contract_rows(inner_low, deout).astype(low)
    gate_grad = contract_rows(input_rows, gate_pre_grad).astype(low)
    up_grad = contract_rows(input_rows, up_pre_grad).astype(low)

    def whole_out(grad):
        rows = grad.shape[0] // z_count
        grad = exchange(grad.reshape(z_count, rows, part), "fsdp")
        grad = grad.reshape(exp_local, split, rows, z_count, part // z_count)
        return grad.transpose(0, 2, 3, 1, 4).reshape(exp_local, rows, hidden).astype(exact)

    grad_down = (
        exchange(down_grad.reshape(z_count, rows_d // split, width), "fsdp")
        .reshape(exp_local, rows_d, width)
        .astype(exact)
    )
    grad_gate = whole_out(gate_grad)
    grad_up = whole_out(up_grad)

    shape = (z_count, ctx_count, capacity, width)
    produced = produced.reshape(shape)
    droute = droute.reshape(shape)
    out_parts = []
    in_parts = []
    gate_sums = []
    for step in range(z_count):
        source = z_index ^ step
        hot = sends[step]
        multi = lax.dynamic_index_in_dim(multi_own, source, 0, False)
        gates = routed_softmax(input_near[step], multi)
        if step == 0:
            gates_own, multi_here = gates, multi
        plane = gates.reshape(tokens, ctx_count, exp_local)
        plane = lax.dynamic_index_in_dim(plane, z_index // split, 2, False)
        back = exchange(produced[step], "ctx")
        weighted = (hot * plane.T[:, None, :]).astype(low)
        out_parts.append(
            jnp.einsum("crt,crd->td", weighted, back, preferred_element_type=exact)
        )
        slot_grad = jnp.sum(cot_sent[step].astype(exact) * back.astype(exact), axis=-1)
        gate_sums.append(jnp.sum(hot.astype(exact) * slot_grad[:, :, None], axis=1).T)
        in_back = exchange(droute[step], "ctx")
        in_parts.append(
            jnp.einsum("crt,crd->td", hot, in_back, preferred_element_type=exact)
        )
    resid_two = resid_one + back_home(out_parts)
    out_hidden = resid_two.astype(low)[None]
    gate_grads = jnp.zeros((tokens, ctx_count, exp_local), exact)
    for step in range(z_count):
        got = swap(gate_sums[step], "fsdp", step) if step else gate_sums[step]
        place = ((z_index ^ step) // split) == jnp.arange(exp_local)
        gate_grads = gate_grads + got[:, :, None] * place.astype(exact)
    gate_grads = gate_grads.reshape(tokens, experts)
    weighted_sum = jnp.sum(gates_own * gate_grads, axis=-1, keepdims=True)
    logit_grad = (gates_own * (gate_grads - weighted_sum)).astype(low)
    input_grad = contract_cols(logit_grad, router_full) + back_home(in_parts)
    router_grad = contract_rows(ffn_input, logit_grad)
    grad_two = cotangent[0].astype(exact)
    resid_norm_grad, ffn_gain_grad = rms_back(input_grad, normed_two, scale_two, ffn_scale)
    grad_one = grad_two + resid_norm_grad

    attn_grad_low = grad_one.astype(low)
    attn_grad_all = gather_ctx(attn_grad_low).reshape(length, width)
    out_weight_grad = contract_rows(out_heads, attn_grad_all)
    grad_heads = contract_cols(attn_grad_low, out_full).astype(low)
    grad_heads = exchange(grad_heads.reshape(tokens, ctx_count, cols).transpose(1, 0, 2), "ctx")
    grad_heads = ordered(by_head(grad_heads), ctx_count)
    value_grad = jnp.einsum("hqk,qhd->khd", probs_low, grad_heads, preferred_element_type=exact)
    prob_grad = jnp.einsum("qhd,khd->hqk", grad_heads, value_low, preferred_element_type=exact)
    delta = jnp.sum(probs * prob_grad, axis=-1, keepdims=True)
    score_grad = (probs * (prob_grad - delta)).astype(low)
    query_rot_grad = scale * jnp.einsum(
        "hqk,khd->qhd", score_grad, key_rot, preferred_element_type=exact
    )
    key_rot_grad = scale * jnp.einsum(
        "hqk,qhd->khd", score_grad, query_rot, preferred_element_type=exact
    )
    query_back = rotate(placed(query_rot_grad, ctx_count), cosine, -sine).reshape(length, cols)
    key_back = rotate(placed(key_rot_grad, ctx_count), cosine, -sine).reshape(length, cols)
    value_grad_low = placed(value_grad.astype(low), ctx_count).reshape(length, cols)
    query_gain_grad = jnp.sum(query_back * query_normed, axis=0)
    key_gain_grad = jnp.sum(key_back * key_normed, axis=0)
    query_d, key_d = query_back * query_scale, key_back * key_scale
    inner_two = total_over_ctx(
        jnp.sum(query_d * query_normed, -1), jnp.sum(key_d * key_normed, -1)
    ) / width
    query_grad_low = (query_rms * (query_d - query_normed * inner_two[0][:, None])).astype(low)
    key_grad_low = (key_rms * (key_d - key_normed * inner_two[1][:, None])).astype(low)
    qkv_grad_low = jnp.concatenate([query_grad_low, key_grad_low, value_grad_low], axis=1)
    attn_input_grad = contract_cols(qkv_grad_low, qkv)
    qkv_weight_grad = contract_rows(attn_all, qkv_grad_low)
    attn_input_grad = scatter_ctx(attn_input_grad.reshape(ctx_count, tokens, width))
    _, normed_one, scale_one = rms_apply(rows_in, attn_scale)
    input_norm_grad, attn_gain_grad = rms_back(
        attn_input_grad, normed_one, scale_one, attn_scale
    )
    grad_hidden = (grad_one + input_norm_grad)[None]

    z_bits = bits_of("fsdp")
    pieces = qkv_weight_grad.reshape(ctx_count, z_count, rows_w, 3 * cols).transpose(1, 0, 2, 3)
    pieces = halved(pieces, "fsdp", z_bits).astype(low)
    pieces = exchange(pieces, "ctx").reshape(ctx_count, rows_w, 3, cols).astype(exact)
    pieces = pieces.transpose(2, 1, 0, 3).reshape(3, rows_w, width)
    grad_out = halved(out_weight_grad.reshape(z_count, rows_w, width), "fsdp", z_bits)
    sums = jnp.concatenate(
        [
            router_grad.reshape(ctx_count * z_count, rows_w * experts),
            ffn_gain_grad.reshape(-1, rows_w),
        ],
        axis=1,
    )
    sums = jnp.sum(exchange(sums, both), axis=0)
    grad_router = sums[: rows_w * experts].reshape(rows_w, experts)
    grad_ffn_gain = sums[rows_w * experts :]
    grad_attn_gain = jnp.sum(exchange(attn_gain_grad.reshape(-1, rows_w), both), axis=0)
    head_gains = jnp.stack([query_gain_grad, key_gain_grad], axis=1)
    head_gains = head_gains.reshape(z_count, rows_w, 2)
    head_gains = jnp.sum(exchange(head_gains, "fsdp"), axis=0)
    return (
        out_hidden,
        grad_hidden,
        grad_attn_gain,
        head_gains[:, 0],
        head_gains[:, 1],
        grad_ffn_gain,
        pieces[0],
        pieces[1],
        pieces[2],
        grad_out,
        grad_router,
        grad_gate,
        grad_up,
        grad_down,
    )


def solution(mesh):
    in_specs = (
        P("fsdp", "ctx", None),
        P("fsdp", "ctx", None),
        P("fsdp", "ctx", None),
        P(("ctx", "fsdp")),
        P(("ctx", "fsdp")),
        P(("ctx", "fsdp")),
        P(("ctx", "fsdp")),
        P(("ctx", "fsdp"), None),
        P(("ctx", "fsdp"), None),
        P(("ctx", "fsdp"), None),
        P(("ctx", "fsdp"), None),
        P(("ctx", "fsdp"), None),
        P("ctx", "fsdp", None),
        P("ctx", "fsdp", None),
        P("ctx", "fsdp", None),
    )
    out_specs = (
        P("fsdp", "ctx", None),
        P("fsdp", "ctx", None),
        P(("ctx", "fsdp")),
        P(("ctx", "fsdp")),
        P(("ctx", "fsdp")),
        P(("ctx", "fsdp")),
        P(("ctx", "fsdp"), None),
        P(("ctx", "fsdp"), None),
        P(("ctx", "fsdp"), None),
        P(("ctx", "fsdp"), None),
        P(("ctx", "fsdp"), None),
        P("ctx", "fsdp", None),
        P("ctx", "fsdp", None),
        P("ctx", "fsdp", None),
    )
    return jax.shard_map(body, mesh=mesh, in_specs=in_specs, out_specs=out_specs, check_vma=False)
```

```python
import functools
import math

import jax
import jax.numpy as jnp
import numpy as np
from jax import lax
from jax.experimental import pallas as pl
from jax.experimental.pallas import tpu as pltpu
from jax.sharding import PartitionSpec as P

HEADS = 16


epsilon = 1e-05
neg_large = -1e30
low = jnp.bfloat16
exact = jnp.float32


def swap(x, axis, bit):
    length = lax.axis_size(axis)
    return lax.ppermute(x, axis, [(i, i ^ bit) for i in range(length)])


def bits_of(axis):
    length = lax.axis_size(axis)
    return [1 << i for i in range(length.bit_length() - 1)]


def doubled(x, axis, bits):
    index = lax.axis_index(axis)
    for bit in bits:
        other = swap(x, axis, bit)
        high = (index & bit) != 0
        x = jnp.stack([jnp.where(high, other, x), jnp.where(high, x, other)])
    count = len(bits)
    order = sorted(range(count), key=lambda i: -bits[count - 1 - i])
    x = x.transpose(order + list(range(count, x.ndim)))
    return x.reshape((1 << count,) + x.shape[count:])


def gather_ctx(x):
    bits = bits_of("ctx")
    half = x.shape[-1] // 2
    far = bits[1:]
    one = doubled(x[..., :half], "ctx", far + bits[:1])
    two = doubled(x[..., half:], "ctx", far[::-1] + bits[:1])
    return jnp.concatenate([one, two], axis=-1)


def everywhere(x):
    x = doubled(x, "fsdp", bits_of("fsdp")[::-1])
    return doubled(x, "ctx", bits_of("ctx"))


def spread(x):
    index = lax.axis_index("fsdp")
    out = x
    for step in range(1, x.shape[0]):
        piece = lax.dynamic_index_in_dim(x, index ^ step, 0, True)
        out = lax.dynamic_update_slice_in_dim(out, swap(piece, "fsdp", step), index ^ step, 0)
    return out


def halved(x, axis, bits):
    index = lax.axis_index(axis)
    count = len(bits)
    x = x.reshape((2,) * count + x.shape[1:])
    left = sorted(bits, reverse=True)
    for bit in bits:
        at = left.index(bit)
        left.remove(bit)
        zero = lax.index_in_dim(x, 0, at, keepdims=False)
        one = lax.index_in_dim(x, 1, at, keepdims=False)
        high = (index & bit) != 0
        got = swap(jnp.where(high, zero, one).astype(low), axis, bit)
        x = jnp.where(high, one, zero).astype(exact) + got.astype(exact)
    return x


def scatter_ctx(x):
    bits = bits_of("ctx")
    half = x.shape[-1] // 2
    far = bits[1:]
    one = halved(x[..., :half], "ctx", bits[:1] + far)
    two = halved(x[..., half:], "ctx", bits[:1] + far[::-1])
    return jnp.concatenate([one, two], axis=-1)


def near_first(x):
    blocks = {0: x}
    for bit in bits_of("fsdp")[::-1]:
        for key in sorted(blocks):
            blocks[key | bit] = swap(blocks[key], "fsdp", bit)
    return [blocks[key] for key in sorted(blocks)]


def back_home(parts):
    parts = [part.astype(exact) for part in parts]
    for bit in bits_of("fsdp"):
        for key in range(len(parts)):
            if key & bit and not key & (bit - 1):
                got = swap(parts[key].astype(low), "fsdp", bit)
                parts[key ^ bit] = parts[key ^ bit] + got.astype(exact)
    return parts[0]


def exchange(x, axis):
    return lax.all_to_all(x, axis, split_axis=0, concat_axis=0, tiled=True)


def rms_apply(vector, gain):
    scale = lax.rsqrt(jnp.mean(vector * vector, axis=-1, keepdims=True) + epsilon)
    normed = vector * scale
    return (normed * gain, normed, scale)


def rms_back(grad, normed, scale, gain):
    dnormed = grad * gain
    gain_grad = jnp.sum(grad * normed, axis=0)
    inner = jnp.mean(dnormed * normed, axis=-1, keepdims=True)
    return (scale * (dnormed - normed * inner), gain_grad)


def rotation(positions, head_size):
    half = head_size // 2
    freq = 10000.0 ** (-jnp.arange(half, dtype=jnp.float32) * (2.0 / head_size))
    angle = positions.astype(jnp.float32)[:, None] * freq[None, :]
    return (jnp.cos(angle)[:, None, :], jnp.sin(angle)[:, None, :])


def rotate(vector, cosine, sine):
    half = vector.shape[-1] // 2
    first = vector[..., :half]
    second = vector[..., half:]
    return jnp.concatenate(
        [first * cosine - second * sine, second * cosine + first * sine], axis=-1
    )


def dot(left, right):
    return jnp.dot(left, right, preferred_element_type=exact)


def contract_rows(left, right):
    return lax.dot_general(
        left, right, (((0,), (0,)), ((), ())), preferred_element_type=exact
    )


def contract_cols(left, right):
    return lax.dot_general(
        left, right, (((1,), (1,)), ((), ())), preferred_element_type=exact
    )


def ordered(x, ctx_count):
    x = x.reshape((ctx_count, 2, -1) + x.shape[1:])
    x = jnp.concatenate([x[:, 0], x[::-1, 1]], axis=0)
    return x.reshape((-1,) + x.shape[2:])


def placed(x, ctx_count):
    x = x.reshape((2 * ctx_count, -1) + x.shape[1:])
    x = jnp.stack([x[:ctx_count], x[ctx_count:][::-1]], axis=1)
    return x.reshape((-1,) + x.shape[3:])


def bits_down(count):
    return [1 << i for i in range(count.bit_length() - 1)][::-1]


class Links:
    def __init__(self, sends, recvs, locals_):
        self.sends, self.recvs, self.locals = sends, recvs, locals_
        self.count = self.local_count = 0
        self.open = {}
        self.seen = {}

    def send(self, src, dst, **to):
        copy = pltpu.make_async_remote_copy(
            src_ref=src,
            dst_ref=dst,
            send_sem=self.sends.at[self.count],
            recv_sem=self.recvs.at[self.count],
            device_id=to,
            device_id_type=pl.DeviceIdType.MESH,
        )
        self.count += 1
        copy.start()
        self.open[id(copy)] = (copy, True)
        return copy

    def move(self, src, dst):
        copy = pltpu.make_async_copy(src, dst, self.locals.at[self.local_count])
        self.local_count += 1
        copy.start()
        self.open[id(copy)] = (copy, False)
        return copy

    def left(self, copy):
        if id(copy) in self.open:
            copy, remote = self.open.pop(id(copy))
            self.seen[id(copy), "left"] = copy
            copy.wait_send() if remote else copy.wait()

    def arrived(self, copy):
        if (id(copy), "in") not in self.seen:
            self.seen[id(copy), "in"] = copy
            copy.wait_recv()

    def close(self):
        for copy, _ in list(self.open.values()):
            self.left(copy)


def greet(c, z, nc, nz):
    barrier = pltpu.get_barrier_semaphore()
    for d in range(1, nc):
        pl.semaphore_signal(
            barrier, inc=1, device_id={"ctx": c ^ d}, device_id_type=pl.DeviceIdType.MESH
        )
    for s in range(1, nz):
        pl.semaphore_signal(
            barrier, inc=1, device_id={"fsdp": z ^ s}, device_id_type=pl.DeviceIdType.MESH
        )
    pl.semaphore_wait(barrier, nc - 1 + nz - 1)


def kdot(left, right, dims=((1,), (0,)), precision=None):
    return lax.dot_general(
        left, right, (dims, ((), ())), preferred_element_type=exact, precision=precision
    )


def slots_of(cfg, mask_rows, upper):
    rank = kdot(mask_rows.astype(low), upper)
    return jnp.where(mask_rows > 0, rank, 0.0)


def plane_ranks(cfg, routes, z):
    nc, tokens = cfg["nc"], cfg["tokens"]
    expert = lax.broadcasted_iota(jnp.int32, (nc, tokens), 0) * cfg["exp_local"] + z // cfg["split"]
    mask = jnp.zeros((nc, tokens), exact)
    for k in range(cfg["top"]):
        mask = jnp.where(routes[k : k + 1, :] == expert, 1.0, mask)
    upper = jnp.where(
        lax.broadcasted_iota(jnp.int32, (tokens, tokens), 0)
        <= lax.broadcasted_iota(jnp.int32, (tokens, tokens), 1),
        1.0,
        0.0,
    ).astype(low)
    return slots_of(cfg, mask, upper)


def fill_hot(cfg, ranks, hot_ref):
    cap, tokens = cfg["cap"], cfg["tokens"]
    number = lax.broadcasted_iota(jnp.int32, (cap, tokens), 0).astype(exact) + 1.0
    for k in range(cfg["nc"]):
        hit = jnp.where(ranks[k : k + 1, :] == number, 1.0, 0.0)
        hot_ref[k * cap : (k + 1) * cap, :] = hit.astype(low)


def front_kernel(
    cfg,
    x_ref, wq_ref, wk_ref, wv_ref, wo_ref, gt_ref, rt_ref, ro_ref, cot_ref, gp_ref, up_ref, cos_ref, sin_ref,
    a1_out, w_full, raw_out, stat_out, rot_out, ob_out, wo_full, r1_out, a2_out, r_all, g_all, t_all,
    gate_full, up_full, cot_rows, cot_near,
    xbuf, wbuf, obw, gbuf, gfull, rbuf, tbuf, raw, stat, total, rq, rk, rot, opos, odev, orecv, r1, a2, cbuf, hot, cs,
    sends, recvs, locals_,
):
    nc, nz, tokens, width = cfg["nc"], cfg["nz"], cfg["tokens"], cfg["width"]
    cols, rows_w, length, cap = cfg["cols"], cfg["rows_w"], cfg["length"], cfg["cap"]
    hs = 128
    heads = cols // hs
    half = tokens // 2
    block = cfg["block"]
    blocks = length // block
    c, z = lax.axis_index("ctx"), lax.axis_index("fsdp")
    links = Links(sends, recvs, locals_)
    ds = pl.ds
    same = [d for d in range(2, nc, 2)]

    own = []
    own.append(links.move(x_ref, xbuf.at[ds(c * tokens, tokens)]))
    for j, ref in enumerate((wq_ref, wk_ref, wv_ref)):
        at = pl.multiple_of(c * cols, 128)
        own.append(links.move(ref.at[:, ds(at, cols)], wbuf.at[j, c, z]))
    own.append(links.move(wo_ref, obw.at[c, z]))
    own.append(links.move(gt_ref, gbuf.at[c, z]))
    own.append(links.move(rt_ref, rbuf.at[c, z]))
    own.append(links.move(ro_ref, tbuf.at[c, z]))
    own.append(links.move(cot_ref, cbuf.at[0]))
    mine = links.move(gp_ref.at[z], gate_full.at[z])
    mine_up = links.move(up_ref.at[z], up_full.at[z])
    greet(c, z, nc, nz)

    slices = []
    for d in range(1, nc):
        peer = c ^ d
        at = pl.multiple_of(peer * cols, 128)
        for j, ref in enumerate((wq_ref, wk_ref, wv_ref)):
            slices.append(links.send(ref.at[:, ds(at, cols)], wbuf.at[j, c, z], ctx=peer))
    small_z = []
    for s in range(1, nz):
        for src, dst in ((gt_ref, gbuf), (rt_ref, rbuf), (ro_ref, tbuf)):
            small_z.append(links.send(src, dst.at[c, z], fsdp=z ^ s))
    x_at = xbuf.at[ds(c * tokens, tokens)]
    x_same = {d: links.send(x_ref, x_at, ctx=c ^ d) for d in same}
    x_side = [links.send(x_ref, x_at, ctx=c ^ 1)]
    for copy in own:
        links.left(copy)

    for copy in slices:
        links.arrived(copy)
    w_near = {}

    def w_send(s, bit):
        place = wbuf.at[:, :, z ^ s]
        w_near[s | bit] = links.send(place, place, fsdp=z ^ bit)

    steps = bits_down(nz)
    for bit in steps:
        w_send(0, bit)
    wo_near, cot_copies = {}, {}

    def wo_send(s, bit):
        place = obw.at[c, z ^ s]
        wo_near[s | bit] = links.send(place, place, fsdp=z ^ bit)

    def cot_send(s, bit):
        cot_copies[s | bit] = links.send(cbuf.at[s], cbuf.at[s | bit], fsdp=z ^ bit)

    for copy in small_z:
        links.arrived(copy)
    small_c = []
    for d in range(1, nc):
        for buf in (gbuf, rbuf, tbuf):
            small_c.append(links.send(buf.at[c], buf.at[c], ctx=c ^ d))
    for d in same:
        links.arrived(x_same[d])
        place = xbuf.at[ds((c ^ d) * tokens, tokens)]
        x_side.append(links.send(place, place, ctx=c ^ 1))

    def forward(waits, send):
        for at, bit in enumerate(steps):
            held = [0]
            for earlier in steps[:at]:
                held += [s | earlier for s in held]
            for s in held[1:]:
                links.arrived(waits[s])
                send(s, bit)

    forward(w_near, w_send)
    for bit in steps:
        wo_send(0, bit)
    for bit in steps:
        cot_send(0, bit)
    for copy in small_c:
        links.arrived(copy)
    per = 128 // rows_w
    groups = nz // per
    for k in range(nc):
        for g in range(groups):
            tile = gbuf[k, g * per]
            for p in range(1, per):
                tile = tile + gbuf[k, g * per + p]
            at = (k * groups + g) * 128
            gfull[:, at : at + 128] = tile
    for copy in x_side:
        links.arrived(copy)
    for copy in list(x_same.values()) + x_side:
        links.left(copy)

    chunk = cfg["chunk"]

    def norm_rows(i, _):
        at = pl.multiple_of(i * chunk, chunk)
        v = xbuf[ds(at, chunk), :].astype(exact)
        v = v * lax.rsqrt(jnp.mean(v * v, axis=-1, keepdims=True) + epsilon) * gfull[0:1, :]
        xbuf[ds(at, chunk), :] = v.astype(low)
        return 0

    lax.fori_loop(0, length // chunk, norm_rows, 0)
    a1_copy = links.move(xbuf, a1_out)

    last = steps[-1]
    for s in range(1, nz):
        if s & last:
            links.arrived(w_near[s])
    experts_in = []
    for s in range(1, nz):
        experts_in.append(links.send(gp_ref.at[z ^ s], gate_full.at[z], fsdp=z ^ s))
    if cfg["carry_up"]:
        for s in range(1, nz):
            experts_in.append(links.send(up_ref.at[z ^ s], up_full.at[z], fsdp=z ^ s))
    w_copy = links.move(wbuf, w_full)

    one_row = lax.broadcasted_iota(jnp.int32, (8, cols), 0)
    pick_q = jnp.where(one_row == 0, 1.0, 0.0)
    pick_k = jnp.where(one_row == 1, 1.0, 0.0)
    best = lax.Precision.HIGHEST

    def project(i, _):
        at = pl.multiple_of(i * block, block)
        rows = xbuf[ds(at, block), :]
        sums = jnp.zeros((8, block), exact)
        for j in range(3):
            weight = wbuf[j].reshape(width, cols)
            v = kdot(rows, weight)
            raw[ds(at, block), j * cols : (j + 1) * cols] = v
            if j < 2:
                sums += kdot(pick_k if j else pick_q, v * v, ((1,), (1,)), best)
        stat[c, :, ds(at, block)] = sums
        return 0

    lax.fori_loop(0, blocks, project, 0)
    raw_copy = links.move(raw, raw_out)
    stats = [links.send(stat.at[c], stat.at[c], ctx=c ^ d) for d in range(1, nc)]
    forward(wo_near, wo_send)
    for s in range(1, nz):
        if s & last:
            links.arrived(wo_near[s])
    wo_same = {d: links.send(obw.at[c], obw.at[c], ctx=c ^ d) for d in same}
    wo_side = [links.send(obw.at[c], obw.at[c], ctx=c ^ 1)]
    for copy in stats:
        links.arrived(copy)
    summed = stat[0]
    for k in range(1, nc):
        summed += stat[k]
    total[...] = summed
    row8 = lax.broadcasted_iota(jnp.int32, (8, hs), 0)

    def columns(i, _):
        at = pl.multiple_of(i * block, block)
        part = total[:, ds(at, block)]
        for row, dst in ((0, rq), (1, rk)):
            sel = jnp.where(row8 == row, 1.0, 0.0)
            ms = kdot(part, sel, ((0,), (0,)), best)
            dst[ds(at, block), :] = lax.rsqrt(ms / width + epsilon)
        return 0

    lax.fori_loop(0, blocks, columns, 0)
    stat_copy = links.move(total, stat_out)

    def turn(i, _):
        d, side = i // 2, i % 2
        at = pl.multiple_of(d * tokens + side * half, half)
        to = pl.multiple_of(jnp.where(side == 0, d, 2 * nc - 1 - d) * half, half)
        cosine, sine = cos_ref[ds(at, half), :], sin_ref[ds(at, half), :]
        for h in range(heads):
            for j, scale in ((0, rq), (1, rk)):
                lane = j * cols + h * hs
                gain = gfull[1 + j : 2 + j, ds(pl.multiple_of(c * cols + h * hs, hs), hs)]
                v = raw[ds(at, half), lane : lane + hs] * scale[ds(at, half), :] * gain
                v = v * cosine + pltpu.roll(v, hs // 2, 1) * sine
                rot[j, ds(to, half), h * hs : (h + 1) * hs] = v.astype(low)
        rot[2, ds(to, half), :] = raw[ds(at, half), 2 * cols : 3 * cols].astype(low)
        return 0

    lax.fori_loop(0, 2 * nc, turn, 0)
    rot_copy = links.move(rot, rot_out)
    forward(cot_copies, cot_send)

    scale = hs ** -0.5
    for h in range(heads):
        lanes = slice(h * hs, (h + 1) * hs)
        for i in range(blocks):
            count = (i + 1) * block
            q = rot[0, i * block : count, lanes]
            s = kdot(q, rot[1, :count, lanes], ((1,), (1,))) * scale
            row = lax.broadcasted_iota(jnp.int32, (block, count), 0) + i * block
            col = lax.broadcasted_iota(jnp.int32, (block, count), 1)
            s = jnp.where(col <= row, s, neg_large)
            p = jnp.exp(s - jnp.max(s, axis=-1, keepdims=True))
            p = p * (1.0 / jnp.sum(p, axis=-1, keepdims=True))
            opos[i * block : count, lanes] = kdot(p.astype(low), rot[2, :count, lanes]).astype(low)

    def place(i, _):
        d, side = i // 2, i % 2
        to = pl.multiple_of(d * tokens + side * half, half)
        at = pl.multiple_of(jnp.where(side == 0, d, 2 * nc - 1 - d) * half, half)
        odev[ds(to, half), :] = opos[ds(at, half), :]
        return 0

    lax.fori_loop(0, 2 * nc, place, 0)
    ob_copy = links.move(odev, ob_out)
    mixed = []
    for d in range(1, nc):
        src = odev.at[ds((c ^ d) * tokens, tokens)]
        mixed.append(links.send(src, orecv.at[c], ctx=c ^ d))
    own_mixed = links.move(odev.at[ds(c * tokens, tokens)], orecv.at[c])
    for d in same:
        links.arrived(wo_same[d])
        place_at = obw.at[c ^ d]
        wo_side.append(links.send(place_at, place_at, ctx=c ^ 1))

    for s in range(1, nz):
        if s & last:
            links.arrived(cot_copies[s])
    near_copy = links.move(cbuf, cot_near)
    rows_sent = []
    slot_busy = [[], []]
    for s in range(nz):
        slot = s % 2
        for copy in slot_busy[slot]:
            links.left(copy)
        fill_hot(cfg, plane_ranks(cfg, tbuf[c, z ^ s], z), hot)
        cs[slot] = kdot(hot[...], cbuf[s]).astype(low)
        busy = []
        for d in range(1, nc):
            src = cs.at[slot, ds((c ^ d) * cap, cap)]
            copy = links.send(src, cot_rows.at[s, c], ctx=c ^ d)
            rows_sent.append(copy)
            busy.append(copy)
        busy.append(links.move(cs.at[slot, ds(c * cap, cap)], cot_rows.at[s, c]))
        slot_busy[slot] = busy

    for copy in wo_side:
        links.arrived(copy)
    wo_copy = links.move(obw, wo_full)
    for copy in mixed:
        links.arrived(copy)
    links.left(own_mixed)
    r1[...] = jnp.zeros_like(r1)

    def mix(k, _):
        r1[...] += kdot(orecv[k], obw[k].reshape(cols, width))
        return 0

    lax.fori_loop(0, nc, mix, 0)
    xin = links.move(x_ref, a2)
    links.left(xin)
    v = r1[...] + a2[...].astype(exact)
    r1[...] = v
    n2 = v * lax.rsqrt(jnp.mean(v * v, axis=-1, keepdims=True) + epsilon)
    a2[...] = (n2 * gfull[3:4, :]).astype(low)
    links.move(r1, r1_out)
    links.move(a2, a2_out)
    links.move(rbuf, r_all)
    links.move(gfull, g_all)
    links.move(tbuf, t_all)
    for copy in experts_in + rows_sent:
        links.arrived(copy)
    links.close()


def front(cfg, x, w_query, w_key, w_value, w_out, gains, router, routes, cot, gate_pieces, up_pieces, cosine, sine):
    nc, nz, tokens, width = cfg["nc"], cfg["nz"], cfg["tokens"], cfg["width"]
    cols, rows_w, length, cap = cfg["cols"], cfg["rows_w"], cfg["length"], cfg["cap"]
    rows, part = gate_pieces.shape[1:]
    shape = jax.ShapeDtypeStruct
    any_, vmem = pl.BlockSpec(memory_space=pl.ANY), pl.BlockSpec(memory_space=pltpu.VMEM)
    top_rows = routes.shape[0]
    outs = [
        shape((length, width), low),
        shape((3, nc, nz, rows_w, cols), low),
        shape((length, 3 * cols), exact),
        shape((8, length), exact),
        shape((3, length, cols), low),
        shape((length, cols), low),
        shape((nc, nz, rows_w, width), low),
        shape((tokens, width), exact),
        shape((tokens, width), low),
        shape((nc, nz, rows_w, 128), low),
        shape((8, width), exact),
        shape((nc, nz, top_rows, tokens), jnp.int32),
        shape((nz, rows, part), low),
        shape((nz, rows, part), low),
        shape((nz, nc, cap, width), low),
        shape((nz, tokens, width), low),
    ]
    scratch = [
        pltpu.VMEM((length, width), low),
        pltpu.VMEM((3, nc, nz, rows_w, cols), low),
        pltpu.VMEM((nc, nz, rows_w, width), low),
        pltpu.VMEM((nc, nz, 8, 128), exact),
        pltpu.VMEM((8, width), exact),
        pltpu.VMEM((nc, nz, rows_w, 128), low),
        pltpu.VMEM((nc, nz, top_rows, tokens), jnp.int32),
        pltpu.VMEM((length, 3 * cols), exact),
        pltpu.VMEM((nc, 8, length), exact),
        pltpu.VMEM((8, length), exact),
        pltpu.VMEM((length, 128), exact),
        pltpu.VMEM((length, 128), exact),
        pltpu.VMEM((3, length, cols), low),
        pltpu.VMEM((length, cols), low),
        pltpu.VMEM((length, cols), low),
        pltpu.VMEM((nc, tokens, cols), low),
        pltpu.VMEM((tokens, width), exact),
        pltpu.VMEM((tokens, width), low),
        pltpu.VMEM((nz, tokens, width), low),
        pltpu.VMEM((nc * cap, tokens), low),
        pltpu.VMEM((2, nc * cap, width), low),
        pltpu.SemaphoreType.DMA((cfg["copies"],)),
        pltpu.SemaphoreType.DMA((cfg["copies"],)),
        pltpu.SemaphoreType.DMA((64,)),
    ]
    return pl.pallas_call(
        functools.partial(front_kernel, cfg),
        out_shape=outs,
        in_specs=[any_] * 11 + [vmem] * 2,
        out_specs=[any_] * len(outs),
        scratch_shapes=scratch,
        compiler_params=pltpu.CompilerParams(
            collective_id=0, has_side_effects=True, vmem_limit_bytes=cfg["vmem"]
        ),
        name="front",
    )(x, w_query, w_key, w_value, w_out, gains, router, routes, cot, gate_pieces, up_pieces, cosine, sine)


def tables(nc, tokens, head_size):
    half = tokens // 2
    local = np.arange(tokens)
    device = np.arange(nc)[:, None]
    position = np.where(
        local < half, device * half + local, (2 * nc - 1 - device) * half + local - half
    ).reshape(-1)
    freq = np.float32(10000.0) ** (-np.arange(head_size // 2, dtype=np.float32) * (2.0 / head_size))
    angle = position.astype(np.float32)[:, None] * freq.astype(np.float32)
    cosine = np.concatenate([np.cos(angle), np.cos(angle)], axis=1)
    sine = np.concatenate([-np.sin(angle), np.sin(angle)], axis=1)
    return jnp.asarray(cosine, exact), jnp.asarray(sine, exact)


def body(
    hidden_in,
    cotangent,
    routes,
    attn_gain,
    query_gain,
    key_gain,
    ffn_gain,
    w_query,
    w_key,
    w_value,
    w_out,
    w_router,
    w_gate,
    w_up,
    w_down,
):
    tokens = hidden_in.shape[1]
    width = hidden_in.shape[2]
    head_size = width // HEADS
    ctx_count = lax.axis_size("ctx")
    z_count = lax.axis_size("fsdp")
    both = ("ctx", "fsdp")
    top = routes.shape[2]
    exp_local = w_gate.shape[0]
    split = z_count // exp_local
    hidden = w_gate.shape[2]
    part = hidden // split
    experts = exp_local * ctx_count
    capacity = tokens * top * 4 // (3 * experts)
    heads = HEADS // ctx_count
    cols = heads * head_size
    length = tokens * ctx_count
    scale = head_size ** (-0.5)
    c_index = lax.axis_index("ctx")
    z_index = lax.axis_index("fsdp")
    rows_w = w_query.shape[0]

    cfg = dict(
        nc=ctx_count,
        nz=z_count,
        tokens=tokens,
        width=width,
        cols=cols,
        rows_w=rows_w,
        length=length,
        cap=capacity,
        top=top,
        exp_local=exp_local,
        split=split,
        block=math.gcd(length, 256),
        chunk=math.gcd(length, 64),
        copies=(ctx_count - 1) * (8 + z_count) + (z_count - 1) * 8 + 2 * ctx_count + 8,
        carry_up=True,
        vmem=60 * 2**20,
    )
    index = c_index * z_count + z_index
    per = 128 // rows_w
    gains = jnp.stack([attn_gain, query_gain, key_gain, ffn_gain]).astype(exact)
    gains = lax.dynamic_update_slice(
        jnp.zeros((8, 128), exact), gains, (0, jnp.mod(index, per) * rows_w)
    )
    router_tile = jnp.pad(w_router, ((0, 0), (0, 128 - experts)))
    route_tile = jnp.pad(routes[0].T, ((0, 8 - top), (0, 0)), constant_values=-1)

    def pieces_of(weight):
        rows = weight.shape[1]
        weight = weight.reshape(exp_local, rows, z_count, split, part // z_count)
        return weight.transpose(0, 3, 1, 2, 4).reshape(z_count, rows, part)

    (
        attn_all, w_full, raw, squares, rot, out_heads, wo_full, resid_one, ffn_input,
        router_full, gains, routes_all, gate_full, up_full, cot_rows, cot_near,
    ) = front(
        cfg, hidden_in[0], w_query, w_key, w_value, w_out, gains, router_tile, route_tile,
        cotangent[0], pieces_of(w_gate), pieces_of(w_up), *tables(ctx_count, tokens, head_size),
    )
    gate_full = gate_full.reshape(-1, part)
    up_full = up_full.reshape(-1, part)
    w_full = w_full.reshape(3, width, cols)
    out_full = wo_full.reshape(width, width)
    router_full = router_full.reshape(width, 128)[:, :experts]
    cot_rows = cot_rows.reshape(-1, width)
    attn_scale, ffn_scale = gains[0], gains[3]
    query_scale = lax.dynamic_slice_in_dim(gains[1], c_index * cols, cols)
    key_scale = lax.dynamic_slice_in_dim(gains[2], c_index * cols, cols)
    routes_all = routes_all[:, :, :top].swapaxes(2, 3)

    multi_all = jnp.sum(
        (routes_all[..., None] == jnp.arange(experts, dtype=jnp.int32)).astype(exact), axis=-2
    ).reshape(ctx_count, z_count, tokens, experts)
    own_expert = c_index * exp_local + z_index // split
    lower = (
        jnp.arange(tokens)[:, None] >= jnp.arange(tokens)[None, :]
    ).astype(low)

    def slots(mask):
        rank = jnp.einsum("ts,bs->bt", lower, mask.astype(low), preferred_element_type=exact)
        rank = rank.astype(jnp.int32) - 1
        hit = rank[:, None, :] == jnp.arange(capacity, dtype=jnp.int32)[None, :, None]
        return (hit & (mask[:, None, :] > 0)).astype(low)

    multi_own = lax.dynamic_index_in_dim(multi_all, c_index, 0, False)
    sends = []
    metas = []
    for step in range(z_count):
        source = z_index ^ step
        multi = lax.dynamic_index_in_dim(multi_own, source, 0, False)
        plane = multi.reshape(tokens, ctx_count, exp_local)
        plane = lax.dynamic_index_in_dim(plane, z_index // split, 2, False)
        sends.append(slots(plane.T))
        there = lax.dynamic_index_in_dim(multi_all, source, 1, False)
        mine = lax.dynamic_index_in_dim(there, own_expert, 2, False)
        metas.append(
            jnp.einsum(
                "crt,cte->cre", slots(mine), there.astype(low), preferred_element_type=exact
            )
        )
    meta = jnp.stack(metas).reshape(-1, experts)

    def pick(hot, block):
        rows = jnp.einsum("crt,td->crd", hot, block, preferred_element_type=exact)
        return rows.astype(low)

    cot_sent = [pick(hot, cot_near[step]) for step, hot in enumerate(sends)]
    rows_d = w_down.shape[1]
    down_full = spread(w_down.reshape(z_count, rows_d // split, width)).reshape(part, width)

    def total_over_ctx(one, two):
        both_sums = jnp.stack([one, two])
        return jnp.sum(lax.all_gather(both_sums, "ctx", axis=0), axis=0)

    queries, keys = raw[:, :cols], raw[:, cols : 2 * cols]
    rms_two = lax.rsqrt(squares[:2] / width + epsilon)
    query_rms, key_rms = rms_two[0][:, None], rms_two[1][:, None]
    query_normed, key_normed = queries * query_rms, keys * key_rms
    half = tokens // 2
    row = jnp.arange(length, dtype=jnp.int32)
    device, local = row // tokens, row % tokens
    positions = jnp.where(
        local < half, device * half + local, (2 * ctx_count - 1 - device) * half + local - half
    )
    cosine, sine = rotation(positions, head_size)

    def by_head(x):
        return x.reshape(length, heads, head_size)

    query_rot, key_rot, value_low = by_head(rot[0]), by_head(rot[1]), by_head(rot[2])
    allowed = (row[None, :] <= row[:, None])[None]
    scores = (
        jnp.einsum("qhd,khd->hqk", query_rot, key_rot, preferred_element_type=exact) * scale
    )
    scores = jnp.where(allowed, scores, neg_large)
    log_total = jax.nn.logsumexp(scores, axis=-1, keepdims=True)
    probs = jnp.exp(scores - log_total)
    probs_low = probs.astype(low)
    rows_in = hidden_in[0].astype(exact)
    scale_two = lax.rsqrt(jnp.mean(resid_one * resid_one, axis=-1, keepdims=True) + epsilon)
    normed_two = resid_one * scale_two

    input_near = near_first(ffn_input)
    input_rows = jnp.stack(
        [exchange(pick(hot, block), "ctx") for hot, block in zip(sends, input_near)]
    ).reshape(-1, width)

    def routed_softmax(rows, multi):
        logits = jnp.where(multi > 0, dot(rows, router_full), neg_large)
        top_value = jnp.max(logits, axis=-1, keepdims=True)
        weight = jnp.exp(logits - top_value)
        return weight / jnp.sum(weight, axis=-1, keepdims=True)

    row_gates = routed_softmax(input_rows, meta)
    row_gate = lax.dynamic_slice_in_dim(row_gates, own_expert, 1, 1)
    deout = (row_gate * cot_rows.astype(exact)).astype(low)
    gate_pre = dot(input_rows, gate_full)
    up_pre = dot(input_rows, up_full)
    sigmoid_gate = jax.nn.sigmoid(gate_pre)
    activated = gate_pre * sigmoid_gate
    inner_low = (activated * up_pre).astype(low)
    produced = dot(inner_low, down_full).astype(low)
    inner_grad = contract_cols(deout, down_full)
    gate_pre_grad = (
        inner_grad * up_pre * sigmoid_gate * (1.0 + gate_pre * (1.0 - sigmoid_gate))
    ).astype(low)
    up_pre_grad = (inner_grad * activated).astype(low)
    droute = (
        contract_cols(gate_pre_grad, gate_full) + contract_cols(up_pre_grad, up_full)
    ).astype(low)
    down_grad = contract_rows(inner_low, deout).astype(low)
    gate_grad = contract_rows(input_rows, gate_pre_grad).astype(low)
    up_grad = contract_rows(input_rows, up_pre_grad).astype(low)

    def whole_out(grad):
        rows = grad.shape[0] // z_count
        grad = spread(grad.reshape(z_count, rows, part))
        grad = grad.reshape(exp_local, split, rows, z_count, part // z_count)
        return grad.transpose(0, 2, 3, 1, 4).reshape(exp_local, rows, hidden).astype(exact)

    grad_down = (
        spread(down_grad.reshape(z_count, rows_d // split, width))
        .reshape(exp_local, rows_d, width)
        .astype(exact)
    )
    grad_gate = whole_out(gate_grad)
    grad_up = whole_out(up_grad)

    shape = (z_count, ctx_count, capacity, width)
    produced = produced.reshape(shape)
    droute = droute.reshape(shape)
    out_parts = []
    in_parts = []
    gate_sums = []
    for step in range(z_count):
        source = z_index ^ step
        hot = sends[step]
        multi = lax.dynamic_index_in_dim(multi_own, source, 0, False)
        gates = routed_softmax(input_near[step], multi)
        if step == 0:
            gates_own, multi_here = gates, multi
        plane = gates.reshape(tokens, ctx_count, exp_local)
        plane = lax.dynamic_index_in_dim(plane, z_index // split, 2, False)
        back = exchange(produced[step], "ctx")
        weighted = (hot * plane.T[:, None, :]).astype(low)
        out_parts.append(
            jnp.einsum("crt,crd->td", weighted, back, preferred_element_type=exact)
        )
        slot_grad = jnp.sum(cot_sent[step].astype(exact) * back.astype(exact), axis=-1)
        gate_sums.append(jnp.sum(hot.astype(exact) * slot_grad[:, :, None], axis=1).T)
        in_back = exchange(droute[step], "ctx")
        in_parts.append(
            jnp.einsum("crt,crd->td", hot, in_back, preferred_element_type=exact)
        )
    resid_two = resid_one + back_home(out_parts)
    out_hidden = resid_two.astype(low)[None]
    gate_grads = jnp.zeros((tokens, ctx_count, exp_local), exact)
    for step in range(z_count):
        got = swap(gate_sums[step], "fsdp", step) if step else gate_sums[step]
        place = ((z_index ^ step) // split) == jnp.arange(exp_local)
        gate_grads = gate_grads + got[:, :, None] * place.astype(exact)
    gate_grads = gate_grads.reshape(tokens, experts)
    weighted_sum = jnp.sum(gates_own * gate_grads, axis=-1, keepdims=True)
    logit_grad = (gates_own * (gate_grads - weighted_sum)).astype(low)
    input_grad = contract_cols(logit_grad, router_full) + back_home(in_parts)
    router_grad = contract_rows(ffn_input, logit_grad)
    grad_two = cotangent[0].astype(exact)
    resid_norm_grad, ffn_gain_grad = rms_back(input_grad, normed_two, scale_two, ffn_scale)
    grad_one = grad_two + resid_norm_grad

    attn_grad_low = grad_one.astype(low)
    attn_grad_all = gather_ctx(attn_grad_low).reshape(length, width)
    out_weight_grad = contract_rows(out_heads, attn_grad_all)
    grad_heads = contract_cols(attn_grad_low, out_full).astype(low)
    grad_heads = exchange(grad_heads.reshape(tokens, ctx_count, cols).transpose(1, 0, 2), "ctx")
    grad_heads = ordered(by_head(grad_heads), ctx_count)
    value_grad = jnp.einsum("hqk,qhd->khd", probs_low, grad_heads, preferred_element_type=exact)
    prob_grad = jnp.einsum("qhd,khd->hqk", grad_heads, value_low, preferred_element_type=exact)
    delta = jnp.sum(probs * prob_grad, axis=-1, keepdims=True)
    score_grad = (probs * (prob_grad - delta)).astype(low)
    query_rot_grad = scale * jnp.einsum(
        "hqk,khd->qhd", score_grad, key_rot, preferred_element_type=exact
    )
    key_rot_grad = scale * jnp.einsum(
        "hqk,qhd->khd", score_grad, query_rot, preferred_element_type=exact
    )
    query_back = rotate(placed(query_rot_grad, ctx_count), cosine, -sine).reshape(length, cols)
    key_back = rotate(placed(key_rot_grad, ctx_count), cosine, -sine).reshape(length, cols)
    value_grad_low = placed(value_grad.astype(low), ctx_count).reshape(length, cols)
    query_gain_grad = jnp.sum(query_back * query_normed, axis=0)
    key_gain_grad = jnp.sum(key_back * key_normed, axis=0)
    query_d, key_d = query_back * query_scale, key_back * key_scale
    inner_two = total_over_ctx(
        jnp.sum(query_d * query_normed, -1), jnp.sum(key_d * key_normed, -1)
    ) / width
    query_grad_low = (query_rms * (query_d - query_normed * inner_two[0][:, None])).astype(low)
    key_grad_low = (key_rms * (key_d - key_normed * inner_two[1][:, None])).astype(low)
    qkv_grad_low = jnp.concatenate([query_grad_low, key_grad_low, value_grad_low], axis=1)
    attn_input_grad = (
        contract_cols(query_grad_low, w_full[0])
        + contract_cols(key_grad_low, w_full[1])
        + contract_cols(value_grad_low, w_full[2])
    )
    qkv_weight_grad = contract_rows(attn_all, qkv_grad_low)
    attn_input_grad = scatter_ctx(attn_input_grad.reshape(ctx_count, tokens, width))
    _, normed_one, scale_one = rms_apply(rows_in, attn_scale)
    input_norm_grad, attn_gain_grad = rms_back(
        attn_input_grad, normed_one, scale_one, attn_scale
    )
    grad_hidden = (grad_one + input_norm_grad)[None]

    z_bits = bits_of("fsdp")
    pieces = qkv_weight_grad.reshape(ctx_count, z_count, rows_w, 3 * cols).transpose(1, 0, 2, 3)
    pieces = halved(pieces, "fsdp", z_bits).astype(low)
    pieces = exchange(pieces, "ctx").reshape(ctx_count, rows_w, 3, cols).astype(exact)
    pieces = pieces.transpose(2, 1, 0, 3).reshape(3, rows_w, width)
    grad_out = halved(out_weight_grad.reshape(z_count, rows_w, width), "fsdp", z_bits)
    sums = jnp.concatenate(
        [
            router_grad.reshape(ctx_count * z_count, rows_w * experts),
            ffn_gain_grad.reshape(-1, rows_w),
        ],
        axis=1,
    )
    sums = jnp.sum(exchange(sums, both), axis=0)
    grad_router = sums[: rows_w * experts].reshape(rows_w, experts)
    grad_ffn_gain = sums[rows_w * experts :]
    grad_attn_gain = jnp.sum(exchange(attn_gain_grad.reshape(-1, rows_w), both), axis=0)
    head_gains = jnp.stack([query_gain_grad, key_gain_grad], axis=1)
    head_gains = head_gains.reshape(z_count, rows_w, 2)
    head_gains = jnp.sum(exchange(head_gains, "fsdp"), axis=0)
    return (
        out_hidden,
        grad_hidden,
        grad_attn_gain,
        head_gains[:, 0],
        head_gains[:, 1],
        grad_ffn_gain,
        pieces[0],
        pieces[1],
        pieces[2],
        grad_out,
        grad_router,
        grad_gate,
        grad_up,
        grad_down,
    )


def solution(mesh):
    in_specs = (
        P("fsdp", "ctx", None),
        P("fsdp", "ctx", None),
        P("fsdp", "ctx", None),
        P(("ctx", "fsdp")),
        P(("ctx", "fsdp")),
        P(("ctx", "fsdp")),
        P(("ctx", "fsdp")),
        P(("ctx", "fsdp"), None),
        P(("ctx", "fsdp"), None),
        P(("ctx", "fsdp"), None),
        P(("ctx", "fsdp"), None),
        P(("ctx", "fsdp"), None),
        P("ctx", "fsdp", None),
        P("ctx", "fsdp", None),
        P("ctx", "fsdp", None),
    )
    out_specs = (
        P("fsdp", "ctx", None),
        P("fsdp", "ctx", None),
        P(("ctx", "fsdp")),
        P(("ctx", "fsdp")),
        P(("ctx", "fsdp")),
        P(("ctx", "fsdp")),
        P(("ctx", "fsdp"), None),
        P(("ctx", "fsdp"), None),
        P(("ctx", "fsdp"), None),
        P(("ctx", "fsdp"), None),
        P(("ctx", "fsdp"), None),
        P("ctx", "fsdp", None),
        P("ctx", "fsdp", None),
        P("ctx", "fsdp", None),
    )
    return jax.shard_map(body, mesh=mesh, in_specs=in_specs, out_specs=out_specs, check_vma=False)
```

```python
import functools
import math

import jax
import jax.numpy as jnp
import numpy as np
from jax import lax
from jax.experimental import pallas as pl
from jax.experimental.pallas import tpu as pltpu
from jax.sharding import PartitionSpec as P

HEADS = 16


epsilon = 1e-05
neg_large = -1e30
low = jnp.bfloat16
exact = jnp.float32


def swap(x, axis, bit):
    length = lax.axis_size(axis)
    return lax.ppermute(x, axis, [(i, i ^ bit) for i in range(length)])


def bits_of(axis):
    length = lax.axis_size(axis)
    return [1 << i for i in range(length.bit_length() - 1)]


def doubled(x, axis, bits):
    index = lax.axis_index(axis)
    for bit in bits:
        other = swap(x, axis, bit)
        high = (index & bit) != 0
        x = jnp.stack([jnp.where(high, other, x), jnp.where(high, x, other)])
    count = len(bits)
    order = sorted(range(count), key=lambda i: -bits[count - 1 - i])
    x = x.transpose(order + list(range(count, x.ndim)))
    return x.reshape((1 << count,) + x.shape[count:])


def gather_ctx(x):
    bits = bits_of("ctx")
    half = x.shape[-1] // 2
    far = bits[1:]
    one = doubled(x[..., :half], "ctx", far + bits[:1])
    two = doubled(x[..., half:], "ctx", far[::-1] + bits[:1])
    return jnp.concatenate([one, two], axis=-1)


def spread(x):
    index = lax.axis_index("fsdp")
    out = x
    for step in range(1, x.shape[0]):
        piece = lax.dynamic_index_in_dim(x, index ^ step, 0, True)
        out = lax.dynamic_update_slice_in_dim(out, swap(piece, "fsdp", step), index ^ step, 0)
    return out


def halved(x, axis, bits):
    index = lax.axis_index(axis)
    count = len(bits)
    x = x.reshape((2,) * count + x.shape[1:])
    left = sorted(bits, reverse=True)
    for bit in bits:
        at = left.index(bit)
        left.remove(bit)
        zero = lax.index_in_dim(x, 0, at, keepdims=False)
        one = lax.index_in_dim(x, 1, at, keepdims=False)
        high = (index & bit) != 0
        got = swap(jnp.where(high, zero, one).astype(low), axis, bit)
        x = jnp.where(high, one, zero).astype(exact) + got.astype(exact)
    return x


def scatter_ctx(x):
    bits = bits_of("ctx")
    half = x.shape[-1] // 2
    far = bits[1:]
    one = halved(x[..., :half], "ctx", bits[:1] + far)
    two = halved(x[..., half:], "ctx", bits[:1] + far[::-1])
    return jnp.concatenate([one, two], axis=-1)


def exchange(x, axis):
    return lax.all_to_all(x, axis, split_axis=0, concat_axis=0, tiled=True)


def rms_apply(vector, gain):
    scale = lax.rsqrt(jnp.mean(vector * vector, axis=-1, keepdims=True) + epsilon)
    normed = vector * scale
    return (normed * gain, normed, scale)


def rms_back(grad, normed, scale, gain):
    dnormed = grad * gain
    gain_grad = jnp.sum(grad * normed, axis=0)
    inner = jnp.mean(dnormed * normed, axis=-1, keepdims=True)
    return (scale * (dnormed - normed * inner), gain_grad)


def rotation(positions, head_size):
    half = head_size // 2
    freq = 10000.0 ** (-jnp.arange(half, dtype=jnp.float32) * (2.0 / head_size))
    angle = positions.astype(jnp.float32)[:, None] * freq[None, :]
    return (jnp.cos(angle)[:, None, :], jnp.sin(angle)[:, None, :])


def rotate(vector, cosine, sine):
    half = vector.shape[-1] // 2
    first = vector[..., :half]
    second = vector[..., half:]
    return jnp.concatenate(
        [first * cosine - second * sine, second * cosine + first * sine], axis=-1
    )


def dot(left, right):
    return jnp.dot(left, right, preferred_element_type=exact)


def contract_rows(left, right):
    return lax.dot_general(
        left, right, (((0,), (0,)), ((), ())), preferred_element_type=exact
    )


def contract_cols(left, right):
    return lax.dot_general(
        left, right, (((1,), (1,)), ((), ())), preferred_element_type=exact
    )


def ordered(x, ctx_count):
    x = x.reshape((ctx_count, 2, -1) + x.shape[1:])
    x = jnp.concatenate([x[:, 0], x[::-1, 1]], axis=0)
    return x.reshape((-1,) + x.shape[2:])


def placed(x, ctx_count):
    x = x.reshape((2 * ctx_count, -1) + x.shape[1:])
    x = jnp.stack([x[:ctx_count], x[ctx_count:][::-1]], axis=1)
    return x.reshape((-1,) + x.shape[3:])


def bits_down(count):
    return [1 << i for i in range(count.bit_length() - 1)][::-1]


class Links:
    def __init__(self, sends, recvs, locals_):
        self.sends, self.recvs, self.locals = sends, recvs, locals_
        self.count = self.local_count = 0
        self.open = {}
        self.seen = {}

    def send(self, src, dst, **to):
        copy = pltpu.make_async_remote_copy(
            src_ref=src,
            dst_ref=dst,
            send_sem=self.sends.at[self.count],
            recv_sem=self.recvs.at[self.count],
            device_id=to,
            device_id_type=pl.DeviceIdType.MESH,
        )
        self.count += 1
        copy.start()
        self.open[id(copy)] = (copy, True)
        return copy

    def move(self, src, dst):
        copy = pltpu.make_async_copy(src, dst, self.locals.at[self.local_count])
        self.local_count += 1
        copy.start()
        self.open[id(copy)] = (copy, False)
        return copy

    def left(self, copy):
        if id(copy) in self.open:
            copy, remote = self.open.pop(id(copy))
            self.seen[id(copy), "left"] = copy
            copy.wait_send() if remote else copy.wait()

    def arrived(self, copy):
        if (id(copy), "in") not in self.seen:
            self.seen[id(copy), "in"] = copy
            copy.wait_recv()

    def close(self):
        for copy, _ in list(self.open.values()):
            self.left(copy)


def greet(c, z, nc, nz):
    barrier = pltpu.get_barrier_semaphore()
    for d in range(1, nc):
        pl.semaphore_signal(
            barrier, inc=1, device_id={"ctx": c ^ d}, device_id_type=pl.DeviceIdType.MESH
        )
    for s in range(1, nz):
        pl.semaphore_signal(
            barrier, inc=1, device_id={"fsdp": z ^ s}, device_id_type=pl.DeviceIdType.MESH
        )
    pl.semaphore_wait(barrier, nc - 1 + nz - 1)


def kdot(left, right, dims=((1,), (0,)), precision=None):
    return lax.dot_general(
        left, right, (dims, ((), ())), preferred_element_type=exact, precision=precision
    )


def slots_of(cfg, mask_rows, upper):
    rank = kdot(mask_rows.astype(low), upper)
    return jnp.where(mask_rows > 0, rank, 0.0)


def plane_ranks(cfg, routes, z):
    nc, tokens = cfg["nc"], cfg["tokens"]
    expert = lax.broadcasted_iota(jnp.int32, (nc, tokens), 0) * cfg["exp_local"] + z // cfg["split"]
    mask = jnp.zeros((nc, tokens), exact)
    for k in range(cfg["top"]):
        mask = jnp.where(routes[k : k + 1, :] == expert, 1.0, mask)
    upper = jnp.where(
        lax.broadcasted_iota(jnp.int32, (tokens, tokens), 0)
        <= lax.broadcasted_iota(jnp.int32, (tokens, tokens), 1),
        1.0,
        0.0,
    ).astype(low)
    return slots_of(cfg, mask, upper)


def fill_hot(cfg, ranks, hot_ref):
    cap, tokens = cfg["cap"], cfg["tokens"]
    number = lax.broadcasted_iota(jnp.int32, (cap, tokens), 0).astype(exact) + 1.0
    for k in range(cfg["nc"]):
        hit = jnp.where(ranks[k : k + 1, :] == number, 1.0, 0.0)
        hot_ref[k * cap : (k + 1) * cap, :] = hit.astype(low)


def front_kernel(
    cfg,
    x_ref, wq_ref, wk_ref, wv_ref, wo_ref, gt_ref, rt_ref, ro_ref, cot_ref, gp_ref, up_ref, dp_ref, cos_ref, sin_ref,
    a1_out, w_full, raw_out, stat_out, rot_out, ob_out, wo_full, r1_out, r_all, g_all, t_all,
    gate_full, up_full, down_full, cot_rows, cot_near, in_rows, in_near,
    xbuf, wbuf, obw, gbuf, gfull, rbuf, tbuf, raw, stat, total, rq, rk, rot, opos, odev, orecv, r1, a2, cbuf, abuf, hot, cs,
    sends, recvs, locals_,
):
    nc, nz, tokens, width = cfg["nc"], cfg["nz"], cfg["tokens"], cfg["width"]
    cols, rows_w, length, cap = cfg["cols"], cfg["rows_w"], cfg["length"], cfg["cap"]
    hs = 128
    heads = cols // hs
    half = tokens // 2
    block = cfg["block"]
    blocks = length // block
    c, z = lax.axis_index("ctx"), lax.axis_index("fsdp")
    links = Links(sends, recvs, locals_)
    ds = pl.ds
    same = [d for d in range(2, nc, 2)]

    own = []
    own.append(links.move(x_ref, xbuf.at[ds(c * tokens, tokens)]))
    for j, ref in enumerate((wq_ref, wk_ref, wv_ref)):
        at = pl.multiple_of(c * cols, 128)
        own.append(links.move(ref.at[:, ds(at, cols)], wbuf.at[j, c, z]))
    own.append(links.move(wo_ref, obw.at[c, z]))
    own.append(links.move(gt_ref, gbuf.at[c, z]))
    own.append(links.move(rt_ref, rbuf.at[c, z]))
    own.append(links.move(ro_ref, tbuf.at[c, z]))
    own.append(links.move(cot_ref, cbuf.at[0]))
    mine = links.move(gp_ref.at[z], gate_full.at[z])
    mine_up = links.move(up_ref.at[z], up_full.at[z])
    mine_down = links.move(dp_ref.at[z], down_full.at[z])
    greet(c, z, nc, nz)

    slices = []
    for d in range(1, nc):
        peer = c ^ d
        at = pl.multiple_of(peer * cols, 128)
        for j, ref in enumerate((wq_ref, wk_ref, wv_ref)):
            slices.append(links.send(ref.at[:, ds(at, cols)], wbuf.at[j, c, z], ctx=peer))
    small_z = []
    for s in range(1, nz):
        for src, dst in ((gt_ref, gbuf), (rt_ref, rbuf), (ro_ref, tbuf)):
            small_z.append(links.send(src, dst.at[c, z], fsdp=z ^ s))
    x_at = xbuf.at[ds(c * tokens, tokens)]
    x_same = {d: links.send(x_ref, x_at, ctx=c ^ d) for d in same}
    x_side = [links.send(x_ref, x_at, ctx=c ^ 1)]
    for copy in own:
        links.left(copy)

    for copy in slices:
        links.arrived(copy)
    w_near = {}

    def w_send(s, bit):
        place = wbuf.at[:, :, z ^ s]
        w_near[s | bit] = links.send(place, place, fsdp=z ^ bit)

    steps = bits_down(nz)
    for bit in steps:
        w_send(0, bit)
    wo_near, cot_copies = {}, {}

    def wo_send(s, bit):
        place = obw.at[c, z ^ s]
        wo_near[s | bit] = links.send(place, place, fsdp=z ^ bit)

    def cot_send(s, bit):
        cot_copies[s | bit] = links.send(cbuf.at[s], cbuf.at[s | bit], fsdp=z ^ bit)

    for copy in small_z:
        links.arrived(copy)
    small_c = []
    for d in range(1, nc):
        for buf in (gbuf, rbuf, tbuf):
            small_c.append(links.send(buf.at[c], buf.at[c], ctx=c ^ d))
    for d in same:
        links.arrived(x_same[d])
        place = xbuf.at[ds((c ^ d) * tokens, tokens)]
        x_side.append(links.send(place, place, ctx=c ^ 1))

    def forward(waits, send):
        for at, bit in enumerate(steps):
            held = [0]
            for earlier in steps[:at]:
                held += [s | earlier for s in held]
            for s in held[1:]:
                links.arrived(waits[s])
                send(s, bit)

    forward(w_near, w_send)
    for bit in steps:
        wo_send(0, bit)
    for bit in steps:
        cot_send(0, bit)
    for copy in small_c:
        links.arrived(copy)
    per = 128 // rows_w
    groups = nz // per
    for k in range(nc):
        for g in range(groups):
            tile = gbuf[k, g * per]
            for p in range(1, per):
                tile = tile + gbuf[k, g * per + p]
            at = (k * groups + g) * 128
            gfull[:, at : at + 128] = tile
    for copy in x_side:
        links.arrived(copy)
    for copy in list(x_same.values()) + x_side:
        links.left(copy)

    chunk = cfg["chunk"]

    def norm_rows(i, _):
        at = pl.multiple_of(i * chunk, chunk)
        v = xbuf[ds(at, chunk), :].astype(exact)
        v = v * lax.rsqrt(jnp.mean(v * v, axis=-1, keepdims=True) + epsilon) * gfull[0:1, :]
        xbuf[ds(at, chunk), :] = v.astype(low)
        return 0

    lax.fori_loop(0, length // chunk, norm_rows, 0)
    a1_copy = links.move(xbuf, a1_out)

    last = steps[-1]
    for s in range(1, nz):
        if s & last:
            links.arrived(w_near[s])
    experts_in = []
    for s in range(1, nz):
        experts_in.append(links.send(gp_ref.at[z ^ s], gate_full.at[z], fsdp=z ^ s))
    w_copy = links.move(wbuf, w_full)

    one_row = lax.broadcasted_iota(jnp.int32, (8, cols), 0)
    pick_q = jnp.where(one_row == 0, 1.0, 0.0)
    pick_k = jnp.where(one_row == 1, 1.0, 0.0)
    best = lax.Precision.HIGHEST

    def project(i, _):
        at = pl.multiple_of(i * block, block)
        rows = xbuf[ds(at, block), :]
        sums = jnp.zeros((8, block), exact)
        for j in range(3):
            weight = wbuf[j].reshape(width, cols)
            v = kdot(rows, weight)
            raw[ds(at, block), j * cols : (j + 1) * cols] = v
            if j < 2:
                sums += kdot(pick_k if j else pick_q, v * v, ((1,), (1,)), best)
        stat[c, :, ds(at, block)] = sums
        return 0

    lax.fori_loop(0, blocks, project, 0)
    raw_copy = links.move(raw, raw_out)
    stats = [links.send(stat.at[c], stat.at[c], ctx=c ^ d) for d in range(1, nc)]
    forward(wo_near, wo_send)
    for s in range(1, nz):
        if s & last:
            links.arrived(wo_near[s])
    wo_same = {d: links.send(obw.at[c], obw.at[c], ctx=c ^ d) for d in same}
    wo_side = [links.send(obw.at[c], obw.at[c], ctx=c ^ 1)]
    for copy in stats:
        links.arrived(copy)
    summed = stat[0]
    for k in range(1, nc):
        summed += stat[k]
    total[...] = summed
    row8 = lax.broadcasted_iota(jnp.int32, (8, hs), 0)

    def columns(i, _):
        at = pl.multiple_of(i * block, block)
        part = total[:, ds(at, block)]
        for row, dst in ((0, rq), (1, rk)):
            sel = jnp.where(row8 == row, 1.0, 0.0)
            ms = kdot(part, sel, ((0,), (0,)), best)
            dst[ds(at, block), :] = lax.rsqrt(ms / width + epsilon)
        return 0

    lax.fori_loop(0, blocks, columns, 0)
    stat_copy = links.move(total, stat_out)

    def turn(i, _):
        d, side = i // 2, i % 2
        at = pl.multiple_of(d * tokens + side * half, half)
        to = pl.multiple_of(jnp.where(side == 0, d, 2 * nc - 1 - d) * half, half)
        cosine, sine = cos_ref[ds(at, half), :], sin_ref[ds(at, half), :]
        for h in range(heads):
            for j, scale in ((0, rq), (1, rk)):
                lane = j * cols + h * hs
                gain = gfull[1 + j : 2 + j, ds(pl.multiple_of(c * cols + h * hs, hs), hs)]
                v = raw[ds(at, half), lane : lane + hs] * scale[ds(at, half), :] * gain
                v = v * cosine + pltpu.roll(v, hs // 2, 1) * sine
                rot[j, ds(to, half), h * hs : (h + 1) * hs] = v.astype(low)
        rot[2, ds(to, half), :] = raw[ds(at, half), 2 * cols : 3 * cols].astype(low)
        return 0

    lax.fori_loop(0, 2 * nc, turn, 0)
    rot_copy = links.move(rot, rot_out)
    forward(cot_copies, cot_send)
    for s in range(1, nz):
        experts_in.append(links.send(up_ref.at[z ^ s], up_full.at[z], fsdp=z ^ s))

    scale = hs ** -0.5
    for h in range(heads):
        lanes = slice(h * hs, (h + 1) * hs)
        for i in range(blocks):
            count = (i + 1) * block
            q = rot[0, i * block : count, lanes]
            s = kdot(q, rot[1, :count, lanes], ((1,), (1,))) * scale
            row = lax.broadcasted_iota(jnp.int32, (block, count), 0) + i * block
            col = lax.broadcasted_iota(jnp.int32, (block, count), 1)
            s = jnp.where(col <= row, s, neg_large)
            p = jnp.exp(s - jnp.max(s, axis=-1, keepdims=True))
            p = p * (1.0 / jnp.sum(p, axis=-1, keepdims=True))
            opos[i * block : count, lanes] = kdot(p.astype(low), rot[2, :count, lanes]).astype(low)

    def place(i, _):
        d, side = i // 2, i % 2
        to = pl.multiple_of(d * tokens + side * half, half)
        at = pl.multiple_of(jnp.where(side == 0, d, 2 * nc - 1 - d) * half, half)
        odev[ds(to, half), :] = opos[ds(at, half), :]
        return 0

    lax.fori_loop(0, 2 * nc, place, 0)
    ob_copy = links.move(odev, ob_out)
    mixed = []
    for d in range(1, nc):
        src = odev.at[ds((c ^ d) * tokens, tokens)]
        mixed.append(links.send(src, orecv.at[c], ctx=c ^ d))
    own_mixed = links.move(odev.at[ds(c * tokens, tokens)], orecv.at[c])
    for d in same:
        links.arrived(wo_same[d])
        place_at = obw.at[c ^ d]
        wo_side.append(links.send(place_at, place_at, ctx=c ^ 1))

    for s in range(1, nz):
        if s & last:
            links.arrived(cot_copies[s])
    near_copy = links.move(cbuf, cot_near)
    rows_sent = []
    slot_busy = [[], []]

    def dispatch(s, near, landing):
        slot = s % 2
        for copy in slot_busy[slot]:
            links.left(copy)
        fill_hot(cfg, plane_ranks(cfg, tbuf[c, z ^ s], z), hot)
        cs[slot] = kdot(hot[...], near[s]).astype(low)
        busy = []
        for d in range(1, nc):
            src = cs.at[slot, ds((c ^ d) * cap, cap)]
            copy = links.send(src, landing.at[s, c], ctx=c ^ d)
            rows_sent.append(copy)
            busy.append(copy)
        busy.append(links.move(cs.at[slot, ds(c * cap, cap)], landing.at[s, c]))
        slot_busy[slot] = busy

    for s in range(nz):
        dispatch(s, cbuf, cot_rows)

    for copy in wo_side:
        links.arrived(copy)
    wo_copy = links.move(obw, wo_full)
    for copy in mixed:
        links.arrived(copy)
    links.left(own_mixed)
    r1[...] = jnp.zeros_like(r1)

    def mix(k, _):
        r1[...] += kdot(orecv[k], obw[k].reshape(cols, width))
        return 0

    lax.fori_loop(0, nc, mix, 0)
    xin = links.move(x_ref, a2)
    links.left(xin)
    v = r1[...] + a2[...].astype(exact)
    r1[...] = v
    n2 = v * lax.rsqrt(jnp.mean(v * v, axis=-1, keepdims=True) + epsilon)
    abuf[0] = (n2 * gfull[3:4, :]).astype(low)
    in_copies = {}

    def in_send(s, bit):
        in_copies[s | bit] = links.send(abuf.at[s], abuf.at[s | bit], fsdp=z ^ bit)

    for bit in steps:
        in_send(0, bit)
    links.move(r1, r1_out)
    dispatch(0, abuf, in_rows)
    forward(in_copies, in_send)
    for s in range(1, nz):
        experts_in.append(links.send(dp_ref.at[z ^ s], down_full.at[z], fsdp=z ^ s))
    links.move(rbuf, r_all)
    links.move(gfull, g_all)
    links.move(tbuf, t_all)
    for s in range(1, nz):
        links.arrived(in_copies[s])
        dispatch(s, abuf, in_rows)
    links.move(abuf, in_near)
    for copy in experts_in + rows_sent:
        links.arrived(copy)
    links.close()


def front(cfg, x, w_query, w_key, w_value, w_out, gains, router, routes, cot, gate_pieces, up_pieces, down_pieces, cosine, sine):
    nc, nz, tokens, width = cfg["nc"], cfg["nz"], cfg["tokens"], cfg["width"]
    cols, rows_w, length, cap = cfg["cols"], cfg["rows_w"], cfg["length"], cfg["cap"]
    rows, part = gate_pieces.shape[1:]
    rows_d = down_pieces.shape[1]
    shape = jax.ShapeDtypeStruct
    any_, vmem = pl.BlockSpec(memory_space=pl.ANY), pl.BlockSpec(memory_space=pltpu.VMEM)
    top_rows = routes.shape[0]
    outs = [
        shape((length, width), low),
        shape((3, nc, nz, rows_w, cols), low),
        shape((length, 3 * cols), exact),
        shape((8, length), exact),
        shape((3, length, cols), low),
        shape((length, cols), low),
        shape((nc, nz, rows_w, width), low),
        shape((tokens, width), exact),
        shape((nc, nz, rows_w, 128), low),
        shape((8, width), exact),
        shape((nc, nz, top_rows, tokens), jnp.int32),
        shape((nz, rows, part), low),
        shape((nz, rows, part), low),
        shape((nz, rows_d, width), low),
        shape((nz, nc, cap, width), low),
        shape((nz, tokens, width), low),
        shape((nz, nc, cap, width), low),
        shape((nz, tokens, width), low),
    ]
    scratch = [
        pltpu.VMEM((length, width), low),
        pltpu.VMEM((3, nc, nz, rows_w, cols), low),
        pltpu.VMEM((nc, nz, rows_w, width), low),
        pltpu.VMEM((nc, nz, 8, 128), exact),
        pltpu.VMEM((8, width), exact),
        pltpu.VMEM((nc, nz, rows_w, 128), low),
        pltpu.VMEM((nc, nz, top_rows, tokens), jnp.int32),
        pltpu.VMEM((length, 3 * cols), exact),
        pltpu.VMEM((nc, 8, length), exact),
        pltpu.VMEM((8, length), exact),
        pltpu.VMEM((length, 128), exact),
        pltpu.VMEM((length, 128), exact),
        pltpu.VMEM((3, length, cols), low),
        pltpu.VMEM((length, cols), low),
        pltpu.VMEM((length, cols), low),
        pltpu.VMEM((nc, tokens, cols), low),
        pltpu.VMEM((tokens, width), exact),
        pltpu.VMEM((tokens, width), low),
        pltpu.VMEM((nz, tokens, width), low),
        pltpu.VMEM((nz, tokens, width), low),
        pltpu.VMEM((nc * cap, tokens), low),
        pltpu.VMEM((2, nc * cap, width), low),
        pltpu.SemaphoreType.DMA((cfg["copies"],)),
        pltpu.SemaphoreType.DMA((cfg["copies"],)),
        pltpu.SemaphoreType.DMA((64,)),
    ]
    return pl.pallas_call(
        functools.partial(front_kernel, cfg),
        out_shape=outs,
        in_specs=[any_] * 12 + [vmem] * 2,
        out_specs=[any_] * len(outs),
        scratch_shapes=scratch,
        compiler_params=pltpu.CompilerParams(
            collective_id=0, has_side_effects=True, vmem_limit_bytes=cfg["vmem"]
        ),
        name="front",
    )(x, w_query, w_key, w_value, w_out, gains, router, routes, cot, gate_pieces, up_pieces, down_pieces, cosine, sine)


def expert_kernel(
    cfg,
    rows_ref, cotr_ref, rt_ref, tb_ref, wg_ref, wu_ref, wd_ref, near_ref, cotn_ref, r1_ref, gain_ref,
    hidden_out, dr1_out, datt_out, dlog_out, fgain_out, gd_land, gg_land, gu_out,
    back, in_back, out_land, in_land, ebh, rbh,
    wg, wu, wd, rows, cotb, gin, dg, du, eb, rb, tile, ranks, hot, metab, dgs, dgl,
    sends, recvs, locals_,
):
    nc, nz, tokens, width = cfg["nc"], cfg["nz"], cfg["tokens"], cfg["width"]
    cap, part, split, exp_local = cfg["cap"], cfg["part"], cfg["split"], cfg["exp_local"]
    ch = nc * cap
    total = nz * ch
    c, z = lax.axis_index("ctx"), lax.axis_index("fsdp")
    links = Links(sends, recvs, locals_)
    ds = pl.ds
    expert = c * exp_local + z // split
    best = lax.Precision.HIGHEST
    peers = list(range(1, nc))

    loads = [links.move(wg_ref, wg), links.move(wu_ref, wu), links.move(wd_ref, wd)]
    loads.append(links.move(rows_ref, rows))
    cot_base = links.local_count
    links.local_count += nz
    send_base = links.count
    links.count += 2 * nz * (nc - 1)
    keep_base = links.local_count
    links.local_count += 2 * nz
    off_base = links.local_count
    links.local_count += 2 * nz

    def cot_load(s, slot):
        return pltpu.make_async_copy(
            cotr_ref.at[ds(s * ch, ch)], cotb.at[slot], locals_.at[cot_base + s]
        )

    def chunk_copies(s, which):
        buf, landing = ((ebh, back), (rbh, in_back))[which]
        base = send_base + which * nz * (nc - 1) + s * (nc - 1)
        out = []
        for d in peers:
            out.append(
                pltpu.make_async_remote_copy(
                    src_ref=buf.at[s, ds((c ^ d) * cap, cap)],
                    dst_ref=landing.at[s, c],
                    send_sem=sends.at[base + d - 1],
                    recv_sem=recvs.at[base + d - 1],
                    device_id={"ctx": c ^ d},
                    device_id_type=pl.DeviceIdType.MESH,
                )
            )
        return out

    def keep_copy(s, which):
        landing = (back, in_back)[which]
        return pltpu.make_async_copy(
            (ebh, rbh)[which].at[s, ds(c * cap, cap)],
            landing.at[s, c],
            locals_.at[keep_base + which * nz + s],
        )

    def off_copy(s, which):
        return pltpu.make_async_copy(
            (eb, rb)[which], (ebh, rbh)[which].at[s], locals_.at[off_base + which * nz + s]
        )

    cot_load(nz - 1, 0).start()
    greet(c, z, nc, nz)
    for copy in loads:
        links.left(copy)

    expert_rows = lax.broadcasted_iota(jnp.int32, (128, tokens), 0)
    upper = jnp.where(
        lax.broadcasted_iota(jnp.int32, (tokens, tokens), 0)
        <= lax.broadcasted_iota(jnp.int32, (tokens, tokens), 1),
        1.0,
        0.0,
    ).astype(low)

    def routed(block):
        chosen = jnp.zeros((128, tokens), exact)
        for k in range(cfg["top"]):
            chosen = jnp.where(block[k : k + 1, :] == expert_rows, 1.0, chosen)
        return chosen

    sub = min(256, ch)
    lane = lax.broadcasted_iota(jnp.int32, (sub, 128), 1)

    def work(i, _):
        s = nz - 1 - i
        slot = lax.rem(i, 2)

        @pl.when(i + 1 < nz)
        def _():
            cot_load(s - 1, 1 - slot).start()

        for k in range(nc):
            block = tb_ref[k, z ^ s]
            found = jnp.where(block == expert, 1.0, 0.0)
            ranks[k : k + 1, :] = jnp.max(found, axis=0, keepdims=True)
        ranks[...] = slots_of(cfg, ranks[...], upper)
        fill_hot(cfg, ranks[...], hot)
        for k in range(nc):
            chosen = routed(tb_ref[k, z ^ s]).astype(low)
            metab[k * cap : (k + 1) * cap, :] = kdot(
                hot[k * cap : (k + 1) * cap, :], chosen, ((1,), (1,))
            )
        cot_load(s, slot).wait()

        def some_rows(j, _):
            here = pl.multiple_of(j * sub, sub)
            at = pl.multiple_of(s * ch + j * sub, sub)
            span, to = ds(here, sub), ds(at, sub)
            block = rows[to, :]
            logits = kdot(block, rt_ref[...], ((1,), (1,)))
            logits = jnp.where(metab[span, :] > 0.5, logits, neg_large)
            weight = jnp.exp(logits - jnp.max(logits, axis=-1, keepdims=True))
            gate = jnp.sum(jnp.where(lane == expert, weight, 0.0), axis=-1, keepdims=True)
            gate = gate / jnp.sum(weight, axis=-1, keepdims=True)
            g = kdot(block, wg[...])
            u = kdot(block, wu[...])
            sg = 1.0 / (1.0 + jnp.exp(-g))
            act = g * sg
            inner = (act * u).astype(low)
            gin[to, :] = (inner.astype(exact) * gate).astype(low)
            eb[span, :] = kdot(inner, wd[...]).astype(low)
            dinner = kdot(cotb[slot, span, :], wd[...], ((1,), (1,))) * gate
            dg_low = (dinner * u * sg * (1.0 + g * (1.0 - sg))).astype(low)
            du_low = (dinner * act).astype(low)
            dg[to, :] = dg_low
            du[to, :] = du_low
            rb[span, :] = (
                kdot(dg_low, wg[...], ((1,), (1,))) + kdot(du_low, wu[...], ((1,), (1,)))
            ).astype(low)
            return 0

        lax.fori_loop(0, ch // sub, some_rows, 0)
        for which in (0, 1):
            off_copy(s, which).start()
        for which in (0, 1):
            off_copy(s, which).wait()
            for copy in chunk_copies(s, which):
                copy.start()
            keep_copy(s, which).start()
        return 0

    lax.fori_loop(0, nz, work, 0)

    rows_d = part // nz
    step = 256 if nz * ch <= 2048 else 128
    tile_base = links.local_count
    links.local_count += width // step

    def tile_load(k):
        return pltpu.make_async_copy(
            cotr_ref.at[:, ds(k * step, step)], tile.at[lax.rem(k, 2)], locals_.at[tile_base + k]
        )

    tile_load(0).start()

    def down_tile(k, _):
        @pl.when(k + 1 < width // step)
        def _():
            tile_load(k + 1).start()

        tile_load(k).wait()
        at = pl.multiple_of(k * step, step)
        wd[:, ds(at, step)] = kdot(gin[...], tile[lax.rem(k, 2)], ((0,), (0,))).astype(low)
        return 0

    lax.fori_loop(0, width // step, down_tile, 0)
    grads_out = []
    for s in range(1, nz):
        src = wd.at[ds(pl.multiple_of((z ^ s) * rows_d, rows_d), rows_d)]
        grads_out.append(links.send(src, gd_land.at[z], fsdp=z ^ s))
    links.move(wd.at[ds(pl.multiple_of(z * rows_d, rows_d), rows_d)], gd_land.at[z])
    rows_g = width // nz

    def rows_tile(left, dst):
        def one(k, _):
            at = pl.multiple_of(k * step, step)
            dst[ds(at, step), :] = kdot(rows[:, ds(at, step)], left[...], ((0,), (0,))).astype(low)
            return 0

        lax.fori_loop(0, width // step, one, 0)

    rows_tile(dg, wg)
    for s in range(1, nz):
        src = wg.at[ds(pl.multiple_of((z ^ s) * rows_g, rows_g), rows_g)]
        grads_out.append(links.send(src, gg_land.at[z], fsdp=z ^ s))
    links.move(wg.at[ds(pl.multiple_of(z * rows_g, rows_g), rows_g)], gg_land.at[z])
    rows_tile(du, wu)
    links.move(wu, gu_out)

    spare = {}
    at = 0
    for name, count in (
        ("back", ch), ("in_back", ch), ("near", tokens), ("cot", tokens), ("out0", tokens),
        ("in0", tokens),
    ):
        spare[name] = rows.at[at : at + count]
        at += count
    stage = {0: (spare["out0"], spare["in0"]), 1: (cotb.at[0, 0:tokens], cotb.at[1, 0:tokens])}
    extra = (cotb.at[0, tokens : 2 * tokens], cotb.at[1, tokens : 2 * tokens])
    pick_rows = lax.broadcasted_iota(jnp.int32, (nc, 128), 0)
    pick_lane = lax.broadcasted_iota(jnp.int32, (nc, 128), 1)
    homeward = {}
    gate_home = {}
    busy = {0: [], 1: []}
    gates_own = None
    sums = None
    for s in range(nz - 1, -1, -1):
        for which in (0, 1):
            out = chunk_copies(s, which)
            for copy in out:
                copy.wait_recv()
            keep_copy(s, which).wait()
        fetch = []
        for k in range(nc):
            fetch.append(links.move(back.at[s, k], rows.at[k * cap : (k + 1) * cap]))
            fetch.append(links.move(in_back.at[s, k], rows.at[ch + k * cap : ch + (k + 1) * cap]))
        fetch.append(links.move(near_ref.at[s], spare["near"]))
        fetch.append(links.move(cotn_ref.at[s], spare["cot"]))
        block = tb_ref[c, z ^ s]
        fill_hot(cfg, plane_ranks(cfg, block, z), hot)
        chosen = routed(block)
        for copy in fetch:
            links.left(copy)
        logits = kdot(rt_ref[...], spare["near"][...], ((1,), (1,)))
        logits = jnp.where(chosen > 0.5, logits, neg_large)
        weight = jnp.exp(logits - jnp.max(logits, axis=0, keepdims=True))
        gates = weight / jnp.sum(weight, axis=0, keepdims=True)
        sel = jnp.where(pick_lane == pick_rows * exp_local + z // split, 1.0, 0.0)
        plane = kdot(sel, gates, ((1,), (0,)), best)
        slot_grad = kdot(spare["back"][...], spare["cot"][...], ((1,), (1,)))
        for k in range(nc):
            span = slice(k * cap, (k + 1) * cap)
            hit = hot[span, :].astype(exact)
            dgs[s, k : k + 1, :] = jnp.sum(hit * slot_grad[span, :], axis=0, keepdims=True)
        in_part = kdot(hot[...], spare["in_back"][...], ((0,), (0,)))
        for k in range(nc):
            span = slice(k * cap, (k + 1) * cap)
            hot[span, :] = (hot[span, :].astype(exact) * plane[k : k + 1, :]).astype(low)
        out_part = kdot(hot[...], spare["back"][...], ((0,), (0,)))
        lowest = s & -s
        bit = 1
        while bit < nz and (s == 0 or bit < lowest):
            for copy in homeward[s | bit]:
                links.arrived(copy)
            got = [links.move(out_land.at[s | bit], extra[0]), links.move(in_land.at[s | bit], extra[1])]
            for copy in got:
                links.left(copy)
            out_part += extra[0][...].astype(exact)
            in_part += extra[1][...].astype(exact)
            bit *= 2
        if s:
            slot = s % 2
            for copy in busy[slot]:
                links.left(copy)
            stage[slot][0][...] = out_part.astype(low)
            stage[slot][1][...] = in_part.astype(low)
            homeward[s] = [
                links.send(stage[slot][0], out_land.at[s], fsdp=z ^ lowest),
                links.send(stage[slot][1], in_land.at[s], fsdp=z ^ lowest),
            ]
            busy[slot] = homeward[s]
            gate_home[s] = links.send(dgs.at[s], dgl.at[s], fsdp=z ^ s)
        else:
            gates_own = gates
            sums = (out_part, in_part)

    dgate = jnp.zeros((128, tokens), exact)
    for s in range(nz):
        if s:
            links.arrived(gate_home[s])
        here = dgl[s] if s else dgs[0]
        sel = jnp.where(pick_lane == pick_rows * exp_local + (z ^ s) // split, 1.0, 0.0)
        dgate += kdot(sel, here, ((0,), (0,)), best)
    dchosen = gates_own * (dgate - jnp.sum(gates_own * dgate, axis=0, keepdims=True))
    dlog = dchosen.astype(low)
    hot[0:128, :] = dlog
    dlog_copy = links.move(hot.at[0:128], dlog_out)
    out_part, in_part = sums
    da2 = in_part + kdot(dlog, rt_ref[...], ((0,), (0,)))
    r1 = r1_ref[...]
    for copies in busy.values():
        for copy in copies:
            links.left(copy)
    stage[0][0][...] = (r1 + out_part).astype(low)
    links.move(stage[0][0], hidden_out)
    rs = lax.rsqrt(jnp.mean(r1 * r1, axis=-1, keepdims=True) + epsilon)
    n2 = r1 * rs
    dm = da2 * gain_ref[3:4, :]
    fgain_out[...] = jnp.broadcast_to(jnp.sum(da2 * n2, axis=0, keepdims=True), (8, width))
    inner_mean = jnp.mean(dm * n2, axis=-1, keepdims=True)
    dr1 = spare["cot"][...].astype(exact) + rs * (dm - n2 * inner_mean)
    dr1_out[...] = dr1
    datt_out[...] = dr1.astype(low)
    for s in range(nz):
        for which in (0, 1):
            out = chunk_copies(s, which)
            for copy in out:
                copy.wait_send()
    for copy in grads_out:
        links.arrived(copy)
    links.close()


def run_experts(cfg, rows, cot_rows, router_t, routes, wg, wu, wd, near, cot_near, r1, gains):
    nc, nz, tokens, width = cfg["nc"], cfg["nz"], cfg["tokens"], cfg["width"]
    cap, part = cfg["cap"], cfg["part"]
    ch = nc * cap
    shape = jax.ShapeDtypeStruct
    any_, vmem = pl.BlockSpec(memory_space=pl.ANY), pl.BlockSpec(memory_space=pltpu.VMEM)
    outs = [
        (shape((tokens, width), low), any_),
        (shape((tokens, width), exact), vmem),
        (shape((tokens, width), low), vmem),
        (shape((128, tokens), low), any_),
        (shape((8, width), exact), vmem),
        (shape((nz, part // nz, width), low), any_),
        (shape((nz, width // nz, part), low), any_),
        (shape((width, part), low), any_),
        (shape((nz, nc, cap, width), low), any_),
        (shape((nz, nc, cap, width), low), any_),
        (shape((nz, tokens, width), low), any_),
        (shape((nz, tokens, width), low), any_),
        (shape((nz, ch, width), low), any_),
        (shape((nz, ch, width), low), any_),
    ]
    step = 256 if nz * ch <= 2048 else 128
    scratch = [
        pltpu.VMEM((width, part), low),
        pltpu.VMEM((width, part), low),
        pltpu.VMEM((part, width), low),
        pltpu.VMEM((nz * ch, width), low),
        pltpu.VMEM((2, ch, width), low),
        pltpu.VMEM((nz * ch, part), low),
        pltpu.VMEM((nz * ch, part), low),
        pltpu.VMEM((nz * ch, part), low),
        pltpu.VMEM((ch, width), low),
        pltpu.VMEM((ch, width), low),
        pltpu.VMEM((2, nz * ch, step), low),
        pltpu.VMEM((nc, tokens), exact),
        pltpu.VMEM((ch, tokens), low),
        pltpu.VMEM((ch, 128), exact),
        pltpu.VMEM((nz, nc, tokens), exact),
        pltpu.VMEM((nz, nc, tokens), exact),
        pltpu.SemaphoreType.DMA((2 * nz * nc + 8 * nz,)),
        pltpu.SemaphoreType.DMA((2 * nz * nc + 8 * nz,)),
        pltpu.SemaphoreType.DMA((2 * nz * nc + 16 * nz + width // step + 16,)),
    ]
    return pl.pallas_call(
        functools.partial(expert_kernel, cfg),
        out_shape=[o[0] for o in outs],
        in_specs=[any_, any_, vmem, vmem, any_, any_, any_, any_, any_, vmem, vmem],
        out_specs=[o[1] for o in outs],
        scratch_shapes=scratch,
        compiler_params=pltpu.CompilerParams(
            collective_id=1, has_side_effects=True, vmem_limit_bytes=cfg["vmem"]
        ),
        name="experts",
    )(rows, cot_rows, router_t, routes, wg, wu, wd, near, cot_near, r1, gains)


def tables(nc, tokens, head_size):
    half = tokens // 2
    local = np.arange(tokens)
    device = np.arange(nc)[:, None]
    position = np.where(
        local < half, device * half + local, (2 * nc - 1 - device) * half + local - half
    ).reshape(-1)
    freq = np.float32(10000.0) ** (-np.arange(head_size // 2, dtype=np.float32) * (2.0 / head_size))
    angle = position.astype(np.float32)[:, None] * freq.astype(np.float32)
    cosine = np.concatenate([np.cos(angle), np.cos(angle)], axis=1)
    sine = np.concatenate([-np.sin(angle), np.sin(angle)], axis=1)
    return jnp.asarray(cosine, exact), jnp.asarray(sine, exact)


def body(
    hidden_in,
    cotangent,
    routes,
    attn_gain,
    query_gain,
    key_gain,
    ffn_gain,
    w_query,
    w_key,
    w_value,
    w_out,
    w_router,
    w_gate,
    w_up,
    w_down,
):
    tokens = hidden_in.shape[1]
    width = hidden_in.shape[2]
    head_size = width // HEADS
    ctx_count = lax.axis_size("ctx")
    z_count = lax.axis_size("fsdp")
    both = ("ctx", "fsdp")
    top = routes.shape[2]
    exp_local = w_gate.shape[0]
    split = z_count // exp_local
    hidden = w_gate.shape[2]
    part = hidden // split
    experts = exp_local * ctx_count
    capacity = tokens * top * 4 // (3 * experts)
    heads = HEADS // ctx_count
    cols = heads * head_size
    length = tokens * ctx_count
    scale = head_size ** (-0.5)
    c_index = lax.axis_index("ctx")
    z_index = lax.axis_index("fsdp")
    rows_w = w_query.shape[0]

    cfg = dict(
        nc=ctx_count,
        nz=z_count,
        tokens=tokens,
        width=width,
        cols=cols,
        rows_w=rows_w,
        length=length,
        cap=capacity,
        top=top,
        exp_local=exp_local,
        split=split,
        block=math.gcd(length, 256 if length <= 2048 else 128),
        chunk=math.gcd(length, 64),
        copies=(ctx_count - 1) * (8 + 2 * z_count) + (z_count - 1) * 12 + 2 * ctx_count + 8,
        part=part,
        vmem=62 * 2**20,
    )
    index = c_index * z_count + z_index
    per = 128 // rows_w
    gains = jnp.stack([attn_gain, query_gain, key_gain, ffn_gain]).astype(exact)
    gains = lax.dynamic_update_slice(
        jnp.zeros((8, 128), exact), gains, (0, jnp.mod(index, per) * rows_w)
    )
    router_tile = jnp.pad(w_router, ((0, 0), (0, 128 - experts)))
    route_tile = jnp.pad(routes[0].T, ((0, 8 - top), (0, 0)), constant_values=-1)

    def pieces_of(weight):
        rows = weight.shape[1]
        weight = weight.reshape(exp_local, rows, z_count, split, part // z_count)
        return weight.transpose(0, 3, 1, 2, 4).reshape(z_count, rows, part)

    (
        attn_all, w_full, raw, squares, rot, out_heads, wo_full, resid_one,
        router_full, gains, routes_all, gate_full, up_full, down_full, cot_rows, cot_near,
        input_rows, input_near,
    ) = front(
        cfg, hidden_in[0], w_query, w_key, w_value, w_out, gains, router_tile, route_tile,
        cotangent[0], pieces_of(w_gate), pieces_of(w_up),
        w_down.reshape(z_count, -1, width), *tables(ctx_count, tokens, head_size),
    )
    gate_full = gate_full.reshape(-1, part)
    up_full = up_full.reshape(-1, part)
    down_full = down_full.reshape(-1, width)
    ffn_input = input_near[0]
    router_t = router_full.reshape(width, 128).T
    (
        resid_two, grad_one, attn_grad_low, logit_grad, ffn_gain_grad, down_land, gate_land,
        up_grad, *_,
    ) = run_experts(
        cfg, input_rows.reshape(-1, width), cot_rows.reshape(-1, width), router_t, routes_all,
        gate_full, up_full, down_full, input_near, cot_near, resid_one, gains,
    )
    out_hidden = resid_two[None]
    ffn_gain_grad = ffn_gain_grad[0]
    router_grad = lax.dot_general(
        ffn_input, logit_grad[:experts], (((0,), (1,)), ((), ())), preferred_element_type=exact
    )

    def whole_out(grad):
        grad = grad.reshape(exp_local, split, -1, z_count, part // z_count)
        return grad.transpose(0, 2, 3, 1, 4).reshape(exp_local, -1, hidden).astype(exact)

    grad_down = down_land.reshape(exp_local, -1, width).astype(exact)
    grad_gate = whole_out(gate_land)
    grad_up = whole_out(spread(up_grad.reshape(z_count, -1, part)))
    w_full = w_full.reshape(3, width, cols)
    out_full = wo_full.reshape(width, width)
    attn_scale = gains[0]
    query_scale = lax.dynamic_slice_in_dim(gains[1], c_index * cols, cols)
    key_scale = lax.dynamic_slice_in_dim(gains[2], c_index * cols, cols)
    def total_over_ctx(one, two):
        both_sums = jnp.stack([one, two])
        return jnp.sum(lax.all_gather(both_sums, "ctx", axis=0), axis=0)

    queries, keys = raw[:, :cols], raw[:, cols : 2 * cols]
    rms_two = lax.rsqrt(squares[:2] / width + epsilon)
    query_rms, key_rms = rms_two[0][:, None], rms_two[1][:, None]
    query_normed, key_normed = queries * query_rms, keys * key_rms
    half = tokens // 2
    row = jnp.arange(length, dtype=jnp.int32)
    device, local = row // tokens, row % tokens
    positions = jnp.where(
        local < half, device * half + local, (2 * ctx_count - 1 - device) * half + local - half
    )
    cosine, sine = rotation(positions, head_size)

    def by_head(x):
        return x.reshape(length, heads, head_size)

    query_rot, key_rot, value_low = by_head(rot[0]), by_head(rot[1]), by_head(rot[2])
    allowed = (row[None, :] <= row[:, None])[None]
    scores = (
        jnp.einsum("qhd,khd->hqk", query_rot, key_rot, preferred_element_type=exact) * scale
    )
    scores = jnp.where(allowed, scores, neg_large)
    log_total = jax.nn.logsumexp(scores, axis=-1, keepdims=True)
    probs = jnp.exp(scores - log_total)
    probs_low = probs.astype(low)
    rows_in = hidden_in[0].astype(exact)
    attn_grad_all = gather_ctx(attn_grad_low).reshape(length, width)
    out_weight_grad = contract_rows(out_heads, attn_grad_all)
    grad_heads = contract_cols(attn_grad_low, out_full).astype(low)
    grad_heads = exchange(grad_heads.reshape(tokens, ctx_count, cols).transpose(1, 0, 2), "ctx")
    grad_heads = ordered(by_head(grad_heads), ctx_count)
    value_grad = jnp.einsum("hqk,qhd->khd", probs_low, grad_heads, preferred_element_type=exact)
    prob_grad = jnp.einsum("qhd,khd->hqk", grad_heads, value_low, preferred_element_type=exact)
    delta = jnp.sum(probs * prob_grad, axis=-1, keepdims=True)
    score_grad = (probs * (prob_grad - delta)).astype(low)
    query_rot_grad = scale * jnp.einsum(
        "hqk,khd->qhd", score_grad, key_rot, preferred_element_type=exact
    )
    key_rot_grad = scale * jnp.einsum(
        "hqk,qhd->khd", score_grad, query_rot, preferred_element_type=exact
    )
    query_back = rotate(placed(query_rot_grad, ctx_count), cosine, -sine).reshape(length, cols)
    key_back = rotate(placed(key_rot_grad, ctx_count), cosine, -sine).reshape(length, cols)
    value_grad_low = placed(value_grad.astype(low), ctx_count).reshape(length, cols)
    query_gain_grad = jnp.sum(query_back * query_normed, axis=0)
    key_gain_grad = jnp.sum(key_back * key_normed, axis=0)
    query_d, key_d = query_back * query_scale, key_back * key_scale
    inner_two = total_over_ctx(
        jnp.sum(query_d * query_normed, -1), jnp.sum(key_d * key_normed, -1)
    ) / width
    query_grad_low = (query_rms * (query_d - query_normed * inner_two[0][:, None])).astype(low)
    key_grad_low = (key_rms * (key_d - key_normed * inner_two[1][:, None])).astype(low)
    qkv_grad_low = jnp.concatenate([query_grad_low, key_grad_low, value_grad_low], axis=1)
    attn_input_grad = (
        contract_cols(query_grad_low, w_full[0])
        + contract_cols(key_grad_low, w_full[1])
        + contract_cols(value_grad_low, w_full[2])
    )
    qkv_weight_grad = contract_rows(attn_all, qkv_grad_low)
    attn_input_grad = scatter_ctx(attn_input_grad.reshape(ctx_count, tokens, width))
    _, normed_one, scale_one = rms_apply(rows_in, attn_scale)
    input_norm_grad, attn_gain_grad = rms_back(
        attn_input_grad, normed_one, scale_one, attn_scale
    )
    grad_hidden = (grad_one + input_norm_grad)[None]

    z_bits = bits_of("fsdp")
    pieces = qkv_weight_grad.reshape(ctx_count, z_count, rows_w, 3 * cols).transpose(1, 0, 2, 3)
    pieces = halved(pieces, "fsdp", z_bits).astype(low)
    pieces = exchange(pieces, "ctx").reshape(ctx_count, rows_w, 3, cols).astype(exact)
    pieces = pieces.transpose(2, 1, 0, 3).reshape(3, rows_w, width)
    grad_out = halved(out_weight_grad.reshape(z_count, rows_w, width), "fsdp", z_bits)
    sums = jnp.concatenate(
        [
            router_grad.reshape(ctx_count * z_count, rows_w * experts),
            ffn_gain_grad.reshape(-1, rows_w),
        ],
        axis=1,
    )
    sums = jnp.sum(exchange(sums, both), axis=0)
    grad_router = sums[: rows_w * experts].reshape(rows_w, experts)
    grad_ffn_gain = sums[rows_w * experts :]
    grad_attn_gain = jnp.sum(exchange(attn_gain_grad.reshape(-1, rows_w), both), axis=0)
    head_gains = jnp.stack([query_gain_grad, key_gain_grad], axis=1)
    head_gains = head_gains.reshape(z_count, rows_w, 2)
    head_gains = jnp.sum(exchange(head_gains, "fsdp"), axis=0)
    return (
        out_hidden,
        grad_hidden,
        grad_attn_gain,
        head_gains[:, 0],
        head_gains[:, 1],
        grad_ffn_gain,
        pieces[0],
        pieces[1],
        pieces[2],
        grad_out,
        grad_router,
        grad_gate,
        grad_up,
        grad_down,
    )


def solution(mesh):
    in_specs = (
        P("fsdp", "ctx", None),
        P("fsdp", "ctx", None),
        P("fsdp", "ctx", None),
        P(("ctx", "fsdp")),
        P(("ctx", "fsdp")),
        P(("ctx", "fsdp")),
        P(("ctx", "fsdp")),
        P(("ctx", "fsdp"), None),
        P(("ctx", "fsdp"), None),
        P(("ctx", "fsdp"), None),
        P(("ctx", "fsdp"), None),
        P(("ctx", "fsdp"), None),
        P("ctx", "fsdp", None),
        P("ctx", "fsdp", None),
        P("ctx", "fsdp", None),
    )
    out_specs = (
        P("fsdp", "ctx", None),
        P("fsdp", "ctx", None),
        P(("ctx", "fsdp")),
        P(("ctx", "fsdp")),
        P(("ctx", "fsdp")),
        P(("ctx", "fsdp")),
        P(("ctx", "fsdp"), None),
        P(("ctx", "fsdp"), None),
        P(("ctx", "fsdp"), None),
        P(("ctx", "fsdp"), None),
        P(("ctx", "fsdp"), None),
        P("ctx", "fsdp", None),
        P("ctx", "fsdp", None),
        P("ctx", "fsdp", None),
    )
    return jax.shard_map(body, mesh=mesh, in_specs=in_specs, out_specs=out_specs, check_vma=False)
```

```python
import functools
import math

import jax
import jax.numpy as jnp
import numpy as np
from jax import lax
from jax.experimental import pallas as pl
from jax.experimental.pallas import tpu as pltpu
from jax.sharding import PartitionSpec as P

HEADS = 16


epsilon = 1e-05
neg_large = -1e30
low = jnp.bfloat16
exact = jnp.float32


def exchange(x, axis):
    return lax.all_to_all(x, axis, split_axis=0, concat_axis=0, tiled=True)


def bits_down(count):
    return [1 << i for i in range(count.bit_length() - 1)][::-1]


class Links:
    def __init__(self, sends, recvs, locals_):
        self.sends, self.recvs, self.locals = sends, recvs, locals_
        self.count = self.local_count = 0
        self.open = {}
        self.seen = {}

    def send(self, src, dst, **to):
        copy = pltpu.make_async_remote_copy(
            src_ref=src,
            dst_ref=dst,
            send_sem=self.sends.at[self.count],
            recv_sem=self.recvs.at[self.count],
            device_id=to,
            device_id_type=pl.DeviceIdType.MESH,
        )
        self.count += 1
        copy.start()
        self.open[id(copy)] = (copy, True)
        return copy

    def move(self, src, dst):
        copy = pltpu.make_async_copy(src, dst, self.locals.at[self.local_count])
        self.local_count += 1
        copy.start()
        self.open[id(copy)] = (copy, False)
        return copy

    def left(self, copy):
        if id(copy) in self.open:
            copy, remote = self.open.pop(id(copy))
            self.seen[id(copy), "left"] = copy
            copy.wait_send() if remote else copy.wait()

    def arrived(self, copy):
        if (id(copy), "in") not in self.seen:
            self.seen[id(copy), "in"] = copy
            copy.wait_recv()

    def close(self):
        for copy, _ in list(self.open.values()):
            self.left(copy)


def greet(c, z, nc, nz):
    barrier = pltpu.get_barrier_semaphore()
    for d in range(1, nc):
        pl.semaphore_signal(
            barrier, inc=1, device_id={"ctx": c ^ d}, device_id_type=pl.DeviceIdType.MESH
        )
    for s in range(1, nz):
        pl.semaphore_signal(
            barrier, inc=1, device_id={"fsdp": z ^ s}, device_id_type=pl.DeviceIdType.MESH
        )
    pl.semaphore_wait(barrier, nc - 1 + nz - 1)


def kdot(left, right, dims=((1,), (0,)), precision=None):
    return lax.dot_general(
        left, right, (dims, ((), ())), preferred_element_type=exact, precision=precision
    )


def slots_of(cfg, mask_rows, upper):
    rank = kdot(mask_rows.astype(low), upper)
    return jnp.where(mask_rows > 0, rank, 0.0)


def plane_ranks(cfg, routes, z):
    nc, tokens = cfg["nc"], cfg["tokens"]
    expert = lax.broadcasted_iota(jnp.int32, (nc, tokens), 0) * cfg["exp_local"] + z // cfg["split"]
    mask = jnp.zeros((nc, tokens), exact)
    for k in range(cfg["top"]):
        mask = jnp.where(routes[k : k + 1, :] == expert, 1.0, mask)
    upper = jnp.where(
        lax.broadcasted_iota(jnp.int32, (tokens, tokens), 0)
        <= lax.broadcasted_iota(jnp.int32, (tokens, tokens), 1),
        1.0,
        0.0,
    ).astype(low)
    return slots_of(cfg, mask, upper)


def fill_hot(cfg, ranks, hot_ref):
    cap, tokens = cfg["cap"], cfg["tokens"]
    number = lax.broadcasted_iota(jnp.int32, (cap, tokens), 0).astype(exact) + 1.0
    for k in range(cfg["nc"]):
        hit = jnp.where(ranks[k : k + 1, :] == number, 1.0, 0.0)
        hot_ref[k * cap : (k + 1) * cap, :] = hit.astype(low)


def front_kernel(
    cfg,
    x_ref, wq_ref, wk_ref, wv_ref, wo_ref, gt_ref, rt_ref, ro_ref, cot_ref, gp_ref, up_ref, dp_ref, cos_ref, sin_ref,
    a1_out, w_full, raw_out, stat_out, rot_out, ob_out, wo_full, r1_out, r_all, g_all, t_all,
    gate_full, up_full, down_full, cot_rows, cot_near, in_rows, in_near,
    xbuf, wbuf, obw, gbuf, gfull, rbuf, tbuf, raw, stat, total, rq, rk, rot, opos, odev, orecv, r1, a2, cbuf, abuf, hot, cs,
    sends, recvs, locals_,
):
    nc, nz, tokens, width = cfg["nc"], cfg["nz"], cfg["tokens"], cfg["width"]
    cols, rows_w, length, cap = cfg["cols"], cfg["rows_w"], cfg["length"], cfg["cap"]
    hs = 128
    heads = cols // hs
    half = tokens // 2
    block = cfg["block"]
    blocks = length // block
    c, z = lax.axis_index("ctx"), lax.axis_index("fsdp")
    links = Links(sends, recvs, locals_)
    ds = pl.ds
    same = [d for d in range(2, nc, 2)]

    own = []
    own.append(links.move(x_ref, xbuf.at[ds(c * tokens, tokens)]))
    for j, ref in enumerate((wq_ref, wk_ref, wv_ref)):
        at = pl.multiple_of(c * cols, 128)
        own.append(links.move(ref.at[:, ds(at, cols)], wbuf.at[j, c, z]))
    own.append(links.move(wo_ref, obw.at[c, z]))
    own.append(links.move(gt_ref, gbuf.at[c, z]))
    own.append(links.move(rt_ref, rbuf.at[c, z]))
    own.append(links.move(ro_ref, tbuf.at[c, z]))
    own.append(links.move(cot_ref, cbuf.at[0]))
    mine = links.move(gp_ref.at[z], gate_full.at[z])
    mine_up = links.move(up_ref.at[z], up_full.at[z])
    mine_down = links.move(dp_ref.at[z], down_full.at[z])
    greet(c, z, nc, nz)

    slices = []
    for d in range(1, nc):
        peer = c ^ d
        at = pl.multiple_of(peer * cols, 128)
        for j, ref in enumerate((wq_ref, wk_ref, wv_ref)):
            slices.append(links.send(ref.at[:, ds(at, cols)], wbuf.at[j, c, z], ctx=peer))
    small_z = []
    for s in range(1, nz):
        for src, dst in ((gt_ref, gbuf), (rt_ref, rbuf), (ro_ref, tbuf)):
            small_z.append(links.send(src, dst.at[c, z], fsdp=z ^ s))
    x_at = xbuf.at[ds(c * tokens, tokens)]
    x_same = {d: links.send(x_ref, x_at, ctx=c ^ d) for d in same}
    x_side = [links.send(x_ref, x_at, ctx=c ^ 1)]
    for copy in own:
        links.left(copy)

    for copy in slices:
        links.arrived(copy)
    w_near = {}

    def w_send(s, bit):
        place = wbuf.at[:, :, z ^ s]
        w_near[s | bit] = links.send(place, place, fsdp=z ^ bit)

    steps = bits_down(nz)
    for bit in steps:
        w_send(0, bit)
    wo_near, cot_copies = {}, {}

    def wo_send(s, bit):
        place = obw.at[c, z ^ s]
        wo_near[s | bit] = links.send(place, place, fsdp=z ^ bit)

    def cot_send(s, bit):
        cot_copies[s | bit] = links.send(cbuf.at[s], cbuf.at[s | bit], fsdp=z ^ bit)

    for copy in small_z:
        links.arrived(copy)
    small_c = []
    for d in range(1, nc):
        for buf in (gbuf, rbuf, tbuf):
            small_c.append(links.send(buf.at[c], buf.at[c], ctx=c ^ d))
    for d in same:
        links.arrived(x_same[d])
        place = xbuf.at[ds((c ^ d) * tokens, tokens)]
        x_side.append(links.send(place, place, ctx=c ^ 1))

    def forward(waits, send):
        for at, bit in enumerate(steps):
            held = [0]
            for earlier in steps[:at]:
                held += [s | earlier for s in held]
            for s in held[1:]:
                links.arrived(waits[s])
                send(s, bit)

    forward(w_near, w_send)
    for bit in steps:
        wo_send(0, bit)
    for bit in steps:
        cot_send(0, bit)
    for copy in small_c:
        links.arrived(copy)
    per = 128 // rows_w
    groups = nz // per
    for k in range(nc):
        for g in range(groups):
            tile = gbuf[k, g * per]
            for p in range(1, per):
                tile = tile + gbuf[k, g * per + p]
            at = (k * groups + g) * 128
            gfull[:, at : at + 128] = tile
    for copy in x_side:
        links.arrived(copy)
    for copy in list(x_same.values()) + x_side:
        links.left(copy)

    chunk = cfg["chunk"]

    def norm_rows(i, _):
        at = pl.multiple_of(i * chunk, chunk)
        v = xbuf[ds(at, chunk), :].astype(exact)
        v = v * lax.rsqrt(jnp.mean(v * v, axis=-1, keepdims=True) + epsilon) * gfull[0:1, :]
        xbuf[ds(at, chunk), :] = v.astype(low)
        return 0

    lax.fori_loop(0, length // chunk, norm_rows, 0)
    a1_copy = links.move(xbuf, a1_out)

    last = steps[-1]
    for s in range(1, nz):
        if s & last:
            links.arrived(w_near[s])
    experts_in = []
    for s in range(1, nz):
        experts_in.append(links.send(gp_ref.at[z ^ s], gate_full.at[z], fsdp=z ^ s))
    w_copy = links.move(wbuf, w_full)

    one_row = lax.broadcasted_iota(jnp.int32, (8, cols), 0)
    pick_q = jnp.where(one_row == 0, 1.0, 0.0)
    pick_k = jnp.where(one_row == 1, 1.0, 0.0)
    best = lax.Precision.HIGHEST

    def project(i, _):
        at = pl.multiple_of(i * block, block)
        rows = xbuf[ds(at, block), :]
        sums = jnp.zeros((8, block), exact)
        for j in range(3):
            weight = wbuf[j].reshape(width, cols)
            v = kdot(rows, weight)
            raw[ds(at, block), j * cols : (j + 1) * cols] = v
            if j < 2:
                sums += kdot(pick_k if j else pick_q, v * v, ((1,), (1,)), best)
        stat[c, :, ds(at, block)] = sums
        return 0

    lax.fori_loop(0, blocks, project, 0)
    raw_copy = links.move(raw, raw_out)
    stats = [links.send(stat.at[c], stat.at[c], ctx=c ^ d) for d in range(1, nc)]
    forward(wo_near, wo_send)
    for s in range(1, nz):
        if s & last:
            links.arrived(wo_near[s])
    wo_same = {d: links.send(obw.at[c], obw.at[c], ctx=c ^ d) for d in same}
    wo_side = [links.send(obw.at[c], obw.at[c], ctx=c ^ 1)]
    for copy in stats:
        links.arrived(copy)
    summed = stat[0]
    for k in range(1, nc):
        summed += stat[k]
    total[...] = summed
    row8 = lax.broadcasted_iota(jnp.int32, (8, hs), 0)

    def columns(i, _):
        at = pl.multiple_of(i * block, block)
        part = total[:, ds(at, block)]
        for row, dst in ((0, rq), (1, rk)):
            sel = jnp.where(row8 == row, 1.0, 0.0)
            ms = kdot(part, sel, ((0,), (0,)), best)
            dst[ds(at, block), :] = lax.rsqrt(ms / width + epsilon)
        return 0

    lax.fori_loop(0, blocks, columns, 0)
    stat_copy = links.move(total, stat_out)

    def turn(i, _):
        d, side = i // 2, i % 2
        at = pl.multiple_of(d * tokens + side * half, half)
        to = pl.multiple_of(jnp.where(side == 0, d, 2 * nc - 1 - d) * half, half)
        cosine, sine = cos_ref[ds(at, half), :], sin_ref[ds(at, half), :]
        for h in range(heads):
            for j, scale in ((0, rq), (1, rk)):
                lane = j * cols + h * hs
                gain = gfull[1 + j : 2 + j, ds(pl.multiple_of(c * cols + h * hs, hs), hs)]
                v = raw[ds(at, half), lane : lane + hs] * scale[ds(at, half), :] * gain
                v = v * cosine + pltpu.roll(v, hs // 2, 1) * sine
                rot[j, ds(to, half), h * hs : (h + 1) * hs] = v.astype(low)
        rot[2, ds(to, half), :] = raw[ds(at, half), 2 * cols : 3 * cols].astype(low)
        return 0

    lax.fori_loop(0, 2 * nc, turn, 0)
    rot_copy = links.move(rot, rot_out)
    forward(cot_copies, cot_send)
    for s in range(1, nz):
        experts_in.append(links.send(up_ref.at[z ^ s], up_full.at[z], fsdp=z ^ s))

    scale = hs ** -0.5
    for h in range(heads):
        lanes = slice(h * hs, (h + 1) * hs)
        for i in range(blocks):
            count = (i + 1) * block
            q = rot[0, i * block : count, lanes]
            s = kdot(q, rot[1, :count, lanes], ((1,), (1,))) * scale
            row = lax.broadcasted_iota(jnp.int32, (block, count), 0) + i * block
            col = lax.broadcasted_iota(jnp.int32, (block, count), 1)
            s = jnp.where(col <= row, s, neg_large)
            p = jnp.exp(s - jnp.max(s, axis=-1, keepdims=True))
            p = p * (1.0 / jnp.sum(p, axis=-1, keepdims=True))
            opos[i * block : count, lanes] = kdot(p.astype(low), rot[2, :count, lanes]).astype(low)

    def place(i, _):
        d, side = i // 2, i % 2
        to = pl.multiple_of(d * tokens + side * half, half)
        at = pl.multiple_of(jnp.where(side == 0, d, 2 * nc - 1 - d) * half, half)
        odev[ds(to, half), :] = opos[ds(at, half), :]
        return 0

    lax.fori_loop(0, 2 * nc, place, 0)
    ob_copy = links.move(odev, ob_out)
    mixed = []
    for d in range(1, nc):
        src = odev.at[ds((c ^ d) * tokens, tokens)]
        mixed.append(links.send(src, orecv.at[c], ctx=c ^ d))
    own_mixed = links.move(odev.at[ds(c * tokens, tokens)], orecv.at[c])
    for d in same:
        links.arrived(wo_same[d])
        place_at = obw.at[c ^ d]
        wo_side.append(links.send(place_at, place_at, ctx=c ^ 1))

    for s in range(1, nz):
        if s & last:
            links.arrived(cot_copies[s])
    near_copy = links.move(cbuf, cot_near)
    rows_sent = []
    slot_busy = [[], []]

    def dispatch(s, near, landing):
        slot = s % 2
        for copy in slot_busy[slot]:
            links.left(copy)
        fill_hot(cfg, plane_ranks(cfg, tbuf[c, z ^ s], z), hot)
        cs[slot] = kdot(hot[...], near[s]).astype(low)
        busy = []
        for d in range(1, nc):
            src = cs.at[slot, ds((c ^ d) * cap, cap)]
            copy = links.send(src, landing.at[s, c], ctx=c ^ d)
            rows_sent.append(copy)
            busy.append(copy)
        busy.append(links.move(cs.at[slot, ds(c * cap, cap)], landing.at[s, c]))
        slot_busy[slot] = busy

    for s in range(nz):
        dispatch(s, cbuf, cot_rows)

    for copy in wo_side:
        links.arrived(copy)
    wo_copy = links.move(obw, wo_full)
    for copy in mixed:
        links.arrived(copy)
    links.left(own_mixed)
    r1[...] = jnp.zeros_like(r1)

    def mix(k, _):
        r1[...] += kdot(orecv[k], obw[k].reshape(cols, width))
        return 0

    lax.fori_loop(0, nc, mix, 0)
    xin = links.move(x_ref, a2)
    links.left(xin)
    v = r1[...] + a2[...].astype(exact)
    r1[...] = v
    n2 = v * lax.rsqrt(jnp.mean(v * v, axis=-1, keepdims=True) + epsilon)
    abuf[0] = (n2 * gfull[3:4, :]).astype(low)
    in_copies = {}

    def in_send(s, bit):
        in_copies[s | bit] = links.send(abuf.at[s], abuf.at[s | bit], fsdp=z ^ bit)

    for bit in steps:
        in_send(0, bit)
    links.move(r1, r1_out)
    dispatch(0, abuf, in_rows)
    forward(in_copies, in_send)
    for s in range(1, nz):
        experts_in.append(links.send(dp_ref.at[z ^ s], down_full.at[z], fsdp=z ^ s))
    links.move(rbuf, r_all)
    links.move(gfull, g_all)
    links.move(tbuf, t_all)
    for s in range(1, nz):
        links.arrived(in_copies[s])
        dispatch(s, abuf, in_rows)
    links.move(abuf, in_near)
    for copy in experts_in + rows_sent:
        links.arrived(copy)
    links.close()


def front(cfg, x, w_query, w_key, w_value, w_out, gains, router, routes, cot, gate_pieces, up_pieces, down_pieces, cosine, sine):
    nc, nz, tokens, width = cfg["nc"], cfg["nz"], cfg["tokens"], cfg["width"]
    cols, rows_w, length, cap = cfg["cols"], cfg["rows_w"], cfg["length"], cfg["cap"]
    rows, part = gate_pieces.shape[1:]
    rows_d = down_pieces.shape[1]
    shape = jax.ShapeDtypeStruct
    any_, vmem = pl.BlockSpec(memory_space=pl.ANY), pl.BlockSpec(memory_space=pltpu.VMEM)
    top_rows = routes.shape[0]
    outs = [
        shape((length, width), low),
        shape((3, nc, nz, rows_w, cols), low),
        shape((length, 3 * cols), exact),
        shape((8, length), exact),
        shape((3, length, cols), low),
        shape((length, cols), low),
        shape((nc, nz, rows_w, width), low),
        shape((tokens, width), exact),
        shape((nc, nz, rows_w, 128), low),
        shape((8, width), exact),
        shape((nc, nz, top_rows, tokens), jnp.int32),
        shape((nz, rows, part), low),
        shape((nz, rows, part), low),
        shape((nz, rows_d, width), low),
        shape((nz, nc, cap, width), low),
        shape((nz, tokens, width), low),
        shape((nz, nc, cap, width), low),
        shape((nz, tokens, width), low),
    ]
    scratch = [
        pltpu.VMEM((length, width), low),
        pltpu.VMEM((3, nc, nz, rows_w, cols), low),
        pltpu.VMEM((nc, nz, rows_w, width), low),
        pltpu.VMEM((nc, nz, 8, 128), exact),
        pltpu.VMEM((8, width), exact),
        pltpu.VMEM((nc, nz, rows_w, 128), low),
        pltpu.VMEM((nc, nz, top_rows, tokens), jnp.int32),
        pltpu.VMEM((length, 3 * cols), exact),
        pltpu.VMEM((nc, 8, length), exact),
        pltpu.VMEM((8, length), exact),
        pltpu.VMEM((length, 128), exact),
        pltpu.VMEM((length, 128), exact),
        pltpu.VMEM((3, length, cols), low),
        pltpu.VMEM((length, cols), low),
        pltpu.VMEM((length, cols), low),
        pltpu.VMEM((nc, tokens, cols), low),
        pltpu.VMEM((tokens, width), exact),
        pltpu.VMEM((tokens, width), low),
        pltpu.VMEM((nz, tokens, width), low),
        pltpu.VMEM((nz, tokens, width), low),
        pltpu.VMEM((nc * cap, tokens), low),
        pltpu.VMEM((2, nc * cap, width), low),
        pltpu.SemaphoreType.DMA((cfg["copies"],)),
        pltpu.SemaphoreType.DMA((cfg["copies"],)),
        pltpu.SemaphoreType.DMA((64,)),
    ]
    return pl.pallas_call(
        functools.partial(front_kernel, cfg),
        out_shape=outs,
        in_specs=[any_] * 12 + [vmem] * 2,
        out_specs=[any_] * len(outs),
        scratch_shapes=scratch,
        compiler_params=pltpu.CompilerParams(
            collective_id=0, has_side_effects=True, vmem_limit_bytes=cfg["vmem"]
        ),
        name="front",
    )(x, w_query, w_key, w_value, w_out, gains, router, routes, cot, gate_pieces, up_pieces, down_pieces, cosine, sine)


def expert_kernel(
    cfg,
    rows_ref, cotr_ref, rt_ref, tb_ref, wg_ref, wu_ref, wd_ref, near_ref, cotn_ref, r1_ref, gain_ref,
    hidden_out, dr1_out, datt_out, dlog_out, fgain_out, gd_land, gg_land, gu_out,
    back, in_back, out_land, in_land, ebh, rbh,
    wg, wu, wd, rows, cotb, gin, dg, du, eb, rb, tile, ranks, hot, metab, dgs, dgl,
    sends, recvs, locals_,
):
    nc, nz, tokens, width = cfg["nc"], cfg["nz"], cfg["tokens"], cfg["width"]
    cap, part, split, exp_local = cfg["cap"], cfg["part"], cfg["split"], cfg["exp_local"]
    ch = nc * cap
    total = nz * ch
    c, z = lax.axis_index("ctx"), lax.axis_index("fsdp")
    links = Links(sends, recvs, locals_)
    ds = pl.ds
    expert = c * exp_local + z // split
    best = lax.Precision.HIGHEST
    peers = list(range(1, nc))

    loads = [links.move(wg_ref, wg), links.move(wu_ref, wu), links.move(wd_ref, wd)]
    loads.append(links.move(rows_ref, rows))
    cot_base = links.local_count
    links.local_count += nz
    send_base = links.count
    links.count += 2 * nz * (nc - 1)
    keep_base = links.local_count
    links.local_count += 2 * nz
    off_base = links.local_count
    links.local_count += 2 * nz

    def cot_load(s, slot):
        return pltpu.make_async_copy(
            cotr_ref.at[ds(s * ch, ch)], cotb.at[slot], locals_.at[cot_base + s]
        )

    def chunk_copies(s, which):
        buf, landing = ((ebh, back), (rbh, in_back))[which]
        base = send_base + which * nz * (nc - 1) + s * (nc - 1)
        out = []
        for d in peers:
            out.append(
                pltpu.make_async_remote_copy(
                    src_ref=buf.at[s, ds((c ^ d) * cap, cap)],
                    dst_ref=landing.at[s, c],
                    send_sem=sends.at[base + d - 1],
                    recv_sem=recvs.at[base + d - 1],
                    device_id={"ctx": c ^ d},
                    device_id_type=pl.DeviceIdType.MESH,
                )
            )
        return out

    def keep_copy(s, which):
        landing = (back, in_back)[which]
        return pltpu.make_async_copy(
            (ebh, rbh)[which].at[s, ds(c * cap, cap)],
            landing.at[s, c],
            locals_.at[keep_base + which * nz + s],
        )

    def off_copy(s, which):
        return pltpu.make_async_copy(
            (eb, rb)[which], (ebh, rbh)[which].at[s], locals_.at[off_base + which * nz + s]
        )

    cot_load(nz - 1, 0).start()
    greet(c, z, nc, nz)
    for copy in loads:
        links.left(copy)

    expert_rows = lax.broadcasted_iota(jnp.int32, (128, tokens), 0)
    upper = jnp.where(
        lax.broadcasted_iota(jnp.int32, (tokens, tokens), 0)
        <= lax.broadcasted_iota(jnp.int32, (tokens, tokens), 1),
        1.0,
        0.0,
    ).astype(low)

    def routed(block):
        chosen = jnp.zeros((128, tokens), exact)
        for k in range(cfg["top"]):
            chosen = jnp.where(block[k : k + 1, :] == expert_rows, 1.0, chosen)
        return chosen

    sub = min(256, ch)
    lane = lax.broadcasted_iota(jnp.int32, (sub, 128), 1)

    def work(i, _):
        s = nz - 1 - i
        slot = lax.rem(i, 2)

        @pl.when(i + 1 < nz)
        def _():
            cot_load(s - 1, 1 - slot).start()

        for k in range(nc):
            block = tb_ref[k, z ^ s]
            found = jnp.where(block == expert, 1.0, 0.0)
            ranks[k : k + 1, :] = jnp.max(found, axis=0, keepdims=True)
        ranks[...] = slots_of(cfg, ranks[...], upper)
        fill_hot(cfg, ranks[...], hot)
        for k in range(nc):
            chosen = routed(tb_ref[k, z ^ s]).astype(low)
            metab[k * cap : (k + 1) * cap, :] = kdot(
                hot[k * cap : (k + 1) * cap, :], chosen, ((1,), (1,))
            )
        cot_load(s, slot).wait()

        def some_rows(j, _):
            here = pl.multiple_of(j * sub, sub)
            at = pl.multiple_of(s * ch + j * sub, sub)
            span, to = ds(here, sub), ds(at, sub)
            block = rows[to, :]
            logits = kdot(block, rt_ref[...], ((1,), (1,)))
            logits = jnp.where(metab[span, :] > 0.5, logits, neg_large)
            weight = jnp.exp(logits - jnp.max(logits, axis=-1, keepdims=True))
            gate = jnp.sum(jnp.where(lane == expert, weight, 0.0), axis=-1, keepdims=True)
            gate = gate / jnp.sum(weight, axis=-1, keepdims=True)
            g = kdot(block, wg[...])
            u = kdot(block, wu[...])
            sg = 1.0 / (1.0 + jnp.exp(-g))
            act = g * sg
            inner = (act * u).astype(low)
            gin[to, :] = (inner.astype(exact) * gate).astype(low)
            eb[span, :] = kdot(inner, wd[...]).astype(low)
            dinner = kdot(cotb[slot, span, :], wd[...], ((1,), (1,))) * gate
            dg_low = (dinner * u * sg * (1.0 + g * (1.0 - sg))).astype(low)
            du_low = (dinner * act).astype(low)
            dg[to, :] = dg_low
            du[to, :] = du_low
            rb[span, :] = (
                kdot(dg_low, wg[...], ((1,), (1,))) + kdot(du_low, wu[...], ((1,), (1,)))
            ).astype(low)
            return 0

        lax.fori_loop(0, ch // sub, some_rows, 0)
        for which in (0, 1):
            off_copy(s, which).start()
        for which in (0, 1):
            off_copy(s, which).wait()
            for copy in chunk_copies(s, which):
                copy.start()
            keep_copy(s, which).start()
        return 0

    lax.fori_loop(0, nz, work, 0)

    rows_d = part // nz
    step = 256 if nz * ch <= 2048 else 128
    tile_base = links.local_count
    links.local_count += width // step

    def tile_load(k):
        return pltpu.make_async_copy(
            cotr_ref.at[:, ds(k * step, step)], tile.at[lax.rem(k, 2)], locals_.at[tile_base + k]
        )

    tile_load(0).start()

    def down_tile(k, _):
        @pl.when(k + 1 < width // step)
        def _():
            tile_load(k + 1).start()

        tile_load(k).wait()
        at = pl.multiple_of(k * step, step)
        wd[:, ds(at, step)] = kdot(gin[...], tile[lax.rem(k, 2)], ((0,), (0,))).astype(low)
        return 0

    lax.fori_loop(0, width // step, down_tile, 0)
    grads_out = []
    for s in range(1, nz):
        src = wd.at[ds(pl.multiple_of((z ^ s) * rows_d, rows_d), rows_d)]
        grads_out.append(links.send(src, gd_land.at[z], fsdp=z ^ s))
    links.move(wd.at[ds(pl.multiple_of(z * rows_d, rows_d), rows_d)], gd_land.at[z])
    rows_g = width // nz

    def rows_tile(left, dst):
        def one(k, _):
            at = pl.multiple_of(k * step, step)
            dst[ds(at, step), :] = kdot(rows[:, ds(at, step)], left[...], ((0,), (0,))).astype(low)
            return 0

        lax.fori_loop(0, width // step, one, 0)

    rows_tile(dg, wg)
    for s in range(1, nz):
        src = wg.at[ds(pl.multiple_of((z ^ s) * rows_g, rows_g), rows_g)]
        grads_out.append(links.send(src, gg_land.at[z], fsdp=z ^ s))
    links.move(wg.at[ds(pl.multiple_of(z * rows_g, rows_g), rows_g)], gg_land.at[z])
    rows_tile(du, wu)
    links.move(wu, gu_out)

    spare = {}
    at = 0
    for name, count in (
        ("back", ch), ("in_back", ch), ("near", tokens), ("cot", tokens), ("out0", tokens),
        ("in0", tokens),
    ):
        spare[name] = rows.at[at : at + count]
        at += count
    stage = {0: (spare["out0"], spare["in0"]), 1: (cotb.at[0, 0:tokens], cotb.at[1, 0:tokens])}
    extra = (cotb.at[0, tokens : 2 * tokens], cotb.at[1, tokens : 2 * tokens])
    pick_rows = lax.broadcasted_iota(jnp.int32, (nc, 128), 0)
    pick_lane = lax.broadcasted_iota(jnp.int32, (nc, 128), 1)
    homeward = {}
    gate_home = {}
    busy = {0: [], 1: []}
    gates_own = None
    sums = None
    for s in range(nz - 1, -1, -1):
        for which in (0, 1):
            out = chunk_copies(s, which)
            for copy in out:
                copy.wait_recv()
            keep_copy(s, which).wait()
        fetch = []
        for k in range(nc):
            fetch.append(links.move(back.at[s, k], rows.at[k * cap : (k + 1) * cap]))
            fetch.append(links.move(in_back.at[s, k], rows.at[ch + k * cap : ch + (k + 1) * cap]))
        fetch.append(links.move(near_ref.at[s], spare["near"]))
        fetch.append(links.move(cotn_ref.at[s], spare["cot"]))
        block = tb_ref[c, z ^ s]
        fill_hot(cfg, plane_ranks(cfg, block, z), hot)
        chosen = routed(block)
        for copy in fetch:
            links.left(copy)
        logits = kdot(rt_ref[...], spare["near"][...], ((1,), (1,)))
        logits = jnp.where(chosen > 0.5, logits, neg_large)
        weight = jnp.exp(logits - jnp.max(logits, axis=0, keepdims=True))
        gates = weight / jnp.sum(weight, axis=0, keepdims=True)
        sel = jnp.where(pick_lane == pick_rows * exp_local + z // split, 1.0, 0.0)
        plane = kdot(sel, gates, ((1,), (0,)), best)
        slot_grad = kdot(spare["back"][...], spare["cot"][...], ((1,), (1,)))
        for k in range(nc):
            span = slice(k * cap, (k + 1) * cap)
            hit = hot[span, :].astype(exact)
            dgs[s, k : k + 1, :] = jnp.sum(hit * slot_grad[span, :], axis=0, keepdims=True)
        in_part = kdot(hot[...], spare["in_back"][...], ((0,), (0,)))
        for k in range(nc):
            span = slice(k * cap, (k + 1) * cap)
            hot[span, :] = (hot[span, :].astype(exact) * plane[k : k + 1, :]).astype(low)
        out_part = kdot(hot[...], spare["back"][...], ((0,), (0,)))
        lowest = s & -s
        bit = 1
        while bit < nz and (s == 0 or bit < lowest):
            for copy in homeward[s | bit]:
                links.arrived(copy)
            got = [links.move(out_land.at[s | bit], extra[0]), links.move(in_land.at[s | bit], extra[1])]
            for copy in got:
                links.left(copy)
            out_part += extra[0][...].astype(exact)
            in_part += extra[1][...].astype(exact)
            bit *= 2
        if s:
            slot = s % 2
            for copy in busy[slot]:
                links.left(copy)
            stage[slot][0][...] = out_part.astype(low)
            stage[slot][1][...] = in_part.astype(low)
            homeward[s] = [
                links.send(stage[slot][0], out_land.at[s], fsdp=z ^ lowest),
                links.send(stage[slot][1], in_land.at[s], fsdp=z ^ lowest),
            ]
            busy[slot] = homeward[s]
            gate_home[s] = links.send(dgs.at[s], dgl.at[s], fsdp=z ^ s)
        else:
            gates_own = gates
            sums = (out_part, in_part)

    dgate = jnp.zeros((128, tokens), exact)
    for s in range(nz):
        if s:
            links.arrived(gate_home[s])
        here = dgl[s] if s else dgs[0]
        sel = jnp.where(pick_lane == pick_rows * exp_local + (z ^ s) // split, 1.0, 0.0)
        dgate += kdot(sel, here, ((0,), (0,)), best)
    dchosen = gates_own * (dgate - jnp.sum(gates_own * dgate, axis=0, keepdims=True))
    dlog = dchosen.astype(low)
    hot[0:128, :] = dlog
    dlog_copy = links.move(hot.at[0:128], dlog_out)
    out_part, in_part = sums
    da2 = in_part + kdot(dlog, rt_ref[...], ((0,), (0,)))
    r1 = r1_ref[...]
    for copies in busy.values():
        for copy in copies:
            links.left(copy)
    stage[0][0][...] = (r1 + out_part).astype(low)
    links.move(stage[0][0], hidden_out)
    rs = lax.rsqrt(jnp.mean(r1 * r1, axis=-1, keepdims=True) + epsilon)
    n2 = r1 * rs
    dm = da2 * gain_ref[3:4, :]
    fgain_out[...] = jnp.broadcast_to(jnp.sum(da2 * n2, axis=0, keepdims=True), (8, width))
    inner_mean = jnp.mean(dm * n2, axis=-1, keepdims=True)
    dr1 = spare["cot"][...].astype(exact) + rs * (dm - n2 * inner_mean)
    dr1_out[...] = dr1
    datt_out[...] = dr1.astype(low)
    for s in range(nz):
        for which in (0, 1):
            out = chunk_copies(s, which)
            for copy in out:
                copy.wait_send()
    for copy in grads_out:
        links.arrived(copy)
    links.close()


def run_experts(cfg, rows, cot_rows, router_t, routes, wg, wu, wd, near, cot_near, r1, gains):
    nc, nz, tokens, width = cfg["nc"], cfg["nz"], cfg["tokens"], cfg["width"]
    cap, part = cfg["cap"], cfg["part"]
    ch = nc * cap
    shape = jax.ShapeDtypeStruct
    any_, vmem = pl.BlockSpec(memory_space=pl.ANY), pl.BlockSpec(memory_space=pltpu.VMEM)
    outs = [
        (shape((tokens, width), low), any_),
        (shape((tokens, width), exact), vmem),
        (shape((tokens, width), low), vmem),
        (shape((128, tokens), low), any_),
        (shape((8, width), exact), vmem),
        (shape((nz, part // nz, width), low), any_),
        (shape((nz, width // nz, part), low), any_),
        (shape((width, part), low), any_),
        (shape((nz, nc, cap, width), low), any_),
        (shape((nz, nc, cap, width), low), any_),
        (shape((nz, tokens, width), low), any_),
        (shape((nz, tokens, width), low), any_),
        (shape((nz, ch, width), low), any_),
        (shape((nz, ch, width), low), any_),
    ]
    step = 256 if nz * ch <= 2048 else 128
    scratch = [
        pltpu.VMEM((width, part), low),
        pltpu.VMEM((width, part), low),
        pltpu.VMEM((part, width), low),
        pltpu.VMEM((nz * ch, width), low),
        pltpu.VMEM((2, ch, width), low),
        pltpu.VMEM((nz * ch, part), low),
        pltpu.VMEM((nz * ch, part), low),
        pltpu.VMEM((nz * ch, part), low),
        pltpu.VMEM((ch, width), low),
        pltpu.VMEM((ch, width), low),
        pltpu.VMEM((2, nz * ch, step), low),
        pltpu.VMEM((nc, tokens), exact),
        pltpu.VMEM((ch, tokens), low),
        pltpu.VMEM((ch, 128), exact),
        pltpu.VMEM((nz, nc, tokens), exact),
        pltpu.VMEM((nz, nc, tokens), exact),
        pltpu.SemaphoreType.DMA((2 * nz * nc + 8 * nz,)),
        pltpu.SemaphoreType.DMA((2 * nz * nc + 8 * nz,)),
        pltpu.SemaphoreType.DMA((2 * nz * nc + 16 * nz + width // step + 16,)),
    ]
    return pl.pallas_call(
        functools.partial(expert_kernel, cfg),
        out_shape=[o[0] for o in outs],
        in_specs=[any_, any_, vmem, vmem, any_, any_, any_, any_, any_, vmem, vmem],
        out_specs=[o[1] for o in outs],
        scratch_shapes=scratch,
        compiler_params=pltpu.CompilerParams(
            collective_id=1, has_side_effects=True, vmem_limit_bytes=cfg["vmem"]
        ),
        name="experts",
    )(rows, cot_rows, router_t, routes, wg, wu, wd, near, cot_near, r1, gains)


def back_kernel(
    cfg,
    x_ref, dr1_ref, datt_ref, a1_ref, w_ref, raw_ref, stat_ref, rot_ref, ob_ref, wo_ref, gain_ref, fgain_ref,
    gu_ref, cos_ref, sin_ref,
    hidden_out, w_out, wo_out, gains_out, gu_land, pair_land, chip_land, wz_land, oz_land,
    wo, datt, a1, w, raw, rot, ob, dland, aq, ak, av, rq, rk, cq, ck, stat, total, dqkv, gw, go, gsum,
    wtemp, otemp, wsum, wl, xrow, xtemp, small_z, small_c,
    sends, recvs, locals_,
):
    nc, nz, tokens, width = cfg["nc"], cfg["nz"], cfg["tokens"], cfg["width"]
    cols, rows_w, length = cfg["cols"], cfg["rows_w"], cfg["length"]
    hs = 128
    heads = cols // hs
    half = tokens // 2
    block = cfg["block"]
    blocks = length // block
    c, z = lax.axis_index("ctx"), lax.axis_index("fsdp")
    links = Links(sends, recvs, locals_)
    ds = pl.ds
    best = lax.Precision.HIGHEST
    same = [d for d in range(2, nc, 2)]
    own_rows = ds(pl.multiple_of(c * tokens, tokens), tokens)

    wo_in = links.move(wo_ref, wo)
    datt_in = links.move(datt_ref, datt.at[own_rows])
    first = [links.move(rot_ref, rot), links.move(raw_ref.at[:, 0 : 2 * cols], raw), links.move(ob_ref, ob)]
    later = [links.move(w_ref, w), links.move(x_ref, xrow)]
    up_own = links.move(gu_ref.at[z], gu_land.at[z])
    greet(c, z, nc, nz)
    up_sends = [links.send(gu_ref.at[z ^ s], gu_land.at[z], fsdp=z ^ s) for s in range(1, nz)]
    links.left(datt_in)
    links.left(wo_in)

    heads_sent = []
    for d in range(1, nc):
        at = pl.multiple_of((c ^ d) * cols, cols)
        spot = dqkv.at[d * tokens : (d + 1) * tokens, 0:cols]
        spot[...] = kdot(datt[own_rows, :], wo[ds(at, cols), :], ((1,), (1,))).astype(low)
        heads_sent.append(links.send(spot, dland.at[c], ctx=c ^ d))
    at = pl.multiple_of(c * cols, cols)
    dland[c] = kdot(datt[own_rows, :], wo[ds(at, cols), :], ((1,), (1,))).astype(low)
    rows_same = {d: links.send(datt.at[own_rows], datt.at[own_rows], ctx=c ^ d) for d in same}
    rows_side = [links.send(datt.at[own_rows], datt.at[own_rows], ctx=c ^ 1)]
    for copy in first:
        links.left(copy)

    row8 = lax.broadcasted_iota(jnp.int32, (8, hs), 0)

    def columns(src, one, two, finish):
        def step(i, _):
            at = pl.multiple_of(i * block, block)
            part = src[:, ds(at, block)]
            for row, dst in ((0, one), (1, two)):
                sel = jnp.where(row8 == row, 1.0, 0.0)
                dst[ds(at, block), :] = finish(kdot(part, sel, ((0,), (0,)), best) / width)
            return 0

        lax.fori_loop(0, blocks, step, 0)

    columns(stat_ref, rq, rk, lambda v: lax.rsqrt(v + epsilon))
    ak[...] = jnp.zeros_like(ak)
    av[...] = jnp.zeros_like(av)
    gsum[...] = jnp.zeros_like(gsum)
    for copy in heads_sent:
        links.arrived(copy)
    for copy in heads_sent:
        links.left(copy)

    def place(i, _):
        d, side = i // 2, i % 2
        at = pl.multiple_of(side * half, half)
        to = pl.multiple_of(jnp.where(side == 0, d, 2 * nc - 1 - d) * half, half)
        aq[ds(to, half), :] = dland[d, ds(at, half), :].astype(exact)
        return 0

    lax.fori_loop(0, 2 * nc, place, 0)
    for d in same:
        links.arrived(rows_same[d])
        there = datt.at[ds(pl.multiple_of((c ^ d) * tokens, tokens), tokens)]
        rows_side.append(links.send(there, there, ctx=c ^ 1))

    scale = hs ** -0.5
    for h in range(heads):
        lanes = slice(h * hs, (h + 1) * hs)
        for i in range(blocks):
            count = (i + 1) * block
            here = slice(i * block, count)
            q, k, v = rot[0, here, lanes], rot[1, :count, lanes], rot[2, :count, lanes]
            do = aq[here, lanes].astype(low)
            s = kdot(q, k, ((1,), (1,))) * scale
            row = lax.broadcasted_iota(jnp.int32, (block, count), 0) + i * block
            col = lax.broadcasted_iota(jnp.int32, (block, count), 1)
            s = jnp.where(col <= row, s, neg_large)
            p = jnp.exp(s - jnp.max(s, axis=-1, keepdims=True))
            p = p * (1.0 / jnp.sum(p, axis=-1, keepdims=True))
            dp = kdot(do, v, ((1,), (1,)))
            delta = jnp.sum(p * dp, axis=-1, keepdims=True)
            dscore = (p * (dp - delta)).astype(low)
            av[:count, lanes] += kdot(p.astype(low), do, ((0,), (0,)))
            ak[:count, lanes] += kdot(dscore, q, ((0,), (0,))) * scale
            aq[here, lanes] = kdot(dscore, k) * scale

    def unturn(i, _):
        d, side = i // 2, i % 2
        at = pl.multiple_of(d * tokens + side * half, half)
        to = pl.multiple_of(jnp.where(side == 0, d, 2 * nc - 1 - d) * half, half)
        cosine, sine = cos_ref[ds(at, half), :], sin_ref[ds(at, half), :]
        for j, acc, scale_ref, sums in ((0, aq, rq, cq), (1, ak, rk, ck)):
            row_sum = jnp.zeros((half, 1), exact)
            for h in range(heads):
                lanes = slice(h * hs, (h + 1) * hs)
                lane = j * cols + h * hs
                v = acc[ds(to, half), lanes]
                v = v * cosine - pltpu.roll(v, hs // 2, 1) * sine
                acc[ds(to, half), lanes] = v
                normed = raw[ds(at, half), lane : lane + hs] * scale_ref[ds(at, half), :]
                v = v * normed
                gsum[j : j + 1, lanes] += jnp.sum(v, axis=0, keepdims=True)
                gain = gain_ref[1 + j : 2 + j, ds(pl.multiple_of(c * cols + h * hs, hs), hs)]
                row_sum += jnp.sum(v * gain, axis=-1, keepdims=True)
            sums[ds(at, half), :] = jnp.broadcast_to(row_sum, (half, hs))
        return 0

    lax.fori_loop(0, 2 * nc, unturn, 0)
    lane8 = lax.broadcasted_iota(jnp.int32, (8, hs), 1)

    def gather_sums(i, _):
        at = pl.multiple_of(i * block, block)
        part = jnp.zeros((8, block), exact)
        for row, src in ((0, cq), (1, ck)):
            sel = jnp.where((row8 == row) & (lane8 == 0), 1.0, 0.0)
            part += kdot(sel, src[ds(at, block), :], ((1,), (1,)), best)
        stat[c, :, ds(at, block)] = part
        return 0

    lax.fori_loop(0, blocks, gather_sums, 0)
    stats = [links.send(stat.at[c], stat.at[c], ctx=c ^ d) for d in range(1, nc)]

    for copy in rows_side:
        links.arrived(copy)
    tile = width // nc
    tile_base = links.local_count
    links.local_count += nc

    def tile_load(k):
        return pltpu.make_async_copy(
            a1_ref.at[:, ds(k * tile, tile)], a1.at[lax.rem(k, 2)], locals_.at[tile_base + k]
        )

    tile_load(0).start()

    def out_tile(k, _):
        at = pl.multiple_of(k * tile, tile)
        v = kdot(ob[...], datt[:, ds(at, tile)], ((0,), (0,))).astype(low)
        go[:, :, ds(at, tile)] = v.reshape(nz, rows_w, tile)
        return 0

    lax.fori_loop(0, nc, out_tile, 0)
    for copy in stats:
        links.arrived(copy)
    summed = stat[0]
    for k in range(1, nc):
        summed += stat[k]
    total[...] = summed
    columns(total, cq, ck, lambda v: v)

    def finish(i, _):
        d, side = i // 2, i % 2
        at = pl.multiple_of(d * tokens + side * half, half)
        to = pl.multiple_of(jnp.where(side == 0, d, 2 * nc - 1 - d) * half, half)
        for j, acc, scale_ref, sums in ((0, aq, rq, cq), (1, ak, rk, ck)):
            for h in range(heads):
                lanes = slice(h * hs, (h + 1) * hs)
                lane = j * cols + h * hs
                gain = gain_ref[1 + j : 2 + j, ds(pl.multiple_of(c * cols + h * hs, hs), hs)]
                normed = raw[ds(at, half), lane : lane + hs] * scale_ref[ds(at, half), :]
                v = acc[ds(to, half), lanes] * gain - normed * sums[ds(at, half), :]
                dqkv[ds(at, half), lane : lane + hs] = (v * scale_ref[ds(at, half), :]).astype(low)
        dqkv[ds(at, half), 2 * cols : 3 * cols] = av[ds(to, half), :].astype(low)
        return 0

    lax.fori_loop(0, 2 * nc, finish, 0)
    for copy in later:
        links.left(copy)
    for copy in list(rows_same.values()) + rows_side:
        links.left(copy)

    def w_tile(k, _):
        @pl.when(k + 1 < nc)
        def _():
            tile_load(k + 1).start()

        tile_load(k).wait()
        v = kdot(a1[lax.rem(k, 2)], dqkv[...], ((0,), (0,))).astype(low)
        for j in range(3):
            gw[j, k] = v[:, j * cols : (j + 1) * cols].reshape(nz, rows_w, cols)
        return 0

    lax.fori_loop(0, nc, w_tile, 0)
    home = {}

    def send_home(s):
        peer = z ^ (s & -s)
        home[s] = (
            links.send(gw.at[:, :, z ^ s], wz_land.at[s], fsdp=peer),
            links.send(go.at[z ^ s], oz_land.at[s], fsdp=peer),
        )

    def taken(s):
        w_sum = gw[:, :, z ^ s].astype(exact)
        o_sum = go[z ^ s].astype(exact)
        bit = 1
        while bit < nz and (s == 0 or bit < (s & -s)):
            for copy in home[s | bit]:
                links.arrived(copy)
            got = [links.move(wz_land.at[s | bit], wtemp), links.move(oz_land.at[s | bit], otemp)]
            for copy in got:
                links.left(copy)
            w_sum += wtemp[...].astype(exact)
            o_sum += otemp[...].astype(exact)
            bit *= 2
        return w_sum, o_sum

    for s in range(nz - 1, 0, -1):
        if s & 1:
            send_home(s)

    def partial(k):
        at = pl.multiple_of(k * tokens, tokens)
        v = jnp.zeros((tokens, width), exact)
        for j in range(3):
            v += kdot(dqkv[ds(at, tokens), j * cols : (j + 1) * cols], w[j], ((1,), (1,)))
        datt[ds(at, tokens), :] = v.astype(low)

    def rows_of(k):
        return datt.at[ds(pl.multiple_of(k * tokens, tokens), tokens)]

    evens = [0] + same
    pair, chip = {}, {}

    def other_core(m, _):
        partial(2 * m + 1 - lax.rem(c, 2))
        return 0

    def this_core(m, _):
        partial(2 * m + lax.rem(c, 2))
        return 0

    lax.fori_loop(0, nc // 2, other_core, 0)
    for m, d in enumerate(evens):
        pair[d] = links.send(rows_of((c ^ 1) ^ d), pair_land.at[m], ctx=c ^ 1)
    lax.fori_loop(0, nc // 2, this_core, 0)
    for m, d in list(enumerate(evens))[::-1]:
        links.arrived(pair[d])
        got = links.move(pair_land.at[m], xtemp)
        links.left(got)
        mine = rows_of(c ^ d)
        if d:
            mine[...] = (mine[...].astype(exact) + xtemp[...].astype(exact)).astype(low)
            chip[d] = links.send(mine, chip_land.at[m], ctx=c ^ d)
        else:
            grad_in = mine[...].astype(exact) + xtemp[...].astype(exact)
            hidden_out[...] = grad_in

    for s in range(nz - 2, 0, -1):
        if not s & 1:
            w_sum, o_sum = taken(s)
            gw[:, :, z ^ s] = w_sum.astype(low)
            go[z ^ s] = o_sum.astype(low)
            send_home(s)

    for m, d in enumerate(evens):
        if d:
            links.arrived(chip[d])
            got = links.move(chip_land.at[m], xtemp)
            links.left(got)
            hidden_out[...] += xtemp[...].astype(exact)
    x = xrow[...].astype(exact)
    rs = lax.rsqrt(jnp.mean(x * x, axis=-1, keepdims=True) + epsilon)
    n1 = x * rs
    grad_in = hidden_out[...]
    gains_out[...] = jnp.zeros_like(gains_out)
    gains_out[0:1, :] = jnp.sum(grad_in * n1, axis=0, keepdims=True)
    for j in range(2):
        own_lanes = ds(pl.multiple_of(c * cols, cols), cols)
        gains_out[1 + j : 2 + j, own_lanes] = gsum[j : j + 1, :]
    gains_out[3:4, :] = fgain_ref[0:1, :]
    dn = grad_in * gain_ref[0:1, :]
    hidden_out[...] = dr1_ref[...] + rs * (dn - n1 * jnp.mean(dn * n1, axis=-1, keepdims=True))

    small_z[0] = gains_out[...]
    z_sums = [links.send(small_z.at[0], small_z.at[s], fsdp=z ^ s) for s in range(1, nz)]
    for copy in z_sums:
        links.arrived(copy)
    v = small_z[0]
    for s in range(1, nz):
        v += small_z[s]
    small_c[0] = v
    c_sums = [links.send(small_c.at[0], small_c.at[d], ctx=c ^ d) for d in range(1, nc)]
    for copy in c_sums:
        links.arrived(copy)
    v = small_c[0]
    for d in range(1, nc):
        v += small_c[d]
    gains_out[...] = v

    w_sum, o_sum = taken(0)
    wo_out[...] = o_sum
    wsum[...] = w_sum.astype(low)
    w_home = [links.send(wsum.at[:, c ^ d], wl.at[:, c], ctx=c ^ d) for d in range(1, nc)]
    w_own = links.move(wsum.at[:, c], wl.at[:, c])
    for copy in w_home:
        links.arrived(copy)
    links.left(w_own)
    for j in range(3):
        for k in range(nc):
            w_out[j, :, k * cols : (k + 1) * cols] = wl[j, k].astype(exact)
    for copy in up_sends:
        links.arrived(copy)
    links.close()


def run_back(cfg, x, dr1, datt, a1, w, raw, stat, rot, ob, wo, gains, fgain, gu, cosine, sine):
    nc, nz, tokens, width = cfg["nc"], cfg["nz"], cfg["tokens"], cfg["width"]
    cols, rows_w, length = cfg["cols"], cfg["rows_w"], cfg["length"]
    shape = jax.ShapeDtypeStruct
    any_, vmem = pl.BlockSpec(memory_space=pl.ANY), pl.BlockSpec(memory_space=pltpu.VMEM)
    outs = [
        (shape((tokens, width), exact), vmem),
        (shape((3, rows_w, width), exact), vmem),
        (shape((rows_w, width), exact), vmem),
        (shape((8, width), exact), vmem),
        (shape(gu.shape, low), any_),
        (shape((nc // 2, tokens, width), low), any_),
        (shape((nc // 2, tokens, width), low), any_),
        (shape((nz, 3, nc, rows_w, cols), low), any_),
        (shape((nz, rows_w, width), low), any_),
    ]
    scratch = [
        pltpu.VMEM((width, width), low),
        pltpu.VMEM((length, width), low),
        pltpu.VMEM((2, length, width // nc), low),
        pltpu.VMEM((3, width, cols), low),
        pltpu.VMEM((length, 2 * cols), exact),
        pltpu.VMEM((3, length, cols), low),
        pltpu.VMEM((length, cols), low),
        pltpu.VMEM((nc, tokens, cols), low),
        pltpu.VMEM((length, cols), exact),
        pltpu.VMEM((length, cols), exact),
        pltpu.VMEM((length, cols), exact),
        pltpu.VMEM((length, 128), exact),
        pltpu.VMEM((length, 128), exact),
        pltpu.VMEM((length, 128), exact),
        pltpu.VMEM((length, 128), exact),
        pltpu.VMEM((nc, 8, length), exact),
        pltpu.VMEM((8, length), exact),
        pltpu.VMEM((length, 3 * cols), low),
        pltpu.VMEM((3, nc, nz, rows_w, cols), low),
        pltpu.VMEM((nz, rows_w, width), low),
        pltpu.VMEM((8, cols), exact),
        pltpu.VMEM((3, nc, rows_w, cols), low),
        pltpu.VMEM((rows_w, width), low),
        pltpu.VMEM((3, nc, rows_w, cols), low),
        pltpu.VMEM((3, nc, rows_w, cols), low),
        pltpu.VMEM((tokens, width), low),
        pltpu.VMEM((tokens, width), low),
        pltpu.VMEM((nz, 8, width), exact),
        pltpu.VMEM((nc, 8, width), exact),
        pltpu.SemaphoreType.DMA((8 * nc + 8 * nz,)),
        pltpu.SemaphoreType.DMA((8 * nc + 8 * nz,)),
        pltpu.SemaphoreType.DMA((4 * nc + 8 * nz + 16,)),
    ]
    return pl.pallas_call(
        functools.partial(back_kernel, cfg),
        out_shape=[o[0] for o in outs],
        in_specs=[any_, vmem, any_, any_, any_, any_, vmem, any_, any_, any_, vmem, vmem, any_, vmem, vmem],
        out_specs=[o[1] for o in outs],
        scratch_shapes=scratch,
        compiler_params=pltpu.CompilerParams(
            collective_id=2, has_side_effects=True, vmem_limit_bytes=cfg["vmem"]
        ),
        name="back",
    )(x, dr1, datt, a1, w, raw, stat, rot, ob, wo, gains, fgain, gu, cosine, sine)


def tables(nc, tokens, head_size):
    half = tokens // 2
    local = np.arange(tokens)
    device = np.arange(nc)[:, None]
    position = np.where(
        local < half, device * half + local, (2 * nc - 1 - device) * half + local - half
    ).reshape(-1)
    freq = np.float32(10000.0) ** (-np.arange(head_size // 2, dtype=np.float32) * (2.0 / head_size))
    angle = position.astype(np.float32)[:, None] * freq.astype(np.float32)
    cosine = np.concatenate([np.cos(angle), np.cos(angle)], axis=1)
    sine = np.concatenate([-np.sin(angle), np.sin(angle)], axis=1)
    return jnp.asarray(cosine, exact), jnp.asarray(sine, exact)


def body(
    hidden_in,
    cotangent,
    routes,
    attn_gain,
    query_gain,
    key_gain,
    ffn_gain,
    w_query,
    w_key,
    w_value,
    w_out,
    w_router,
    w_gate,
    w_up,
    w_down,
):
    tokens = hidden_in.shape[1]
    width = hidden_in.shape[2]
    head_size = width // HEADS
    ctx_count = lax.axis_size("ctx")
    z_count = lax.axis_size("fsdp")
    both = ("ctx", "fsdp")
    top = routes.shape[2]
    exp_local = w_gate.shape[0]
    split = z_count // exp_local
    hidden = w_gate.shape[2]
    part = hidden // split
    experts = exp_local * ctx_count
    capacity = tokens * top * 4 // (3 * experts)
    cols = HEADS // ctx_count * head_size
    length = tokens * ctx_count
    c_index = lax.axis_index("ctx")
    z_index = lax.axis_index("fsdp")
    rows_w = w_query.shape[0]

    cfg = dict(
        nc=ctx_count,
        nz=z_count,
        tokens=tokens,
        width=width,
        cols=cols,
        rows_w=rows_w,
        length=length,
        cap=capacity,
        top=top,
        exp_local=exp_local,
        split=split,
        block=math.gcd(length, 256 if length <= 2048 else 128),
        chunk=math.gcd(length, 64),
        copies=(ctx_count - 1) * (8 + 2 * z_count) + (z_count - 1) * 12 + 2 * ctx_count + 8,
        part=part,
        vmem=62 * 2**20,
    )
    index = c_index * z_count + z_index
    per = 128 // rows_w
    gains = jnp.stack([attn_gain, query_gain, key_gain, ffn_gain]).astype(exact)
    gains = lax.dynamic_update_slice(
        jnp.zeros((8, 128), exact), gains, (0, jnp.mod(index, per) * rows_w)
    )
    router_tile = jnp.pad(w_router, ((0, 0), (0, 128 - experts)))
    route_tile = jnp.pad(routes[0].T, ((0, 8 - top), (0, 0)), constant_values=-1)

    def pieces_of(weight):
        rows = weight.shape[1]
        weight = weight.reshape(exp_local, rows, z_count, split, part // z_count)
        return weight.transpose(0, 3, 1, 2, 4).reshape(z_count, rows, part)

    cosine, sine = tables(ctx_count, tokens, head_size)
    (
        attn_all, w_full, raw, squares, rot, out_heads, wo_full, resid_one,
        router_full, gains, routes_all, gate_full, up_full, down_full, cot_rows, cot_near,
        input_rows, input_near,
    ) = front(
        cfg, hidden_in[0], w_query, w_key, w_value, w_out, gains, router_tile, route_tile,
        cotangent[0], pieces_of(w_gate), pieces_of(w_up),
        w_down.reshape(z_count, -1, width), cosine, sine,
    )
    gate_full = gate_full.reshape(-1, part)
    up_full = up_full.reshape(-1, part)
    down_full = down_full.reshape(-1, width)
    ffn_input = input_near[0]
    router_t = router_full.reshape(width, 128).T
    (
        resid_two, grad_one, attn_grad_low, logit_grad, ffn_gain_grad, down_land, gate_land,
        up_grad, *_,
    ) = run_experts(
        cfg, input_rows.reshape(-1, width), cot_rows.reshape(-1, width), router_t, routes_all,
        gate_full, up_full, down_full, input_near, cot_near, resid_one, gains,
    )
    out_hidden = resid_two[None]
    router_grad = lax.dot_general(
        ffn_input, logit_grad[:experts], (((0,), (1,)), ((), ())), preferred_element_type=exact
    )

    def whole_out(grad):
        grad = grad.reshape(exp_local, split, -1, z_count, part // z_count)
        return grad.transpose(0, 2, 3, 1, 4).reshape(exp_local, -1, hidden).astype(exact)

    grad_down = down_land.reshape(exp_local, -1, width).astype(exact)
    grad_gate = whole_out(gate_land)
    grad_hidden, w_grads, grad_out, gain_grads, up_land, *_ = run_back(
        cfg, hidden_in[0], grad_one, attn_grad_low, attn_all, w_full.reshape(3, width, cols), raw,
        squares, rot, out_heads, wo_full.reshape(width, width), gains, ffn_gain_grad,
        up_grad.reshape(z_count, -1, part), cosine, sine,
    )
    grad_up = whole_out(up_land)
    gain_grads = lax.dynamic_slice_in_dim(gain_grads, index * rows_w, rows_w, 1)
    sums = router_grad.reshape(ctx_count * z_count, rows_w * experts)
    sums = jnp.sum(exchange(sums, both), axis=0)
    return (
        out_hidden,
        grad_hidden[None],
        gain_grads[0],
        gain_grads[1],
        gain_grads[2],
        gain_grads[3],
        w_grads[0],
        w_grads[1],
        w_grads[2],
        grad_out,
        sums.reshape(rows_w, experts),
        grad_gate,
        grad_up,
        grad_down,
    )


def solution(mesh):
    in_specs = (
        P("fsdp", "ctx", None),
        P("fsdp", "ctx", None),
        P("fsdp", "ctx", None),
        P(("ctx", "fsdp")),
        P(("ctx", "fsdp")),
        P(("ctx", "fsdp")),
        P(("ctx", "fsdp")),
        P(("ctx", "fsdp"), None),
        P(("ctx", "fsdp"), None),
        P(("ctx", "fsdp"), None),
        P(("ctx", "fsdp"), None),
        P(("ctx", "fsdp"), None),
        P("ctx", "fsdp", None),
        P("ctx", "fsdp", None),
        P("ctx", "fsdp", None),
    )
    out_specs = (
        P("fsdp", "ctx", None),
        P("fsdp", "ctx", None),
        P(("ctx", "fsdp")),
        P(("ctx", "fsdp")),
        P(("ctx", "fsdp")),
        P(("ctx", "fsdp")),
        P(("ctx", "fsdp"), None),
        P(("ctx", "fsdp"), None),
        P(("ctx", "fsdp"), None),
        P(("ctx", "fsdp"), None),
        P(("ctx", "fsdp"), None),
        P("ctx", "fsdp", None),
        P("ctx", "fsdp", None),
        P("ctx", "fsdp", None),
    )
    return jax.shard_map(body, mesh=mesh, in_specs=in_specs, out_specs=out_specs, check_vma=False)
```

```python
import functools
import math

import jax
import jax.numpy as jnp
import numpy as np
from jax import lax
from jax.experimental import pallas as pl
from jax.experimental.pallas import tpu as pltpu
from jax.sharding import PartitionSpec as P

HEADS = 16


epsilon = 1e-05
neg_large = -1e30
low = jnp.bfloat16
exact = jnp.float32


def exchange(x, axis):
    return lax.all_to_all(x, axis, split_axis=0, concat_axis=0, tiled=True)


def bits_down(count):
    return [1 << i for i in range(count.bit_length() - 1)][::-1]


class Links:
    def __init__(self, sends, recvs, locals_):
        self.sends, self.recvs, self.locals = sends, recvs, locals_
        self.count = self.local_count = 0
        self.open = {}
        self.seen = {}

    def send(self, src, dst, **to):
        copy = pltpu.make_async_remote_copy(
            src_ref=src,
            dst_ref=dst,
            send_sem=self.sends.at[self.count],
            recv_sem=self.recvs.at[self.count],
            device_id=to,
            device_id_type=pl.DeviceIdType.MESH,
        )
        self.count += 1
        copy.start()
        self.open[id(copy)] = (copy, True)
        return copy

    def move(self, src, dst):
        copy = pltpu.make_async_copy(src, dst, self.locals.at[self.local_count])
        self.local_count += 1
        copy.start()
        self.open[id(copy)] = (copy, False)
        return copy

    def left(self, copy):
        if id(copy) in self.open:
            copy, remote = self.open.pop(id(copy))
            self.seen[id(copy), "left"] = copy
            copy.wait_send() if remote else copy.wait()

    def arrived(self, copy):
        if (id(copy), "in") not in self.seen:
            self.seen[id(copy), "in"] = copy
            copy.wait_recv()

    def close(self):
        for copy, _ in list(self.open.values()):
            self.left(copy)


def greet(c, z, nc, nz):
    barrier = pltpu.get_barrier_semaphore()
    for d in range(1, nc):
        pl.semaphore_signal(
            barrier, inc=1, device_id={"ctx": c ^ d}, device_id_type=pl.DeviceIdType.MESH
        )
    for s in range(1, nz):
        pl.semaphore_signal(
            barrier, inc=1, device_id={"fsdp": z ^ s}, device_id_type=pl.DeviceIdType.MESH
        )
    pl.semaphore_wait(barrier, nc - 1 + nz - 1)


def kdot(left, right, dims=((1,), (0,)), precision=None):
    return lax.dot_general(
        left, right, (dims, ((), ())), preferred_element_type=exact, precision=precision
    )


def slots_of(cfg, mask_rows, upper):
    rank = kdot(mask_rows.astype(low), upper)
    return jnp.where(mask_rows > 0, rank, 0.0)


def plane_ranks(cfg, routes, z):
    nc, tokens = cfg["nc"], cfg["tokens"]
    expert = lax.broadcasted_iota(jnp.int32, (nc, tokens), 0) * cfg["exp_local"] + z // cfg["split"]
    mask = jnp.zeros((nc, tokens), exact)
    for k in range(cfg["top"]):
        mask = jnp.where(routes[k : k + 1, :] == expert, 1.0, mask)
    upper = jnp.where(
        lax.broadcasted_iota(jnp.int32, (tokens, tokens), 0)
        <= lax.broadcasted_iota(jnp.int32, (tokens, tokens), 1),
        1.0,
        0.0,
    ).astype(low)
    return slots_of(cfg, mask, upper)


def fill_hot(cfg, ranks, hot_ref):
    cap, tokens = cfg["cap"], cfg["tokens"]
    number = lax.broadcasted_iota(jnp.int32, (cap, tokens), 0).astype(exact) + 1.0
    for k in range(cfg["nc"]):
        hit = jnp.where(ranks[k : k + 1, :] == number, 1.0, 0.0)
        hot_ref[k * cap : (k + 1) * cap, :] = hit.astype(low)


def front_kernel(
    cfg,
    x_ref, wq_ref, wk_ref, wv_ref, wo_ref, gt_ref, rt_ref, ro_ref, cot_ref, gp_ref, up_ref, dp_ref, cos_ref, sin_ref,
    a1_out, w_full, raw_out, stat_out, rot_out, ob_out, wo_full, r1_out, r_all, g_all, t_all,
    gate_full, up_full, down_full, cot_rows, cot_near, in_rows, in_near,
    xbuf, wbuf, obw, gbuf, gfull, rbuf, tbuf, raw, stat, total, rq, rk, rot, opos, odev, orecv, r1, a2, cbuf, abuf, hot, cs,
    sends, recvs, locals_,
):
    nc, nz, tokens, width = cfg["nc"], cfg["nz"], cfg["tokens"], cfg["width"]
    cols, rows_w, length, cap = cfg["cols"], cfg["rows_w"], cfg["length"], cfg["cap"]
    hs = 128
    heads = cols // hs
    half = tokens // 2
    block = cfg["block"]
    blocks = length // block
    c, z = lax.axis_index("ctx"), lax.axis_index("fsdp")
    links = Links(sends, recvs, locals_)
    ds = pl.ds
    same = [d for d in range(2, nc, 2)]
    steps = bits_down(nz)

    own = []
    own.append(links.move(x_ref, xbuf.at[ds(c * tokens, tokens)]))
    for j, ref in enumerate((wq_ref, wk_ref, wv_ref)):
        at = pl.multiple_of(c * cols, 128)
        own.append(links.move(ref.at[:, ds(at, cols)], wbuf.at[j, c, z]))
    own.append(links.move(wo_ref, obw.at[c, z]))
    own.append(links.move(gt_ref, gbuf.at[c, z]))
    own.append(links.move(rt_ref, rbuf.at[c, z]))
    own.append(links.move(ro_ref, tbuf.at[c, z]))
    own.append(links.move(cot_ref, cbuf.at[0]))
    mine = links.move(gp_ref.at[z], gate_full.at[z])
    mine_up = links.move(up_ref.at[z], up_full.at[z])
    mine_down = links.move(dp_ref.at[z], down_full.at[z])
    greet(c, z, nc, nz)

    slices = []
    for d in range(1, nc):
        peer = c ^ d
        at = pl.multiple_of(peer * cols, 128)
        for j, ref in enumerate((wq_ref, wk_ref, wv_ref)):
            slices.append(links.send(ref.at[:, ds(at, cols)], wbuf.at[j, c, z], ctx=peer))
    small_z = []
    for s in range(1, nz):
        for src, dst in ((gt_ref, gbuf), (rt_ref, rbuf), (ro_ref, tbuf)):
            small_z.append(links.send(src, dst.at[c, z], fsdp=z ^ s))
    wo_near, cot_copies = {}, {}

    def wo_send(s, bit):
        place = obw.at[c, z ^ s]
        wo_near[s | bit] = links.send(place, place, fsdp=z ^ bit)

    def cot_send(s, bit):
        cot_copies[s | bit] = links.send(cbuf.at[s], cbuf.at[s | bit], fsdp=z ^ bit)

    x_at = xbuf.at[ds(c * tokens, tokens)]
    x_same = {d: links.send(x_ref, x_at, ctx=c ^ d) for d in same}
    x_side = [links.send(x_ref, x_at, ctx=c ^ 1)]
    for copy in own:
        links.left(copy)
    for bit in steps:
        wo_send(0, bit)
    for bit in steps:
        cot_send(0, bit)

    for copy in slices:
        links.arrived(copy)
    w_near = {}

    def w_send(s, bit):
        place = wbuf.at[:, :, z ^ s]
        w_near[s | bit] = links.send(place, place, fsdp=z ^ bit)

    for bit in steps:
        w_send(0, bit)
    for copy in small_z:
        links.arrived(copy)
    small_c = []
    for d in range(1, nc):
        for buf in (gbuf, rbuf, tbuf):
            small_c.append(links.send(buf.at[c], buf.at[c], ctx=c ^ d))
    for d in same:
        links.arrived(x_same[d])
        place = xbuf.at[ds((c ^ d) * tokens, tokens)]
        x_side.append(links.send(place, place, ctx=c ^ 1))

    def forward(waits, send):
        for at, bit in enumerate(steps):
            held = [0]
            for earlier in steps[:at]:
                held += [s | earlier for s in held]
            for s in held[1:]:
                links.arrived(waits[s])
                send(s, bit)

    forward(w_near, w_send)
    for copy in small_c:
        links.arrived(copy)
    per = 128 // rows_w
    groups = nz // per
    for k in range(nc):
        for g in range(groups):
            tile = gbuf[k, g * per]
            for p in range(1, per):
                tile = tile + gbuf[k, g * per + p]
            at = (k * groups + g) * 128
            gfull[:, at : at + 128] = tile
    for copy in x_side:
        links.arrived(copy)
    for copy in list(x_same.values()) + x_side:
        links.left(copy)

    chunk = cfg["chunk"]

    def norm_rows(i, _):
        at = pl.multiple_of(i * chunk, chunk)
        v = xbuf[ds(at, chunk), :].astype(exact)
        v = v * lax.rsqrt(jnp.mean(v * v, axis=-1, keepdims=True) + epsilon) * gfull[0:1, :]
        xbuf[ds(at, chunk), :] = v.astype(low)
        return 0

    lax.fori_loop(0, length // chunk, norm_rows, 0)
    a1_copy = links.move(xbuf, a1_out)

    last = steps[-1]
    for s in range(1, nz):
        if s & last:
            links.arrived(w_near[s])
    experts_in = []
    for s in range(1, nz):
        experts_in.append(links.send(gp_ref.at[z ^ s], gate_full.at[z], fsdp=z ^ s))
    w_copy = links.move(wbuf, w_full)

    one_row = lax.broadcasted_iota(jnp.int32, (8, cols), 0)
    pick_q = jnp.where(one_row == 0, 1.0, 0.0)
    pick_k = jnp.where(one_row == 1, 1.0, 0.0)
    best = lax.Precision.HIGHEST

    def project(i, _):
        at = pl.multiple_of(i * block, block)
        rows = xbuf[ds(at, block), :]
        sums = jnp.zeros((8, block), exact)
        for j in range(3):
            weight = wbuf[j].reshape(width, cols)
            v = kdot(rows, weight)
            raw[ds(at, block), j * cols : (j + 1) * cols] = v
            if j < 2:
                sums += kdot(pick_k if j else pick_q, v * v, ((1,), (1,)), best)
        stat[c, :, ds(at, block)] = sums
        return 0

    lax.fori_loop(0, blocks, project, 0)
    raw_copy = links.move(raw, raw_out)
    stats = [links.send(stat.at[c], stat.at[c], ctx=c ^ d) for d in range(1, nc)]
    forward(wo_near, wo_send)
    for s in range(1, nz):
        if s & last:
            links.arrived(wo_near[s])
    wo_same = {d: links.send(obw.at[c], obw.at[c], ctx=c ^ d) for d in same}
    wo_side = [links.send(obw.at[c], obw.at[c], ctx=c ^ 1)]
    for copy in stats:
        links.arrived(copy)
    summed = stat[0]
    for k in range(1, nc):
        summed += stat[k]
    total[...] = summed
    row8 = lax.broadcasted_iota(jnp.int32, (8, hs), 0)

    def columns(i, _):
        at = pl.multiple_of(i * block, block)
        part = total[:, ds(at, block)]
        for row, dst in ((0, rq), (1, rk)):
            sel = jnp.where(row8 == row, 1.0, 0.0)
            ms = kdot(part, sel, ((0,), (0,)), best)
            dst[ds(at, block), :] = lax.rsqrt(ms / width + epsilon)
        return 0

    lax.fori_loop(0, blocks, columns, 0)
    stat_copy = links.move(total, stat_out)

    def turn(i, _):
        d, side = i // 2, i % 2
        at = pl.multiple_of(d * tokens + side * half, half)
        to = pl.multiple_of(jnp.where(side == 0, d, 2 * nc - 1 - d) * half, half)
        cosine, sine = cos_ref[ds(at, half), :], sin_ref[ds(at, half), :]
        for h in range(heads):
            for j, scale in ((0, rq), (1, rk)):
                lane = j * cols + h * hs
                gain = gfull[1 + j : 2 + j, ds(pl.multiple_of(c * cols + h * hs, hs), hs)]
                v = raw[ds(at, half), lane : lane + hs] * scale[ds(at, half), :] * gain
                v = v * cosine + pltpu.roll(v, hs // 2, 1) * sine
                rot[j, ds(to, half), h * hs : (h + 1) * hs] = v.astype(low)
        rot[2, ds(to, half), :] = raw[ds(at, half), 2 * cols : 3 * cols].astype(low)
        return 0

    lax.fori_loop(0, 2 * nc, turn, 0)
    rot_copy = links.move(rot, rot_out)
    forward(cot_copies, cot_send)
    for s in range(1, nz):
        experts_in.append(links.send(up_ref.at[z ^ s], up_full.at[z], fsdp=z ^ s))

    scale = hs ** -0.5
    for h in range(heads):
        lanes = slice(h * hs, (h + 1) * hs)
        for i in range(blocks):
            count = (i + 1) * block
            q = rot[0, i * block : count, lanes]
            s = kdot(q, rot[1, :count, lanes], ((1,), (1,))) * scale
            row = lax.broadcasted_iota(jnp.int32, (block, count), 0) + i * block
            col = lax.broadcasted_iota(jnp.int32, (block, count), 1)
            s = jnp.where(col <= row, s, neg_large)
            p = jnp.exp(s - jnp.max(s, axis=-1, keepdims=True))
            p = p * (1.0 / jnp.sum(p, axis=-1, keepdims=True))
            opos[i * block : count, lanes] = kdot(p.astype(low), rot[2, :count, lanes]).astype(low)

    def place(i, _):
        d, side = i // 2, i % 2
        to = pl.multiple_of(d * tokens + side * half, half)
        at = pl.multiple_of(jnp.where(side == 0, d, 2 * nc - 1 - d) * half, half)
        odev[ds(to, half), :] = opos[ds(at, half), :]
        return 0

    lax.fori_loop(0, 2 * nc, place, 0)
    ob_copy = links.move(odev, ob_out)
    mixed = []
    for d in range(1, nc):
        src = odev.at[ds((c ^ d) * tokens, tokens)]
        mixed.append(links.send(src, orecv.at[c], ctx=c ^ d))
    own_mixed = links.move(odev.at[ds(c * tokens, tokens)], orecv.at[c])
    for d in same:
        links.arrived(wo_same[d])
        place_at = obw.at[c ^ d]
        wo_side.append(links.send(place_at, place_at, ctx=c ^ 1))

    for s in range(1, nz):
        if s & last:
            links.arrived(cot_copies[s])
    near_copy = links.move(cbuf, cot_near)
    rows_sent = []
    slot_busy = [[], []]

    def dispatch(s, near, landing):
        slot = s % 2
        for copy in slot_busy[slot]:
            links.left(copy)
        fill_hot(cfg, plane_ranks(cfg, tbuf[c, z ^ s], z), hot)
        cs[slot] = kdot(hot[...], near[s]).astype(low)
        busy = []
        for d in range(1, nc):
            src = cs.at[slot, ds((c ^ d) * cap, cap)]
            copy = links.send(src, landing.at[s, c], ctx=c ^ d)
            rows_sent.append(copy)
            busy.append(copy)
        busy.append(links.move(cs.at[slot, ds(c * cap, cap)], landing.at[s, c]))
        slot_busy[slot] = busy

    for s in range(nz):
        dispatch(s, cbuf, cot_rows)

    for copy in wo_side:
        links.arrived(copy)
    wo_copy = links.move(obw, wo_full)
    for copy in mixed:
        links.arrived(copy)
    links.left(own_mixed)
    r1[...] = jnp.zeros_like(r1)

    def mix(k, _):
        r1[...] += kdot(orecv[k], obw[k].reshape(cols, width))
        return 0

    lax.fori_loop(0, nc, mix, 0)
    xin = links.move(x_ref, a2)
    links.left(xin)
    v = r1[...] + a2[...].astype(exact)
    r1[...] = v
    n2 = v * lax.rsqrt(jnp.mean(v * v, axis=-1, keepdims=True) + epsilon)
    abuf[0] = (n2 * gfull[3:4, :]).astype(low)
    in_copies = {}

    def in_send(s, bit):
        in_copies[s | bit] = links.send(abuf.at[s], abuf.at[s | bit], fsdp=z ^ bit)

    for bit in steps:
        in_send(0, bit)
    links.move(r1, r1_out)
    dispatch(0, abuf, in_rows)
    forward(in_copies, in_send)
    for s in range(1, nz):
        experts_in.append(links.send(dp_ref.at[z ^ s], down_full.at[z], fsdp=z ^ s))
    links.move(rbuf, r_all)
    links.move(gfull, g_all)
    links.move(tbuf, t_all)
    for s in range(1, nz):
        links.arrived(in_copies[s])
        dispatch(s, abuf, in_rows)
    links.move(abuf, in_near)
    for copy in experts_in + rows_sent:
        links.arrived(copy)
    links.close()


def front(cfg, x, w_query, w_key, w_value, w_out, gains, router, routes, cot, gate_pieces, up_pieces, down_pieces, cosine, sine):
    nc, nz, tokens, width = cfg["nc"], cfg["nz"], cfg["tokens"], cfg["width"]
    cols, rows_w, length, cap = cfg["cols"], cfg["rows_w"], cfg["length"], cfg["cap"]
    rows, part = gate_pieces.shape[1:]
    rows_d = down_pieces.shape[1]
    shape = jax.ShapeDtypeStruct
    any_, vmem = pl.BlockSpec(memory_space=pl.ANY), pl.BlockSpec(memory_space=pltpu.VMEM)
    top_rows = routes.shape[0]
    outs = [
        shape((length, width), low),
        shape((3, nc, nz, rows_w, cols), low),
        shape((length, 3 * cols), exact),
        shape((8, length), exact),
        shape((3, length, cols), low),
        shape((length, cols), low),
        shape((nc, nz, rows_w, width), low),
        shape((tokens, width), exact),
        shape((nc, nz, rows_w, 128), low),
        shape((8, width), exact),
        shape((nc, nz, top_rows, tokens), jnp.int32),
        shape((nz, rows, part), low),
        shape((nz, rows, part), low),
        shape((nz, rows_d, width), low),
        shape((nz, nc, cap, width), low),
        shape((nz, tokens, width), low),
        shape((nz, nc, cap, width), low),
        shape((nz, tokens, width), low),
    ]
    scratch = [
        pltpu.VMEM((length, width), low),
        pltpu.VMEM((3, nc, nz, rows_w, cols), low),
        pltpu.VMEM((nc, nz, rows_w, width), low),
        pltpu.VMEM((nc, nz, 8, 128), exact),
        pltpu.VMEM((8, width), exact),
        pltpu.VMEM((nc, nz, rows_w, 128), low),
        pltpu.VMEM((nc, nz, top_rows, tokens), jnp.int32),
        pltpu.VMEM((length, 3 * cols), exact),
        pltpu.VMEM((nc, 8, length), exact),
        pltpu.VMEM((8, length), exact),
        pltpu.VMEM((length, 128), exact),
        pltpu.VMEM((length, 128), exact),
        pltpu.VMEM((3, length, cols), low),
        pltpu.VMEM((length, cols), low),
        pltpu.VMEM((length, cols), low),
        pltpu.VMEM((nc, tokens, cols), low),
        pltpu.VMEM((tokens, width), exact),
        pltpu.VMEM((tokens, width), low),
        pltpu.VMEM((nz, tokens, width), low),
        pltpu.VMEM((nz, tokens, width), low),
        pltpu.VMEM((nc * cap, tokens), low),
        pltpu.VMEM((2, nc * cap, width), low),
        pltpu.SemaphoreType.DMA((cfg["copies"],)),
        pltpu.SemaphoreType.DMA((cfg["copies"],)),
        pltpu.SemaphoreType.DMA((64,)),
    ]
    return pl.pallas_call(
        functools.partial(front_kernel, cfg),
        out_shape=outs,
        in_specs=[any_] * 12 + [vmem] * 2,
        out_specs=[any_] * len(outs),
        scratch_shapes=scratch,
        compiler_params=pltpu.CompilerParams(
            collective_id=0, has_side_effects=True, vmem_limit_bytes=cfg["vmem"]
        ),
        name="front",
    )(x, w_query, w_key, w_value, w_out, gains, router, routes, cot, gate_pieces, up_pieces, down_pieces, cosine, sine)


def expert_kernel(
    cfg,
    rows_ref, cotr_ref, rt_ref, tb_ref, wg_ref, wu_ref, wd_ref, near_ref, cotn_ref, r1_ref, gain_ref,
    hidden_out, dr1_out, datt_out, dlog_out, fgain_out, gd_land, gg_land, gu_out,
    back, in_back, out_land, in_land, ebh, rbh,
    wg, wu, wd, rows, cotb, gin, gdb, du, eb, rb, tile, ranks, hot, metab, gate_rows, dgs, dgl,
    sends, recvs, locals_,
):
    nc, nz, tokens, width = cfg["nc"], cfg["nz"], cfg["tokens"], cfg["width"]
    cap, part, split, exp_local = cfg["cap"], cfg["part"], cfg["split"], cfg["exp_local"]
    ch = nc * cap
    total = nz * ch
    c, z = lax.axis_index("ctx"), lax.axis_index("fsdp")
    links = Links(sends, recvs, locals_)
    ds = pl.ds
    expert = c * exp_local + z // split
    best = lax.Precision.HIGHEST
    peers = list(range(1, nc))

    loads = [links.move(wg_ref, wg), links.move(wu_ref, wu), links.move(wd_ref, wd)]
    loads.append(links.move(rows_ref, rows))
    cot_base = links.local_count
    links.local_count += nz
    send_base = links.count
    links.count += 2 * nz * (nc - 1)
    keep_base = links.local_count
    links.local_count += 2 * nz
    off_base = links.local_count
    links.local_count += 2 * nz

    def cot_load(s, slot):
        return pltpu.make_async_copy(
            cotr_ref.at[ds(s * ch, ch)], cotb.at[slot], locals_.at[cot_base + s]
        )

    def chunk_copies(s, which):
        buf, landing = ((ebh, back), (rbh, in_back))[which]
        base = send_base + which * nz * (nc - 1) + s * (nc - 1)
        out = []
        for d in peers:
            out.append(
                pltpu.make_async_remote_copy(
                    src_ref=buf.at[s, ds((c ^ d) * cap, cap)],
                    dst_ref=landing.at[s, c],
                    send_sem=sends.at[base + d - 1],
                    recv_sem=recvs.at[base + d - 1],
                    device_id={"ctx": c ^ d},
                    device_id_type=pl.DeviceIdType.MESH,
                )
            )
        return out

    def keep_copy(s, which):
        landing = (back, in_back)[which]
        return pltpu.make_async_copy(
            (ebh, rbh)[which].at[s, ds(c * cap, cap)],
            landing.at[s, c],
            locals_.at[keep_base + which * nz + s],
        )

    def off_copy(s, which):
        return pltpu.make_async_copy(
            (eb, rb)[which], (ebh, rbh)[which].at[s], locals_.at[off_base + which * nz + s]
        )

    cot_load(nz - 1, 0).start()
    greet(c, z, nc, nz)
    for copy in loads:
        links.left(copy)

    expert_rows = lax.broadcasted_iota(jnp.int32, (128, tokens), 0)
    upper = jnp.where(
        lax.broadcasted_iota(jnp.int32, (tokens, tokens), 0)
        <= lax.broadcasted_iota(jnp.int32, (tokens, tokens), 1),
        1.0,
        0.0,
    ).astype(low)

    def routed(block):
        chosen = jnp.zeros((128, tokens), exact)
        for k in range(cfg["top"]):
            chosen = jnp.where(block[k : k + 1, :] == expert_rows, 1.0, chosen)
        return chosen

    sub = min(256, ch)
    lane = lax.broadcasted_iota(jnp.int32, (sub, 128), 1)

    def gate_of(block, picked):
        logits = kdot(block, rt_ref[...], ((1,), (1,)))
        logits = jnp.where(picked > 0.5, logits, neg_large)
        weight = jnp.exp(logits - jnp.max(logits, axis=-1, keepdims=True))
        gate = jnp.sum(jnp.where(lane == expert, weight, 0.0), axis=-1, keepdims=True)
        return gate / jnp.sum(weight, axis=-1, keepdims=True)

    def first_work(s, _):
        for k in range(nc):
            block = tb_ref[k, z ^ s]
            found = jnp.where(block == expert, 1.0, 0.0)
            ranks[k : k + 1, :] = jnp.max(found, axis=0, keepdims=True)
        ranks[...] = slots_of(cfg, ranks[...], upper)
        fill_hot(cfg, ranks[...], hot)
        for k in range(nc):
            chosen = routed(tb_ref[k, z ^ s]).astype(low)
            metab[k * cap : (k + 1) * cap, :] = kdot(
                hot[k * cap : (k + 1) * cap, :], chosen, ((1,), (1,))
            )

        def some_rows(j, _):
            here = pl.multiple_of(j * sub, sub)
            at = pl.multiple_of(s * ch + j * sub, sub)
            span, to = ds(here, sub), ds(at, sub)
            block = rows[to, :]
            gate = gate_of(block, metab[span, :])
            g = kdot(block, wg[...])
            u = kdot(block, wu[...])
            inner = (g * (1.0 / (1.0 + jnp.exp(-g))) * u).astype(low)
            gin[to, :] = (inner.astype(exact) * gate).astype(low)
            gate_rows[to, :] = jnp.broadcast_to(gate, (sub, 128))
            return 0

        lax.fori_loop(0, ch // sub, some_rows, 0)
        return 0

    lax.fori_loop(0, nz, first_work, 0)

    rows_d = part // nz
    step = 256 if nz * ch <= 2048 else 128
    tile_base = links.local_count
    links.local_count += width // step

    def tile_load(k):
        return pltpu.make_async_copy(
            cotr_ref.at[:, ds(k * step, step)], tile.at[lax.rem(k, 2)], locals_.at[tile_base + k]
        )

    tile_load(0).start()

    def down_tile(k, _):
        @pl.when(k + 1 < width // step)
        def _():
            tile_load(k + 1).start()

        tile_load(k).wait()
        at = pl.multiple_of(k * step, step)
        gdb[:, ds(at, step)] = kdot(gin[...], tile[lax.rem(k, 2)], ((0,), (0,))).astype(low)
        return 0

    lax.fori_loop(0, width // step, down_tile, 0)
    grads_out = []
    for s in range(1, nz):
        src = gdb.at[ds(pl.multiple_of((z ^ s) * rows_d, rows_d), rows_d)]
        grads_out.append(links.send(src, gd_land.at[z], fsdp=z ^ s))
    links.move(gdb.at[ds(pl.multiple_of(z * rows_d, rows_d), rows_d)], gd_land.at[z])
    def work(i, _):
        s = nz - 1 - i
        slot = lax.rem(i, 2)

        @pl.when(i + 1 < nz)
        def _():
            cot_load(s - 1, 1 - slot).start()

        cot_load(s, slot).wait()

        def some_rows(j, _):
            here = pl.multiple_of(j * sub, sub)
            at = pl.multiple_of(s * ch + j * sub, sub)
            span, to = ds(here, sub), ds(at, sub)
            block = rows[to, :]
            gate = gate_rows[to, 0:1]
            g = kdot(block, wg[...])
            u = kdot(block, wu[...])
            sg = 1.0 / (1.0 + jnp.exp(-g))
            act = g * sg
            inner = (act * u).astype(low)
            eb[span, :] = kdot(inner, wd[...]).astype(low)
            dinner = kdot(cotb[slot, span, :], wd[...], ((1,), (1,))) * gate
            dg_low = (dinner * u * sg * (1.0 + g * (1.0 - sg))).astype(low)
            du_low = (dinner * act).astype(low)
            gin[to, :] = dg_low
            du[to, :] = du_low
            rb[span, :] = (
                kdot(dg_low, wg[...], ((1,), (1,))) + kdot(du_low, wu[...], ((1,), (1,)))
            ).astype(low)
            return 0

        lax.fori_loop(0, ch // sub, some_rows, 0)
        for which in (0, 1):
            off_copy(s, which).start()
        for which in (0, 1):
            off_copy(s, which).wait()
            for copy in chunk_copies(s, which):
                copy.start()
            keep_copy(s, which).start()
        return 0

    lax.fori_loop(0, nz, work, 0)

    rows_g = width // nz

    def rows_tile(left, dst):
        def one(k, _):
            at = pl.multiple_of(k * step, step)
            dst[ds(at, step), :] = kdot(rows[:, ds(at, step)], left[...], ((0,), (0,))).astype(low)
            return 0

        lax.fori_loop(0, width // step, one, 0)

    rows_tile(gin, wg)
    for s in range(1, nz):
        src = wg.at[ds(pl.multiple_of((z ^ s) * rows_g, rows_g), rows_g)]
        grads_out.append(links.send(src, gg_land.at[z], fsdp=z ^ s))
    links.move(wg.at[ds(pl.multiple_of(z * rows_g, rows_g), rows_g)], gg_land.at[z])
    rows_tile(du, wu)
    links.move(wu, gu_out)

    spare = {}
    at = 0
    for name, count in (
        ("back", ch), ("in_back", ch), ("near", tokens), ("cot", tokens), ("out0", tokens),
        ("in0", tokens),
    ):
        spare[name] = rows.at[at : at + count]
        at += count
    stage = {0: (spare["out0"], spare["in0"]), 1: (cotb.at[0, 0:tokens], cotb.at[1, 0:tokens])}
    extra = (cotb.at[0, tokens : 2 * tokens], cotb.at[1, tokens : 2 * tokens])
    pick_rows = lax.broadcasted_iota(jnp.int32, (nc, 128), 0)
    pick_lane = lax.broadcasted_iota(jnp.int32, (nc, 128), 1)
    homeward = {}
    gate_home = {}
    busy = {0: [], 1: []}
    gates_own = None
    sums = None
    for s in range(nz - 1, -1, -1):
        for which in (0, 1):
            out = chunk_copies(s, which)
            for copy in out:
                copy.wait_recv()
            keep_copy(s, which).wait()
        fetch = []
        for k in range(nc):
            fetch.append(links.move(back.at[s, k], rows.at[k * cap : (k + 1) * cap]))
            fetch.append(links.move(in_back.at[s, k], rows.at[ch + k * cap : ch + (k + 1) * cap]))
        fetch.append(links.move(near_ref.at[s], spare["near"]))
        fetch.append(links.move(cotn_ref.at[s], spare["cot"]))
        block = tb_ref[c, z ^ s]
        fill_hot(cfg, plane_ranks(cfg, block, z), hot)
        chosen = routed(block)
        for copy in fetch:
            links.left(copy)
        logits = kdot(rt_ref[...], spare["near"][...], ((1,), (1,)))
        logits = jnp.where(chosen > 0.5, logits, neg_large)
        weight = jnp.exp(logits - jnp.max(logits, axis=0, keepdims=True))
        gates = weight / jnp.sum(weight, axis=0, keepdims=True)
        sel = jnp.where(pick_lane == pick_rows * exp_local + z // split, 1.0, 0.0)
        plane = kdot(sel, gates, ((1,), (0,)), best)
        slot_grad = kdot(spare["back"][...], spare["cot"][...], ((1,), (1,)))
        for k in range(nc):
            span = slice(k * cap, (k + 1) * cap)
            hit = hot[span, :].astype(exact)
            dgs[s, k : k + 1, :] = jnp.sum(hit * slot_grad[span, :], axis=0, keepdims=True)
        in_part = kdot(hot[...], spare["in_back"][...], ((0,), (0,)))
        for k in range(nc):
            span = slice(k * cap, (k + 1) * cap)
            hot[span, :] = (hot[span, :].astype(exact) * plane[k : k + 1, :]).astype(low)
        out_part = kdot(hot[...], spare["back"][...], ((0,), (0,)))
        lowest = s & -s
        bit = 1
        while bit < nz and (s == 0 or bit < lowest):
            for copy in homeward[s | bit]:
                links.arrived(copy)
            got = [links.move(out_land.at[s | bit], extra[0]), links.move(in_land.at[s | bit], extra[1])]
            for copy in got:
                links.left(copy)
            out_part += extra[0][...].astype(exact)
            in_part += extra[1][...].astype(exact)
            bit *= 2
        if s:
            slot = s % 2
            for copy in busy[slot]:
                links.left(copy)
            stage[slot][0][...] = out_part.astype(low)
            stage[slot][1][...] = in_part.astype(low)
            homeward[s] = [
                links.send(stage[slot][0], out_land.at[s], fsdp=z ^ lowest),
                links.send(stage[slot][1], in_land.at[s], fsdp=z ^ lowest),
            ]
            busy[slot] = homeward[s]
            gate_home[s] = links.send(dgs.at[s], dgl.at[s], fsdp=z ^ s)
        else:
            gates_own = gates
            sums = (out_part, in_part)

    dgate = jnp.zeros((128, tokens), exact)
    for s in range(nz):
        if s:
            links.arrived(gate_home[s])
        here = dgl[s] if s else dgs[0]
        sel = jnp.where(pick_lane == pick_rows * exp_local + (z ^ s) // split, 1.0, 0.0)
        dgate += kdot(sel, here, ((0,), (0,)), best)
    dchosen = gates_own * (dgate - jnp.sum(gates_own * dgate, axis=0, keepdims=True))
    dlog = dchosen.astype(low)
    hot[0:128, :] = dlog
    dlog_copy = links.move(hot.at[0:128], dlog_out)
    out_part, in_part = sums
    da2 = in_part + kdot(dlog, rt_ref[...], ((0,), (0,)))
    r1 = r1_ref[...]
    for copies in busy.values():
        for copy in copies:
            links.left(copy)
    stage[0][0][...] = (r1 + out_part).astype(low)
    links.move(stage[0][0], hidden_out)
    rs = lax.rsqrt(jnp.mean(r1 * r1, axis=-1, keepdims=True) + epsilon)
    n2 = r1 * rs
    dm = da2 * gain_ref[3:4, :]
    fgain_out[...] = jnp.broadcast_to(jnp.sum(da2 * n2, axis=0, keepdims=True), (8, width))
    inner_mean = jnp.mean(dm * n2, axis=-1, keepdims=True)
    dr1 = spare["cot"][...].astype(exact) + rs * (dm - n2 * inner_mean)
    dr1_out[...] = dr1
    datt_out[...] = dr1.astype(low)
    for s in range(nz):
        for which in (0, 1):
            out = chunk_copies(s, which)
            for copy in out:
                copy.wait_send()
    for copy in grads_out:
        links.arrived(copy)
    links.close()


def run_experts(cfg, rows, cot_rows, router_t, routes, wg, wu, wd, near, cot_near, r1, gains):
    nc, nz, tokens, width = cfg["nc"], cfg["nz"], cfg["tokens"], cfg["width"]
    cap, part = cfg["cap"], cfg["part"]
    ch = nc * cap
    shape = jax.ShapeDtypeStruct
    any_, vmem = pl.BlockSpec(memory_space=pl.ANY), pl.BlockSpec(memory_space=pltpu.VMEM)
    outs = [
        (shape((tokens, width), low), any_),
        (shape((tokens, width), exact), vmem),
        (shape((tokens, width), low), vmem),
        (shape((128, tokens), low), any_),
        (shape((8, width), exact), vmem),
        (shape((nz, part // nz, width), low), any_),
        (shape((nz, width // nz, part), low), any_),
        (shape((width, part), low), any_),
        (shape((nz, nc, cap, width), low), any_),
        (shape((nz, nc, cap, width), low), any_),
        (shape((nz, tokens, width), low), any_),
        (shape((nz, tokens, width), low), any_),
        (shape((nz, ch, width), low), any_),
        (shape((nz, ch, width), low), any_),
    ]
    step = 256 if nz * ch <= 2048 else 128
    scratch = [
        pltpu.VMEM((width, part), low),
        pltpu.VMEM((width, part), low),
        pltpu.VMEM((part, width), low),
        pltpu.VMEM((nz * ch, width), low),
        pltpu.VMEM((2, ch, width), low),
        pltpu.VMEM((nz * ch, part), low),
        pltpu.VMEM((part, width), low),
        pltpu.VMEM((nz * ch, part), low),
        pltpu.VMEM((ch, width), low),
        pltpu.VMEM((ch, width), low),
        pltpu.VMEM((2, nz * ch, step), low),
        pltpu.VMEM((nc, tokens), exact),
        pltpu.VMEM((ch, tokens), low),
        pltpu.VMEM((ch, 128), exact),
        pltpu.VMEM((nz * ch, 128), exact),
        pltpu.VMEM((nz, nc, tokens), exact),
        pltpu.VMEM((nz, nc, tokens), exact),
        pltpu.SemaphoreType.DMA((2 * nz * nc + 8 * nz,)),
        pltpu.SemaphoreType.DMA((2 * nz * nc + 8 * nz,)),
        pltpu.SemaphoreType.DMA((2 * nz * nc + 16 * nz + width // step + 16,)),
    ]
    return pl.pallas_call(
        functools.partial(expert_kernel, cfg),
        out_shape=[o[0] for o in outs],
        in_specs=[any_, any_, vmem, vmem, any_, any_, any_, any_, any_, vmem, vmem],
        out_specs=[o[1] for o in outs],
        scratch_shapes=scratch,
        compiler_params=pltpu.CompilerParams(
            collective_id=1, has_side_effects=True, vmem_limit_bytes=cfg["vmem"]
        ),
        name="experts",
    )(rows, cot_rows, router_t, routes, wg, wu, wd, near, cot_near, r1, gains)


def back_kernel(
    cfg,
    x_ref, dr1_ref, datt_ref, a1_ref, w_ref, raw_ref, stat_ref, rot_ref, ob_ref, wo_ref, gain_ref, fgain_ref,
    gu_ref, cos_ref, sin_ref,
    hidden_out, w_out, wo_out, gains_out, gu_land, pair_land, chip_land, wz_land, oz_land,
    wo, datt, a1, w, raw, rot, ob, dland, aq, ak, av, rq, rk, cq, ck, stat, total, dqkv, gw, go, gsum,
    wtemp, otemp, wsum, wl, xrow, xtemp, small_z, small_c,
    sends, recvs, locals_,
):
    nc, nz, tokens, width = cfg["nc"], cfg["nz"], cfg["tokens"], cfg["width"]
    cols, rows_w, length = cfg["cols"], cfg["rows_w"], cfg["length"]
    hs = 128
    heads = cols // hs
    half = tokens // 2
    block = cfg["block"]
    blocks = length // block
    c, z = lax.axis_index("ctx"), lax.axis_index("fsdp")
    links = Links(sends, recvs, locals_)
    ds = pl.ds
    best = lax.Precision.HIGHEST
    same = [d for d in range(2, nc, 2)]
    own_rows = ds(pl.multiple_of(c * tokens, tokens), tokens)

    wo_in = links.move(wo_ref, wo)
    datt_in = links.move(datt_ref, datt.at[own_rows])
    first = [links.move(rot_ref, rot), links.move(raw_ref.at[:, 0 : 2 * cols], raw), links.move(ob_ref, ob)]
    later = [links.move(w_ref, w), links.move(x_ref, xrow)]
    up_own = links.move(gu_ref.at[z], gu_land.at[z])
    greet(c, z, nc, nz)
    up_sends = [links.send(gu_ref.at[z ^ s], gu_land.at[z], fsdp=z ^ s) for s in range(1, nz)]
    links.left(datt_in)
    links.left(wo_in)

    heads_sent = []
    for d in range(1, nc):
        at = pl.multiple_of((c ^ d) * cols, cols)
        spot = dqkv.at[d * tokens : (d + 1) * tokens, 0:cols]
        spot[...] = kdot(datt[own_rows, :], wo[ds(at, cols), :], ((1,), (1,))).astype(low)
        heads_sent.append(links.send(spot, dland.at[c], ctx=c ^ d))
    at = pl.multiple_of(c * cols, cols)
    dland[c] = kdot(datt[own_rows, :], wo[ds(at, cols), :], ((1,), (1,))).astype(low)
    rows_same = {d: links.send(datt.at[own_rows], datt.at[own_rows], ctx=c ^ d) for d in same}
    rows_side = [links.send(datt.at[own_rows], datt.at[own_rows], ctx=c ^ 1)]
    for copy in first:
        links.left(copy)

    row8 = lax.broadcasted_iota(jnp.int32, (8, hs), 0)

    def columns(src, one, two, finish):
        def step(i, _):
            at = pl.multiple_of(i * block, block)
            part = src[:, ds(at, block)]
            for row, dst in ((0, one), (1, two)):
                sel = jnp.where(row8 == row, 1.0, 0.0)
                dst[ds(at, block), :] = finish(kdot(part, sel, ((0,), (0,)), best) / width)
            return 0

        lax.fori_loop(0, blocks, step, 0)

    columns(stat_ref, rq, rk, lambda v: lax.rsqrt(v + epsilon))
    ak[...] = jnp.zeros_like(ak)
    av[...] = jnp.zeros_like(av)
    gsum[...] = jnp.zeros_like(gsum)
    for copy in heads_sent:
        links.arrived(copy)
    for copy in heads_sent:
        links.left(copy)

    def place(i, _):
        d, side = i // 2, i % 2
        at = pl.multiple_of(side * half, half)
        to = pl.multiple_of(jnp.where(side == 0, d, 2 * nc - 1 - d) * half, half)
        aq[ds(to, half), :] = dland[d, ds(at, half), :].astype(exact)
        return 0

    lax.fori_loop(0, 2 * nc, place, 0)
    for d in same:
        links.arrived(rows_same[d])
        there = datt.at[ds(pl.multiple_of((c ^ d) * tokens, tokens), tokens)]
        rows_side.append(links.send(there, there, ctx=c ^ 1))

    scale = hs ** -0.5
    for h in range(heads):
        lanes = slice(h * hs, (h + 1) * hs)
        for i in range(blocks):
            count = (i + 1) * block
            here = slice(i * block, count)
            q, k, v = rot[0, here, lanes], rot[1, :count, lanes], rot[2, :count, lanes]
            do = aq[here, lanes].astype(low)
            s = kdot(q, k, ((1,), (1,))) * scale
            row = lax.broadcasted_iota(jnp.int32, (block, count), 0) + i * block
            col = lax.broadcasted_iota(jnp.int32, (block, count), 1)
            s = jnp.where(col <= row, s, neg_large)
            p = jnp.exp(s - jnp.max(s, axis=-1, keepdims=True))
            p = p * (1.0 / jnp.sum(p, axis=-1, keepdims=True))
            dp = kdot(do, v, ((1,), (1,)))
            delta = jnp.sum(p * dp, axis=-1, keepdims=True)
            dscore = (p * (dp - delta)).astype(low)
            av[:count, lanes] += kdot(p.astype(low), do, ((0,), (0,)))
            ak[:count, lanes] += kdot(dscore, q, ((0,), (0,))) * scale
            aq[here, lanes] = kdot(dscore, k) * scale

    def unturn(i, _):
        d, side = i // 2, i % 2
        at = pl.multiple_of(d * tokens + side * half, half)
        to = pl.multiple_of(jnp.where(side == 0, d, 2 * nc - 1 - d) * half, half)
        cosine, sine = cos_ref[ds(at, half), :], sin_ref[ds(at, half), :]
        for j, acc, scale_ref, sums in ((0, aq, rq, cq), (1, ak, rk, ck)):
            row_sum = jnp.zeros((half, 1), exact)
            for h in range(heads):
                lanes = slice(h * hs, (h + 1) * hs)
                lane = j * cols + h * hs
                v = acc[ds(to, half), lanes]
                v = v * cosine - pltpu.roll(v, hs // 2, 1) * sine
                acc[ds(to, half), lanes] = v
                normed = raw[ds(at, half), lane : lane + hs] * scale_ref[ds(at, half), :]
                v = v * normed
                gsum[j : j + 1, lanes] += jnp.sum(v, axis=0, keepdims=True)
                gain = gain_ref[1 + j : 2 + j, ds(pl.multiple_of(c * cols + h * hs, hs), hs)]
                row_sum += jnp.sum(v * gain, axis=-1, keepdims=True)
            sums[ds(at, half), :] = jnp.broadcast_to(row_sum, (half, hs))
        return 0

    lax.fori_loop(0, 2 * nc, unturn, 0)
    lane8 = lax.broadcasted_iota(jnp.int32, (8, hs), 1)

    def gather_sums(i, _):
        at = pl.multiple_of(i * block, block)
        part = jnp.zeros((8, block), exact)
        for row, src in ((0, cq), (1, ck)):
            sel = jnp.where((row8 == row) & (lane8 == 0), 1.0, 0.0)
            part += kdot(sel, src[ds(at, block), :], ((1,), (1,)), best)
        stat[c, :, ds(at, block)] = part
        return 0

    lax.fori_loop(0, blocks, gather_sums, 0)
    stats = [links.send(stat.at[c], stat.at[c], ctx=c ^ d) for d in range(1, nc)]

    for copy in rows_side:
        links.arrived(copy)
    tile = width // nc
    tile_base = links.local_count
    links.local_count += nc

    def tile_load(k):
        return pltpu.make_async_copy(
            a1_ref.at[:, ds(k * tile, tile)], a1.at[lax.rem(k, 2)], locals_.at[tile_base + k]
        )

    tile_load(0).start()

    def out_tile(k, _):
        at = pl.multiple_of(k * tile, tile)
        v = kdot(ob[...], datt[:, ds(at, tile)], ((0,), (0,))).astype(low)
        go[:, :, ds(at, tile)] = v.reshape(nz, rows_w, tile)
        return 0

    lax.fori_loop(0, nc, out_tile, 0)
    for copy in stats:
        links.arrived(copy)
    summed = stat[0]
    for k in range(1, nc):
        summed += stat[k]
    total[...] = summed
    columns(total, cq, ck, lambda v: v)

    def finish(i, _):
        d, side = i // 2, i % 2
        at = pl.multiple_of(d * tokens + side * half, half)
        to = pl.multiple_of(jnp.where(side == 0, d, 2 * nc - 1 - d) * half, half)
        for j, acc, scale_ref, sums in ((0, aq, rq, cq), (1, ak, rk, ck)):
            for h in range(heads):
                lanes = slice(h * hs, (h + 1) * hs)
                lane = j * cols + h * hs
                gain = gain_ref[1 + j : 2 + j, ds(pl.multiple_of(c * cols + h * hs, hs), hs)]
                normed = raw[ds(at, half), lane : lane + hs] * scale_ref[ds(at, half), :]
                v = acc[ds(to, half), lanes] * gain - normed * sums[ds(at, half), :]
                dqkv[ds(at, half), lane : lane + hs] = (v * scale_ref[ds(at, half), :]).astype(low)
        dqkv[ds(at, half), 2 * cols : 3 * cols] = av[ds(to, half), :].astype(low)
        return 0

    lax.fori_loop(0, 2 * nc, finish, 0)
    for copy in later:
        links.left(copy)
    for copy in list(rows_same.values()) + rows_side:
        links.left(copy)

    def w_tile(k, _):
        @pl.when(k + 1 < nc)
        def _():
            tile_load(k + 1).start()

        tile_load(k).wait()
        v = kdot(a1[lax.rem(k, 2)], dqkv[...], ((0,), (0,))).astype(low)
        for j in range(3):
            gw[j, k] = v[:, j * cols : (j + 1) * cols].reshape(nz, rows_w, cols)
        return 0

    lax.fori_loop(0, nc, w_tile, 0)
    home = {}

    def send_home(s):
        peer = z ^ (s & -s)
        home[s] = (
            links.send(gw.at[:, :, z ^ s], wz_land.at[s], fsdp=peer),
            links.send(go.at[z ^ s], oz_land.at[s], fsdp=peer),
        )

    def taken(s):
        w_sum = gw[:, :, z ^ s].astype(exact)
        o_sum = go[z ^ s].astype(exact)
        bit = 1
        while bit < nz and (s == 0 or bit < (s & -s)):
            for copy in home[s | bit]:
                links.arrived(copy)
            got = [links.move(wz_land.at[s | bit], wtemp), links.move(oz_land.at[s | bit], otemp)]
            for copy in got:
                links.left(copy)
            w_sum += wtemp[...].astype(exact)
            o_sum += otemp[...].astype(exact)
            bit *= 2
        return w_sum, o_sum

    for s in range(nz - 1, 0, -1):
        if s & 1:
            send_home(s)

    def partial(k):
        at = pl.multiple_of(k * tokens, tokens)
        v = jnp.zeros((tokens, width), exact)
        for j in range(3):
            v += kdot(dqkv[ds(at, tokens), j * cols : (j + 1) * cols], w[j], ((1,), (1,)))
        datt[ds(at, tokens), :] = v.astype(low)

    def rows_of(k):
        return datt.at[ds(pl.multiple_of(k * tokens, tokens), tokens)]

    evens = [0] + same
    pair, chip = {}, {}

    def other_core(m, _):
        partial(2 * m + 1 - lax.rem(c, 2))
        return 0

    def this_core(m, _):
        partial(2 * m + lax.rem(c, 2))
        return 0

    lax.fori_loop(0, nc // 2, other_core, 0)
    for m, d in enumerate(evens):
        pair[d] = links.send(rows_of((c ^ 1) ^ d), pair_land.at[m], ctx=c ^ 1)
    lax.fori_loop(0, nc // 2, this_core, 0)
    for m, d in list(enumerate(evens))[::-1]:
        links.arrived(pair[d])
        got = links.move(pair_land.at[m], xtemp)
        links.left(got)
        mine = rows_of(c ^ d)
        if d:
            mine[...] = (mine[...].astype(exact) + xtemp[...].astype(exact)).astype(low)
            chip[d] = links.send(mine, chip_land.at[m], ctx=c ^ d)
        else:
            grad_in = mine[...].astype(exact) + xtemp[...].astype(exact)
            hidden_out[...] = grad_in

    for s in range(nz - 2, 0, -1):
        if not s & 1:
            w_sum, o_sum = taken(s)
            gw[:, :, z ^ s] = w_sum.astype(low)
            go[z ^ s] = o_sum.astype(low)
            send_home(s)

    for m, d in enumerate(evens):
        if d:
            links.arrived(chip[d])
            got = links.move(chip_land.at[m], xtemp)
            links.left(got)
            hidden_out[...] += xtemp[...].astype(exact)
    x = xrow[...].astype(exact)
    rs = lax.rsqrt(jnp.mean(x * x, axis=-1, keepdims=True) + epsilon)
    n1 = x * rs
    grad_in = hidden_out[...]
    gains_out[...] = jnp.zeros_like(gains_out)
    gains_out[0:1, :] = jnp.sum(grad_in * n1, axis=0, keepdims=True)
    for j in range(2):
        own_lanes = ds(pl.multiple_of(c * cols, cols), cols)
        gains_out[1 + j : 2 + j, own_lanes] = gsum[j : j + 1, :]
    gains_out[3:4, :] = fgain_ref[0:1, :]
    dn = grad_in * gain_ref[0:1, :]
    hidden_out[...] = dr1_ref[...] + rs * (dn - n1 * jnp.mean(dn * n1, axis=-1, keepdims=True))

    small_z[0] = gains_out[...]
    z_sums = [links.send(small_z.at[0], small_z.at[s], fsdp=z ^ s) for s in range(1, nz)]
    for copy in z_sums:
        links.arrived(copy)
    v = small_z[0]
    for s in range(1, nz):
        v += small_z[s]
    small_c[0] = v
    c_sums = [links.send(small_c.at[0], small_c.at[d], ctx=c ^ d) for d in range(1, nc)]
    for copy in c_sums:
        links.arrived(copy)
    v = small_c[0]
    for d in range(1, nc):
        v += small_c[d]
    gains_out[...] = v

    w_sum, o_sum = taken(0)
    wo_out[...] = o_sum
    wsum[...] = w_sum.astype(low)
    w_home = [links.send(wsum.at[:, c ^ d], wl.at[:, c], ctx=c ^ d) for d in range(1, nc)]
    w_own = links.move(wsum.at[:, c], wl.at[:, c])
    for copy in w_home:
        links.arrived(copy)
    links.left(w_own)
    for j in range(3):
        for k in range(nc):
            w_out[j, :, k * cols : (k + 1) * cols] = wl[j, k].astype(exact)
    for copy in up_sends:
        links.arrived(copy)
    links.close()


def run_back(cfg, x, dr1, datt, a1, w, raw, stat, rot, ob, wo, gains, fgain, gu, cosine, sine):
    nc, nz, tokens, width = cfg["nc"], cfg["nz"], cfg["tokens"], cfg["width"]
    cols, rows_w, length = cfg["cols"], cfg["rows_w"], cfg["length"]
    shape = jax.ShapeDtypeStruct
    any_, vmem = pl.BlockSpec(memory_space=pl.ANY), pl.BlockSpec(memory_space=pltpu.VMEM)
    outs = [
        (shape((tokens, width), exact), vmem),
        (shape((3, rows_w, width), exact), vmem),
        (shape((rows_w, width), exact), vmem),
        (shape((8, width), exact), vmem),
        (shape(gu.shape, low), any_),
        (shape((nc // 2, tokens, width), low), any_),
        (shape((nc // 2, tokens, width), low), any_),
        (shape((nz, 3, nc, rows_w, cols), low), any_),
        (shape((nz, rows_w, width), low), any_),
    ]
    scratch = [
        pltpu.VMEM((width, width), low),
        pltpu.VMEM((length, width), low),
        pltpu.VMEM((2, length, width // nc), low),
        pltpu.VMEM((3, width, cols), low),
        pltpu.VMEM((length, 2 * cols), exact),
        pltpu.VMEM((3, length, cols), low),
        pltpu.VMEM((length, cols), low),
        pltpu.VMEM((nc, tokens, cols), low),
        pltpu.VMEM((length, cols), exact),
        pltpu.VMEM((length, cols), exact),
        pltpu.VMEM((length, cols), exact),
        pltpu.VMEM((length, 128), exact),
        pltpu.VMEM((length, 128), exact),
        pltpu.VMEM((length, 128), exact),
        pltpu.VMEM((length, 128), exact),
        pltpu.VMEM((nc, 8, length), exact),
        pltpu.VMEM((8, length), exact),
        pltpu.VMEM((length, 3 * cols), low),
        pltpu.VMEM((3, nc, nz, rows_w, cols), low),
        pltpu.VMEM((nz, rows_w, width), low),
        pltpu.VMEM((8, cols), exact),
        pltpu.VMEM((3, nc, rows_w, cols), low),
        pltpu.VMEM((rows_w, width), low),
        pltpu.VMEM((3, nc, rows_w, cols), low),
        pltpu.VMEM((3, nc, rows_w, cols), low),
        pltpu.VMEM((tokens, width), low),
        pltpu.VMEM((tokens, width), low),
        pltpu.VMEM((nz, 8, width), exact),
        pltpu.VMEM((nc, 8, width), exact),
        pltpu.SemaphoreType.DMA((8 * nc + 8 * nz,)),
        pltpu.SemaphoreType.DMA((8 * nc + 8 * nz,)),
        pltpu.SemaphoreType.DMA((4 * nc + 8 * nz + 16,)),
    ]
    return pl.pallas_call(
        functools.partial(back_kernel, cfg),
        out_shape=[o[0] for o in outs],
        in_specs=[any_, vmem, any_, any_, any_, any_, vmem, any_, any_, any_, vmem, vmem, any_, vmem, vmem],
        out_specs=[o[1] for o in outs],
        scratch_shapes=scratch,
        compiler_params=pltpu.CompilerParams(
            collective_id=2, has_side_effects=True, vmem_limit_bytes=cfg["vmem"]
        ),
        name="back",
    )(x, dr1, datt, a1, w, raw, stat, rot, ob, wo, gains, fgain, gu, cosine, sine)


def tables(nc, tokens, head_size):
    half = tokens // 2
    local = np.arange(tokens)
    device = np.arange(nc)[:, None]
    position = np.where(
        local < half, device * half + local, (2 * nc - 1 - device) * half + local - half
    ).reshape(-1)
    freq = np.float32(10000.0) ** (-np.arange(head_size // 2, dtype=np.float32) * (2.0 / head_size))
    angle = position.astype(np.float32)[:, None] * freq.astype(np.float32)
    cosine = np.concatenate([np.cos(angle), np.cos(angle)], axis=1)
    sine = np.concatenate([-np.sin(angle), np.sin(angle)], axis=1)
    return jnp.asarray(cosine, exact), jnp.asarray(sine, exact)


def body(
    hidden_in,
    cotangent,
    routes,
    attn_gain,
    query_gain,
    key_gain,
    ffn_gain,
    w_query,
    w_key,
    w_value,
    w_out,
    w_router,
    w_gate,
    w_up,
    w_down,
):
    tokens = hidden_in.shape[1]
    width = hidden_in.shape[2]
    head_size = width // HEADS
    ctx_count = lax.axis_size("ctx")
    z_count = lax.axis_size("fsdp")
    both = ("ctx", "fsdp")
    top = routes.shape[2]
    exp_local = w_gate.shape[0]
    split = z_count // exp_local
    hidden = w_gate.shape[2]
    part = hidden // split
    experts = exp_local * ctx_count
    capacity = tokens * top * 4 // (3 * experts)
    cols = HEADS // ctx_count * head_size
    length = tokens * ctx_count
    c_index = lax.axis_index("ctx")
    z_index = lax.axis_index("fsdp")
    rows_w = w_query.shape[0]

    cfg = dict(
        nc=ctx_count,
        nz=z_count,
        tokens=tokens,
        width=width,
        cols=cols,
        rows_w=rows_w,
        length=length,
        cap=capacity,
        top=top,
        exp_local=exp_local,
        split=split,
        block=math.gcd(length, 256 if length <= 2048 else 128),
        chunk=math.gcd(length, 64),
        copies=(ctx_count - 1) * (8 + 2 * z_count) + (z_count - 1) * 12 + 2 * ctx_count + 8,
        part=part,
        vmem=62 * 2**20,
    )
    index = c_index * z_count + z_index
    per = 128 // rows_w
    gains = jnp.stack([attn_gain, query_gain, key_gain, ffn_gain]).astype(exact)
    gains = lax.dynamic_update_slice(
        jnp.zeros((8, 128), exact), gains, (0, jnp.mod(index, per) * rows_w)
    )
    router_tile = jnp.pad(w_router, ((0, 0), (0, 128 - experts)))
    route_tile = jnp.pad(routes[0].T, ((0, 8 - top), (0, 0)), constant_values=-1)

    def pieces_of(weight):
        rows = weight.shape[1]
        weight = weight.reshape(exp_local, rows, z_count, split, part // z_count)
        return weight.transpose(0, 3, 1, 2, 4).reshape(z_count, rows, part)

    cosine, sine = tables(ctx_count, tokens, head_size)
    (
        attn_all, w_full, raw, squares, rot, out_heads, wo_full, resid_one,
        router_full, gains, routes_all, gate_full, up_full, down_full, cot_rows, cot_near,
        input_rows, input_near,
    ) = front(
        cfg, hidden_in[0], w_query, w_key, w_value, w_out, gains, router_tile, route_tile,
        cotangent[0], pieces_of(w_gate), pieces_of(w_up),
        w_down.reshape(z_count, -1, width), cosine, sine,
    )
    gate_full = gate_full.reshape(-1, part)
    up_full = up_full.reshape(-1, part)
    down_full = down_full.reshape(-1, width)
    ffn_input = input_near[0]
    router_t = router_full.reshape(width, 128).T
    (
        resid_two, grad_one, attn_grad_low, logit_grad, ffn_gain_grad, down_land, gate_land,
        up_grad, *_,
    ) = run_experts(
        cfg, input_rows.reshape(-1, width), cot_rows.reshape(-1, width), router_t, routes_all,
        gate_full, up_full, down_full, input_near, cot_near, resid_one, gains,
    )
    out_hidden = resid_two[None]
    router_grad = lax.dot_general(
        ffn_input, logit_grad[:experts], (((0,), (1,)), ((), ())), preferred_element_type=exact
    )

    def whole_out(grad):
        grad = grad.reshape(exp_local, split, -1, z_count, part // z_count)
        return grad.transpose(0, 2, 3, 1, 4).reshape(exp_local, -1, hidden).astype(exact)

    grad_down = down_land.reshape(exp_local, -1, width).astype(exact)
    grad_gate = whole_out(gate_land)
    grad_hidden, w_grads, grad_out, gain_grads, up_land, *_ = run_back(
        cfg, hidden_in[0], grad_one, attn_grad_low, attn_all, w_full.reshape(3, width, cols), raw,
        squares, rot, out_heads, wo_full.reshape(width, width), gains, ffn_gain_grad,
        up_grad.reshape(z_count, -1, part), cosine, sine,
    )
    grad_up = whole_out(up_land)
    gain_grads = lax.dynamic_slice_in_dim(gain_grads, index * rows_w, rows_w, 1)
    sums = router_grad.reshape(ctx_count * z_count, rows_w * experts)
    sums = jnp.sum(exchange(sums, both), axis=0)
    return (
        out_hidden,
        grad_hidden[None],
        gain_grads[0],
        gain_grads[1],
        gain_grads[2],
        gain_grads[3],
        w_grads[0],
        w_grads[1],
        w_grads[2],
        grad_out,
        sums.reshape(rows_w, experts),
        grad_gate,
        grad_up,
        grad_down,
    )


def solution(mesh):
    in_specs = (
        P("fsdp", "ctx", None),
        P("fsdp", "ctx", None),
        P("fsdp", "ctx", None),
        P(("ctx", "fsdp")),
        P(("ctx", "fsdp")),
        P(("ctx", "fsdp")),
        P(("ctx", "fsdp")),
        P(("ctx", "fsdp"), None),
        P(("ctx", "fsdp"), None),
        P(("ctx", "fsdp"), None),
        P(("ctx", "fsdp"), None),
        P(("ctx", "fsdp"), None),
        P("ctx", "fsdp", None),
        P("ctx", "fsdp", None),
        P("ctx", "fsdp", None),
    )
    out_specs = (
        P("fsdp", "ctx", None),
        P("fsdp", "ctx", None),
        P(("ctx", "fsdp")),
        P(("ctx", "fsdp")),
        P(("ctx", "fsdp")),
        P(("ctx", "fsdp")),
        P(("ctx", "fsdp"), None),
        P(("ctx", "fsdp"), None),
        P(("ctx", "fsdp"), None),
        P(("ctx", "fsdp"), None),
        P(("ctx", "fsdp"), None),
        P("ctx", "fsdp", None),
        P("ctx", "fsdp", None),
        P("ctx", "fsdp", None),
    )
    return jax.shard_map(body, mesh=mesh, in_specs=in_specs, out_specs=out_specs, check_vma=False)
```

```python
import functools
import math

import jax
import jax.numpy as jnp
import numpy as np
from jax import lax
from jax.experimental import pallas as pl
from jax.experimental.pallas import tpu as pltpu
from jax.sharding import PartitionSpec as P

HEADS = 16


epsilon = 1e-05
neg_large = -1e30
low = jnp.bfloat16
exact = jnp.float32


def exchange(x, axis):
    return lax.all_to_all(x, axis, split_axis=0, concat_axis=0, tiled=True)


def bits_down(count):
    return [1 << i for i in range(count.bit_length() - 1)][::-1]


class Links:
    def __init__(self, sends, recvs, locals_):
        self.sends, self.recvs, self.locals = sends, recvs, locals_
        self.count = self.local_count = 0
        self.open = {}
        self.seen = {}

    def send(self, src, dst, **to):
        copy = pltpu.make_async_remote_copy(
            src_ref=src,
            dst_ref=dst,
            send_sem=self.sends.at[self.count],
            recv_sem=self.recvs.at[self.count],
            device_id=to,
            device_id_type=pl.DeviceIdType.MESH,
        )
        self.count += 1
        copy.start()
        self.open[id(copy)] = (copy, True)
        return copy

    def move(self, src, dst):
        copy = pltpu.make_async_copy(src, dst, self.locals.at[self.local_count])
        self.local_count += 1
        copy.start()
        self.open[id(copy)] = (copy, False)
        return copy

    def left(self, copy):
        if id(copy) in self.open:
            copy, remote = self.open.pop(id(copy))
            self.seen[id(copy), "left"] = copy
            copy.wait_send() if remote else copy.wait()

    def arrived(self, copy):
        if (id(copy), "in") not in self.seen:
            self.seen[id(copy), "in"] = copy
            copy.wait_recv()

    def close(self):
        for copy, _ in list(self.open.values()):
            self.left(copy)


def greet(c, z, nc, nz):
    barrier = pltpu.get_barrier_semaphore()
    for d in range(1, nc):
        pl.semaphore_signal(
            barrier, inc=1, device_id={"ctx": c ^ d}, device_id_type=pl.DeviceIdType.MESH
        )
    for s in range(1, nz):
        pl.semaphore_signal(
            barrier, inc=1, device_id={"fsdp": z ^ s}, device_id_type=pl.DeviceIdType.MESH
        )
    pl.semaphore_wait(barrier, nc - 1 + nz - 1)


def kdot(left, right, dims=((1,), (0,)), precision=None):
    return lax.dot_general(
        left, right, (dims, ((), ())), preferred_element_type=exact, precision=precision
    )


def slots_of(cfg, mask_rows, upper):
    rank = kdot(mask_rows.astype(low), upper)
    return jnp.where(mask_rows > 0, rank, 0.0)


def plane_ranks(cfg, routes, z):
    nc, tokens = cfg["nc"], cfg["tokens"]
    expert = lax.broadcasted_iota(jnp.int32, (nc, tokens), 0) * cfg["exp_local"] + z // cfg["split"]
    mask = jnp.zeros((nc, tokens), exact)
    for k in range(cfg["top"]):
        mask = jnp.where(routes[k : k + 1, :] == expert, 1.0, mask)
    upper = jnp.where(
        lax.broadcasted_iota(jnp.int32, (tokens, tokens), 0)
        <= lax.broadcasted_iota(jnp.int32, (tokens, tokens), 1),
        1.0,
        0.0,
    ).astype(low)
    return slots_of(cfg, mask, upper)


def fill_hot(cfg, ranks, hot_ref):
    cap, tokens = cfg["cap"], cfg["tokens"]
    number = lax.broadcasted_iota(jnp.int32, (cap, tokens), 0).astype(exact) + 1.0
    for k in range(cfg["nc"]):
        hit = jnp.where(ranks[k : k + 1, :] == number, 1.0, 0.0)
        hot_ref[k * cap : (k + 1) * cap, :] = hit.astype(low)


def front_kernel(
    cfg,
    x_ref, wq_ref, wk_ref, wv_ref, wo_ref, gt_ref, rt_ref, ro_ref, cot_ref, gp_ref, up_ref, dp_ref, cos_ref, sin_ref,
    a1_out, w_full, raw_out, stat_out, rot_out, ob_out, wo_full, r1_out, r_all, g_all, t_all,
    gate_full, up_full, down_full, cot_rows, cot_near, in_rows, in_near, staged,
    xbuf, wbuf, obw, gbuf, gfull, rbuf, tbuf, raw, stat, total, rq, rk, rot, opos, odev, orecv, r1, xrow, cbuf, abuf, hot, cs,
    sends, recvs, locals_,
):
    nc, nz, tokens, width = cfg["nc"], cfg["nz"], cfg["tokens"], cfg["width"]
    cols, rows_w, length, cap = cfg["cols"], cfg["rows_w"], cfg["length"], cfg["cap"]
    hs = 128
    heads = cols // hs
    half = tokens // 2
    block = cfg["block"]
    blocks = length // block
    c, z = lax.axis_index("ctx"), lax.axis_index("fsdp")
    links = Links(sends, recvs, locals_)
    ds = pl.ds
    same = [d for d in range(2, nc, 2)]
    steps = bits_down(nz)
    last = steps[-1]

    own_wo = links.move(wo_ref, obw.at[c, z])
    own_cot = links.move(cot_ref, cbuf.at[0])
    own_route = links.move(ro_ref, tbuf.at[c, z])
    own = []
    for j, ref in enumerate((wq_ref, wk_ref, wv_ref)):
        at = pl.multiple_of(c * cols, 128)
        own.append(links.move(ref.at[:, ds(at, cols)], wbuf.at[j, c, z]))
    own.append(links.move(gt_ref, gbuf.at[c, z]))
    own.append(links.move(rt_ref, rbuf.at[c, z]))
    own.append(links.move(x_ref, xbuf.at[ds(c * tokens, tokens)]))
    links.move(gp_ref.at[z], gate_full.at[z])
    links.move(up_ref.at[z], up_full.at[z])
    links.move(dp_ref.at[z], down_full.at[z])
    greet(c, z, nc, nz)

    slices = []
    for d in range(1, nc):
        peer = c ^ d
        at = pl.multiple_of(peer * cols, 128)
        for j, ref in enumerate((wq_ref, wk_ref, wv_ref)):
            slices.append(links.send(ref.at[:, ds(at, cols)], wbuf.at[j, c, z], ctx=peer))
    small_z = []
    for s in range(1, nz):
        for src, dst in ((gt_ref, gbuf), (rt_ref, rbuf), (ro_ref, tbuf)):
            small_z.append(links.send(src, dst.at[c, z], fsdp=z ^ s))
    wo_near, cot_copies, w_near = {}, {}, {}

    def wo_send(s, bit):
        place = obw.at[c, z ^ s]
        wo_near[s | bit] = links.send(place, place, fsdp=z ^ bit)

    def cot_send(s, bit):
        cot_copies[s | bit] = links.send(cbuf.at[s], cbuf.at[s | bit], fsdp=z ^ bit)

    def w_send(s, bit):
        place = wbuf.at[:, :, z ^ s]
        w_near[s | bit] = links.send(place, place, fsdp=z ^ bit)

    def forward(waits, send):
        for at, bit in enumerate(steps):
            held = [0]
            for earlier in steps[:at]:
                held += [s | earlier for s in held]
            for s in held[1:]:
                links.arrived(waits[s])
                send(s, bit)

    def all_in(waits):
        for s in range(1, nz):
            links.arrived(waits[s])

    links.left(own_wo)
    links.left(own_route)
    for bit in steps:
        wo_send(0, bit)
    x_at = xbuf.at[ds(c * tokens, tokens)]
    x_same = {d: links.send(x_ref, x_at, ctx=c ^ d) for d in same}
    x_side = [links.send(x_ref, x_at, ctx=c ^ 1)]
    rows_sent = []
    turn_of = [0]

    def dispatch(s, near, landing):
        number = turn_of[0]
        turn_of[0] += 1
        fill_hot(cfg, plane_ranks(cfg, tbuf[c, z ^ s], z), hot)
        cs[...] = kdot(hot[...], near[s]).astype(low)
        off = links.move(cs, staged.at[number])
        links.left(off)
        for d in range(1, nc):
            src = staged.at[number, ds((c ^ d) * cap, cap)]
            rows_sent.append(links.send(src, landing.at[s, c], ctx=c ^ d))
        links.move(cs.at[ds(c * cap, cap)], landing.at[s, c])

    def settle():
        for copy, remote in list(links.open.values()):
            if not remote:
                links.left(copy)

    for copy in own:
        links.left(copy)

    for copy in slices:
        links.arrived(copy)
    for bit in steps:
        w_send(0, bit)
    for copy in small_z:
        links.arrived(copy)
    small_c = []
    for d in range(1, nc):
        for buf in (gbuf, rbuf, tbuf):
            small_c.append(links.send(buf.at[c], buf.at[c], ctx=c ^ d))
    forward(wo_near, wo_send)
    for d in same:
        links.arrived(x_same[d])
        place = xbuf.at[ds((c ^ d) * tokens, tokens)]
        x_side.append(links.send(place, place, ctx=c ^ 1))
    links.left(own_cot)
    dispatch(0, cbuf, cot_rows)
    for copy in small_c:
        links.arrived(copy)
    per = 128 // rows_w
    groups = nz // per
    for k in range(nc):
        for g in range(groups):
            tile = gbuf[k, g * per]
            for p in range(1, per):
                tile = tile + gbuf[k, g * per + p]
            at = (k * groups + g) * 128
            gfull[:, at : at + 128] = tile
    all_in(wo_near)
    wo_same = {d: links.send(obw.at[c], obw.at[c], ctx=c ^ d) for d in same}
    wo_side = [links.send(obw.at[c], obw.at[c], ctx=c ^ 1)]
    for copy in x_side:
        links.arrived(copy)
    for copy in list(x_same.values()) + x_side:
        links.left(copy)

    chunk = cfg["chunk"]

    def norm_rows(i, _):
        at = pl.multiple_of(i * chunk, chunk)
        v = xbuf[ds(at, chunk), :].astype(exact)
        v = v * lax.rsqrt(jnp.mean(v * v, axis=-1, keepdims=True) + epsilon) * gfull[0:1, :]
        xbuf[ds(at, chunk), :] = v.astype(low)
        return 0

    forward(w_near, w_send)
    for bit in steps:
        cot_send(0, bit)
    lax.fori_loop(0, length // chunk, norm_rows, 0)
    links.move(xbuf, a1_out)
    all_in(w_near)
    experts_in = []
    for s in range(1, nz):
        experts_in.append(links.send(gp_ref.at[z ^ s], gate_full.at[z], fsdp=z ^ s))
    links.move(wbuf, w_full)

    one_row = lax.broadcasted_iota(jnp.int32, (8, cols), 0)
    pick_q = jnp.where(one_row == 0, 1.0, 0.0)
    pick_k = jnp.where(one_row == 1, 1.0, 0.0)
    best = lax.Precision.HIGHEST

    def project(i, _):
        at = pl.multiple_of(i * block, block)
        rows = xbuf[ds(at, block), :]
        sums = jnp.zeros((8, block), exact)
        for j in range(3):
            weight = wbuf[j].reshape(width, cols)
            v = kdot(rows, weight)
            raw[ds(at, block), j * cols : (j + 1) * cols] = v
            if j < 2:
                sums += kdot(pick_k if j else pick_q, v * v, ((1,), (1,)), best)
        stat[c, :, ds(at, block)] = sums
        return 0

    lax.fori_loop(0, blocks, project, 0)
    stats = [links.send(stat.at[c], stat.at[c], ctx=c ^ d) for d in range(1, nc)]
    links.move(raw, raw_out)
    for d in same:
        links.arrived(wo_same[d])
        place_at = obw.at[c ^ d]
        wo_side.append(links.send(place_at, place_at, ctx=c ^ 1))
    for copy in stats:
        links.arrived(copy)
    summed = stat[0]
    for k in range(1, nc):
        summed += stat[k]
    total[...] = summed
    row8 = lax.broadcasted_iota(jnp.int32, (8, hs), 0)

    def columns(i, _):
        at = pl.multiple_of(i * block, block)
        part = total[:, ds(at, block)]
        for row, dst in ((0, rq), (1, rk)):
            sel = jnp.where(row8 == row, 1.0, 0.0)
            ms = kdot(part, sel, ((0,), (0,)), best)
            dst[ds(at, block), :] = lax.rsqrt(ms / width + epsilon)
        return 0

    lax.fori_loop(0, blocks, columns, 0)
    links.move(total, stat_out)
    forward(cot_copies, cot_send)
    for s in range(1, nz):
        experts_in.append(links.send(up_ref.at[z ^ s], up_full.at[z], fsdp=z ^ s))

    def turn(i, _):
        d, side = i // 2, i % 2
        at = pl.multiple_of(d * tokens + side * half, half)
        to = pl.multiple_of(jnp.where(side == 0, d, 2 * nc - 1 - d) * half, half)
        cosine, sine = cos_ref[ds(at, half), :], sin_ref[ds(at, half), :]
        for h in range(heads):
            for j, scale in ((0, rq), (1, rk)):
                lane = j * cols + h * hs
                gain = gfull[1 + j : 2 + j, ds(pl.multiple_of(c * cols + h * hs, hs), hs)]
                v = raw[ds(at, half), lane : lane + hs] * scale[ds(at, half), :] * gain
                v = v * cosine + pltpu.roll(v, hs // 2, 1) * sine
                rot[j, ds(to, half), h * hs : (h + 1) * hs] = v.astype(low)
        rot[2, ds(to, half), :] = raw[ds(at, half), 2 * cols : 3 * cols].astype(low)
        return 0

    lax.fori_loop(0, 2 * nc, turn, 0)
    links.move(rot, rot_out)
    settle()
    for bit in steps:
        links.arrived(cot_copies[bit])
        dispatch(bit, cbuf, cot_rows)
        settle()

    scale = hs ** -0.5
    for h in range(heads):
        lanes = slice(h * hs, (h + 1) * hs)
        for i in range(blocks):
            count = (i + 1) * block
            q = rot[0, i * block : count, lanes]
            s = kdot(q, rot[1, :count, lanes], ((1,), (1,))) * scale
            row = lax.broadcasted_iota(jnp.int32, (block, count), 0) + i * block
            col = lax.broadcasted_iota(jnp.int32, (block, count), 1)
            s = jnp.where(col <= row, s, neg_large)
            p = jnp.exp(s - jnp.max(s, axis=-1, keepdims=True))
            p = p * (1.0 / jnp.sum(p, axis=-1, keepdims=True))
            opos[i * block : count, lanes] = kdot(p.astype(low), rot[2, :count, lanes]).astype(low)

    def place(i, _):
        d, side = i // 2, i % 2
        to = pl.multiple_of(d * tokens + side * half, half)
        at = pl.multiple_of(jnp.where(side == 0, d, 2 * nc - 1 - d) * half, half)
        odev[ds(to, half), :] = opos[ds(at, half), :]
        return 0

    lax.fori_loop(0, 2 * nc, place, 0)
    mixed = []
    for d in range(1, nc):
        src = odev.at[ds((c ^ d) * tokens, tokens)]
        mixed.append(links.send(src, orecv.at[c], ctx=c ^ d))
    own_mixed = links.move(odev.at[ds(c * tokens, tokens)], orecv.at[c])
    links.move(odev, ob_out)
    x_in = links.move(x_ref, xrow)
    for copy in wo_side:
        links.arrived(copy)
    links.move(obw, wo_full)
    r1[...] = jnp.zeros_like(r1)
    for copy in mixed:
        links.arrived(copy)
    links.left(own_mixed)

    def mix(k, _):
        r1[...] += kdot(orecv[k], obw[k].reshape(cols, width))
        return 0

    lax.fori_loop(0, nc, mix, 0)
    links.left(x_in)
    v = r1[...] + xrow[...].astype(exact)
    r1[...] = v
    n2 = v * lax.rsqrt(jnp.mean(v * v, axis=-1, keepdims=True) + epsilon)
    abuf[0] = (n2 * gfull[3:4, :]).astype(low)
    in_copies = {}

    def in_send(s, bit):
        in_copies[s | bit] = links.send(abuf.at[s], abuf.at[s | bit], fsdp=z ^ bit)

    for bit in steps:
        in_send(0, bit)
    settle()
    dispatch(0, abuf, in_rows)
    links.move(r1, r1_out)
    links.move(rbuf, r_all)
    links.move(gfull, g_all)
    links.move(tbuf, t_all)
    all_in(cot_copies)
    links.move(cbuf, cot_near)
    for s in range(1, nz):
        if s & (s - 1):
            settle()
            dispatch(s, cbuf, cot_rows)
    forward(in_copies, in_send)
    for s in range(1, nz - 1):
        experts_in.append(links.send(dp_ref.at[z ^ s], down_full.at[z], fsdp=z ^ s))
    for s in list(steps) + [s for s in range(1, nz) if s & (s - 1)]:
        links.arrived(in_copies[s])
        settle()
        dispatch(s, abuf, in_rows)
    links.move(abuf, in_near)
    for copy in experts_in + rows_sent:
        links.arrived(copy)
    links.close()


def front(cfg, x, w_query, w_key, w_value, w_out, gains, router, routes, cot, gate_pieces, up_pieces, down_pieces, cosine, sine):
    nc, nz, tokens, width = cfg["nc"], cfg["nz"], cfg["tokens"], cfg["width"]
    cols, rows_w, length, cap = cfg["cols"], cfg["rows_w"], cfg["length"], cfg["cap"]
    rows, part = gate_pieces.shape[1:]
    shape = jax.ShapeDtypeStruct
    any_, vmem = pl.BlockSpec(memory_space=pl.ANY), pl.BlockSpec(memory_space=pltpu.VMEM)
    top_rows = routes.shape[0]
    outs = [
        shape((length, width), low),
        shape((3, nc, nz, rows_w, cols), low),
        shape((length, 3 * cols), exact),
        shape((8, length), exact),
        shape((3, length, cols), low),
        shape((length, cols), low),
        shape((nc, nz, rows_w, width), low),
        shape((tokens, width), exact),
        shape((nc, nz, rows_w, 128), low),
        shape((8, width), exact),
        shape((nc, nz, top_rows, tokens), jnp.int32),
        shape((nz, rows, part), low),
        shape((nz, rows, part), low),
        shape(down_pieces.shape, low),
        shape((nz, nc, cap, width), low),
        shape((nz, tokens, width), low),
        shape((nz, nc, cap, width), low),
        shape((nz, tokens, width), low),
        shape((2 * nz, nc * cap, width), low),
    ]
    scratch = [
        pltpu.VMEM((length, width), low),
        pltpu.VMEM((3, nc, nz, rows_w, cols), low),
        pltpu.VMEM((nc, nz, rows_w, width), low),
        pltpu.VMEM((nc, nz, 8, 128), exact),
        pltpu.VMEM((8, width), exact),
        pltpu.VMEM((nc, nz, rows_w, 128), low),
        pltpu.VMEM((nc, nz, top_rows, tokens), jnp.int32),
        pltpu.VMEM((length, 3 * cols), exact),
        pltpu.VMEM((nc, 8, length), exact),
        pltpu.VMEM((8, length), exact),
        pltpu.VMEM((length, 128), exact),
        pltpu.VMEM((length, 128), exact),
        pltpu.VMEM((3, length, cols), low),
        pltpu.VMEM((length, cols), low),
        pltpu.VMEM((length, cols), low),
        pltpu.VMEM((nc, tokens, cols), low),
        pltpu.VMEM((tokens, width), exact),
        pltpu.VMEM((tokens, width), low),
        pltpu.VMEM((nz, tokens, width), low),
        pltpu.VMEM((nz, tokens, width), low),
        pltpu.VMEM((nc * cap, tokens), low),
        pltpu.VMEM((nc * cap, width), low),
        pltpu.SemaphoreType.DMA((cfg["copies"],)),
        pltpu.SemaphoreType.DMA((cfg["copies"],)),
        pltpu.SemaphoreType.DMA((32 + 4 * cfg["nz"],)),
    ]
    return pl.pallas_call(
        functools.partial(front_kernel, cfg),
        out_shape=outs,
        in_specs=[any_] * 12 + [vmem] * 2,
        out_specs=[any_] * len(outs),
        scratch_shapes=scratch,
        compiler_params=pltpu.CompilerParams(
            collective_id=0, has_side_effects=True, vmem_limit_bytes=cfg["vmem"]
        ),
        name="front",
    )(x, w_query, w_key, w_value, w_out, gains, router, routes, cot, gate_pieces, up_pieces, down_pieces, cosine, sine)


def expert_kernel(
    cfg,
    rows_ref, cotr_ref, rt_ref, tb_ref, wg_ref, wu_ref, wd_ref, dp_ref, near_ref, cotn_ref, r1_ref, gain_ref,
    hidden_out, dr1_out, datt_out, dlog_out, fgain_out, gd_land, gg_land, gu_out,
    back, in_back, out_land, in_land, ebh, rbh,
    wg, wu, wd, rows, cotb, gin, gdb, du, eb, rb, tile, ranks, hot, metab, gate_rows, dgs, dgl,
    sends, recvs, locals_,
):
    nc, nz, tokens, width = cfg["nc"], cfg["nz"], cfg["tokens"], cfg["width"]
    cap, part, split, exp_local = cfg["cap"], cfg["part"], cfg["split"], cfg["exp_local"]
    ch = nc * cap
    total = nz * ch
    c, z = lax.axis_index("ctx"), lax.axis_index("fsdp")
    links = Links(sends, recvs, locals_)
    ds = pl.ds
    expert = c * exp_local + z // split
    best = lax.Precision.HIGHEST
    peers = list(range(1, nc))

    loads = [links.move(wg_ref, wg), links.move(wu_ref, wu), links.move(rows_ref, rows)]
    rows_d = part // nz

    def down_place(owner):
        return wd.at[ds(pl.multiple_of(owner * rows_d, rows_d), rows_d)]

    down_here = [links.move(wd_ref.at[z ^ s], down_place(z ^ s)) for s in range(nz - 1)]
    cot_base = links.local_count
    links.local_count += nz
    send_base = links.count
    links.count += 2 * nz * (nc - 1)
    keep_base = links.local_count
    links.local_count += 2 * nz
    off_base = links.local_count
    links.local_count += 2 * nz

    def cot_load(s, slot):
        return pltpu.make_async_copy(
            cotr_ref.at[ds(s * ch, ch)], cotb.at[slot], locals_.at[cot_base + s]
        )

    def chunk_copies(s, which):
        buf, landing = ((ebh, back), (rbh, in_back))[which]
        base = send_base + which * nz * (nc - 1) + s * (nc - 1)
        out = []
        for d in peers:
            out.append(
                pltpu.make_async_remote_copy(
                    src_ref=buf.at[s, ds((c ^ d) * cap, cap)],
                    dst_ref=landing.at[s, c],
                    send_sem=sends.at[base + d - 1],
                    recv_sem=recvs.at[base + d - 1],
                    device_id={"ctx": c ^ d},
                    device_id_type=pl.DeviceIdType.MESH,
                )
            )
        return out

    def keep_copy(s, which):
        landing = (back, in_back)[which]
        return pltpu.make_async_copy(
            (ebh, rbh)[which].at[s, ds(c * cap, cap)],
            landing.at[s, c],
            locals_.at[keep_base + which * nz + s],
        )

    def off_copy(s, which):
        return pltpu.make_async_copy(
            (eb, rb)[which], (ebh, rbh)[which].at[s], locals_.at[off_base + which * nz + s]
        )

    cot_load(nz - 1, 0).start()
    greet(c, z, nc, nz)
    far = z ^ (nz - 1)
    down_in = [links.send(dp_ref.at[far], down_place(z), fsdp=far)]
    for copy in loads:
        links.left(copy)

    expert_rows = lax.broadcasted_iota(jnp.int32, (128, tokens), 0)
    upper = jnp.where(
        lax.broadcasted_iota(jnp.int32, (tokens, tokens), 0)
        <= lax.broadcasted_iota(jnp.int32, (tokens, tokens), 1),
        1.0,
        0.0,
    ).astype(low)

    def routed(block):
        chosen = jnp.zeros((128, tokens), exact)
        for k in range(cfg["top"]):
            chosen = jnp.where(block[k : k + 1, :] == expert_rows, 1.0, chosen)
        return chosen

    sub = min(256, ch)
    lane = lax.broadcasted_iota(jnp.int32, (sub, 128), 1)

    def gate_of(block, picked):
        logits = kdot(block, rt_ref[...], ((1,), (1,)))
        logits = jnp.where(picked > 0.5, logits, neg_large)
        weight = jnp.exp(logits - jnp.max(logits, axis=-1, keepdims=True))
        gate = jnp.sum(jnp.where(lane == expert, weight, 0.0), axis=-1, keepdims=True)
        return gate / jnp.sum(weight, axis=-1, keepdims=True)

    def first_work(s, _):
        for k in range(nc):
            block = tb_ref[k, z ^ s]
            found = jnp.where(block == expert, 1.0, 0.0)
            ranks[k : k + 1, :] = jnp.max(found, axis=0, keepdims=True)
        ranks[...] = slots_of(cfg, ranks[...], upper)
        fill_hot(cfg, ranks[...], hot)
        for k in range(nc):
            chosen = routed(tb_ref[k, z ^ s]).astype(low)
            metab[k * cap : (k + 1) * cap, :] = kdot(
                hot[k * cap : (k + 1) * cap, :], chosen, ((1,), (1,))
            )

        def some_rows(j, _):
            here = pl.multiple_of(j * sub, sub)
            at = pl.multiple_of(s * ch + j * sub, sub)
            span, to = ds(here, sub), ds(at, sub)
            block = rows[to, :]
            gate = gate_of(block, metab[span, :])
            g = kdot(block, wg[...])
            u = kdot(block, wu[...])
            inner = (g * (1.0 / (1.0 + jnp.exp(-g))) * u).astype(low)
            gin[to, :] = (inner.astype(exact) * gate).astype(low)
            gate_rows[to, :] = jnp.broadcast_to(gate, (sub, 128))
            return 0

        lax.fori_loop(0, ch // sub, some_rows, 0)
        return 0

    lax.fori_loop(0, nz, first_work, 0)

    step = 256 if nz * ch <= 2048 else 128
    tile_base = links.local_count
    links.local_count += width // step

    def tile_load(k):
        return pltpu.make_async_copy(
            cotr_ref.at[:, ds(k * step, step)], tile.at[lax.rem(k, 2)], locals_.at[tile_base + k]
        )

    tile_load(0).start()

    def down_tile(k, _):
        @pl.when(k + 1 < width // step)
        def _():
            tile_load(k + 1).start()

        tile_load(k).wait()
        at = pl.multiple_of(k * step, step)
        gdb[:, ds(at, step)] = kdot(gin[...], tile[lax.rem(k, 2)], ((0,), (0,))).astype(low)
        return 0

    lax.fori_loop(0, width // step, down_tile, 0)
    grads_out = []
    for s in range(1, nz):
        src = gdb.at[ds(pl.multiple_of((z ^ s) * rows_d, rows_d), rows_d)]
        grads_out.append(links.send(src, gd_land.at[z], fsdp=z ^ s))
    links.move(gdb.at[ds(pl.multiple_of(z * rows_d, rows_d), rows_d)], gd_land.at[z])
    for copy in down_here:
        links.left(copy)
    for copy in down_in:
        links.arrived(copy)

    def work(i, _):
        s = nz - 1 - i
        slot = lax.rem(i, 2)

        @pl.when(i + 1 < nz)
        def _():
            cot_load(s - 1, 1 - slot).start()

        cot_load(s, slot).wait()

        def some_rows(j, _):
            here = pl.multiple_of(j * sub, sub)
            at = pl.multiple_of(s * ch + j * sub, sub)
            span, to = ds(here, sub), ds(at, sub)
            block = rows[to, :]
            gate = gate_rows[to, 0:1]
            g = kdot(block, wg[...])
            u = kdot(block, wu[...])
            sg = 1.0 / (1.0 + jnp.exp(-g))
            act = g * sg
            inner = (act * u).astype(low)
            eb[span, :] = kdot(inner, wd[...]).astype(low)
            dinner = kdot(cotb[slot, span, :], wd[...], ((1,), (1,))) * gate
            dg_low = (dinner * u * sg * (1.0 + g * (1.0 - sg))).astype(low)
            du_low = (dinner * act).astype(low)
            gin[to, :] = dg_low
            du[to, :] = du_low
            rb[span, :] = (
                kdot(dg_low, wg[...], ((1,), (1,))) + kdot(du_low, wu[...], ((1,), (1,)))
            ).astype(low)
            return 0

        lax.fori_loop(0, ch // sub, some_rows, 0)
        for which in (0, 1):
            off_copy(s, which).start()
        for which in (0, 1):
            off_copy(s, which).wait()
            for copy in chunk_copies(s, which):
                copy.start()
            keep_copy(s, which).start()
        return 0

    lax.fori_loop(0, nz, work, 0)

    rows_g = width // nz

    def rows_tile(left, dst):
        def one(k, _):
            at = pl.multiple_of(k * step, step)
            dst[ds(at, step), :] = kdot(rows[:, ds(at, step)], left[...], ((0,), (0,))).astype(low)
            return 0

        lax.fori_loop(0, width // step, one, 0)

    rows_tile(gin, wg)
    for s in range(1, nz):
        src = wg.at[ds(pl.multiple_of((z ^ s) * rows_g, rows_g), rows_g)]
        grads_out.append(links.send(src, gg_land.at[z], fsdp=z ^ s))
    links.move(wg.at[ds(pl.multiple_of(z * rows_g, rows_g), rows_g)], gg_land.at[z])
    rows_tile(du, wu)
    links.move(wu, gu_out)

    spare = {}
    at = 0
    for name, count in (
        ("back", ch), ("in_back", ch), ("near", tokens), ("cot", tokens), ("out0", tokens),
        ("in0", tokens),
    ):
        spare[name] = rows.at[at : at + count]
        at += count
    stage = {0: (spare["out0"], spare["in0"]), 1: (cotb.at[0, 0:tokens], cotb.at[1, 0:tokens])}
    extra = (cotb.at[0, tokens : 2 * tokens], cotb.at[1, tokens : 2 * tokens])
    pick_rows = lax.broadcasted_iota(jnp.int32, (nc, 128), 0)
    pick_lane = lax.broadcasted_iota(jnp.int32, (nc, 128), 1)
    homeward = {}
    gate_home = {}
    busy = {0: [], 1: []}
    gates_own = None
    sums = None
    for s in range(nz - 1, -1, -1):
        for which in (0, 1):
            out = chunk_copies(s, which)
            for copy in out:
                copy.wait_recv()
            keep_copy(s, which).wait()
        fetch = []
        for k in range(nc):
            fetch.append(links.move(back.at[s, k], rows.at[k * cap : (k + 1) * cap]))
            fetch.append(links.move(in_back.at[s, k], rows.at[ch + k * cap : ch + (k + 1) * cap]))
        fetch.append(links.move(near_ref.at[s], spare["near"]))
        fetch.append(links.move(cotn_ref.at[s], spare["cot"]))
        block = tb_ref[c, z ^ s]
        fill_hot(cfg, plane_ranks(cfg, block, z), hot)
        chosen = routed(block)
        for copy in fetch:
            links.left(copy)
        logits = kdot(rt_ref[...], spare["near"][...], ((1,), (1,)))
        logits = jnp.where(chosen > 0.5, logits, neg_large)
        weight = jnp.exp(logits - jnp.max(logits, axis=0, keepdims=True))
        gates = weight / jnp.sum(weight, axis=0, keepdims=True)
        sel = jnp.where(pick_lane == pick_rows * exp_local + z // split, 1.0, 0.0)
        plane = kdot(sel, gates, ((1,), (0,)), best)
        slot_grad = kdot(spare["back"][...], spare["cot"][...], ((1,), (1,)))
        for k in range(nc):
            span = slice(k * cap, (k + 1) * cap)
            hit = hot[span, :].astype(exact)
            dgs[s, k : k + 1, :] = jnp.sum(hit * slot_grad[span, :], axis=0, keepdims=True)
        in_part = kdot(hot[...], spare["in_back"][...], ((0,), (0,)))
        for k in range(nc):
            span = slice(k * cap, (k + 1) * cap)
            hot[span, :] = (hot[span, :].astype(exact) * plane[k : k + 1, :]).astype(low)
        out_part = kdot(hot[...], spare["back"][...], ((0,), (0,)))
        lowest = s & -s
        bit = 1
        while bit < nz and (s == 0 or bit < lowest):
            for copy in homeward[s | bit]:
                links.arrived(copy)
            got = [links.move(out_land.at[s | bit], extra[0]), links.move(in_land.at[s | bit], extra[1])]
            for copy in got:
                links.left(copy)
            out_part += extra[0][...].astype(exact)
            in_part += extra[1][...].astype(exact)
            bit *= 2
        if s:
            slot = s % 2
            for copy in busy[slot]:
                links.left(copy)
            stage[slot][0][...] = out_part.astype(low)
            stage[slot][1][...] = in_part.astype(low)
            homeward[s] = [
                links.send(stage[slot][0], out_land.at[s], fsdp=z ^ lowest),
                links.send(stage[slot][1], in_land.at[s], fsdp=z ^ lowest),
            ]
            busy[slot] = homeward[s]
            gate_home[s] = links.send(dgs.at[s], dgl.at[s], fsdp=z ^ s)
        else:
            gates_own = gates
            sums = (out_part, in_part)

    dgate = jnp.zeros((128, tokens), exact)
    for s in range(nz):
        if s:
            links.arrived(gate_home[s])
        here = dgl[s] if s else dgs[0]
        sel = jnp.where(pick_lane == pick_rows * exp_local + (z ^ s) // split, 1.0, 0.0)
        dgate += kdot(sel, here, ((0,), (0,)), best)
    dchosen = gates_own * (dgate - jnp.sum(gates_own * dgate, axis=0, keepdims=True))
    dlog = dchosen.astype(low)
    hot[0:128, :] = dlog
    dlog_copy = links.move(hot.at[0:128], dlog_out)
    out_part, in_part = sums
    da2 = in_part + kdot(dlog, rt_ref[...], ((0,), (0,)))
    r1 = r1_ref[...]
    for copies in busy.values():
        for copy in copies:
            links.left(copy)
    stage[0][0][...] = (r1 + out_part).astype(low)
    links.move(stage[0][0], hidden_out)
    rs = lax.rsqrt(jnp.mean(r1 * r1, axis=-1, keepdims=True) + epsilon)
    n2 = r1 * rs
    dm = da2 * gain_ref[3:4, :]
    fgain_out[...] = jnp.broadcast_to(jnp.sum(da2 * n2, axis=0, keepdims=True), (8, width))
    inner_mean = jnp.mean(dm * n2, axis=-1, keepdims=True)
    dr1 = spare["cot"][...].astype(exact) + rs * (dm - n2 * inner_mean)
    dr1_out[...] = dr1
    datt_out[...] = dr1.astype(low)
    for s in range(nz):
        for which in (0, 1):
            out = chunk_copies(s, which)
            for copy in out:
                copy.wait_send()
    for copy in grads_out:
        links.arrived(copy)
    links.close()


def run_experts(cfg, rows, cot_rows, router_t, routes, wg, wu, wd, down_pieces, near, cot_near, r1, gains):
    nc, nz, tokens, width = cfg["nc"], cfg["nz"], cfg["tokens"], cfg["width"]
    cap, part = cfg["cap"], cfg["part"]
    ch = nc * cap
    shape = jax.ShapeDtypeStruct
    any_, vmem = pl.BlockSpec(memory_space=pl.ANY), pl.BlockSpec(memory_space=pltpu.VMEM)
    outs = [
        (shape((tokens, width), low), any_),
        (shape((tokens, width), exact), vmem),
        (shape((tokens, width), low), vmem),
        (shape((128, tokens), low), any_),
        (shape((8, width), exact), vmem),
        (shape((nz, part // nz, width), low), any_),
        (shape((nz, width // nz, part), low), any_),
        (shape((width, part), low), any_),
        (shape((nz, nc, cap, width), low), any_),
        (shape((nz, nc, cap, width), low), any_),
        (shape((nz, tokens, width), low), any_),
        (shape((nz, tokens, width), low), any_),
        (shape((nz, ch, width), low), any_),
        (shape((nz, ch, width), low), any_),
    ]
    step = 256 if nz * ch <= 2048 else 128
    scratch = [
        pltpu.VMEM((width, part), low),
        pltpu.VMEM((width, part), low),
        pltpu.VMEM((part, width), low),
        pltpu.VMEM((nz * ch, width), low),
        pltpu.VMEM((2, ch, width), low),
        pltpu.VMEM((nz * ch, part), low),
        pltpu.VMEM((part, width), low),
        pltpu.VMEM((nz * ch, part), low),
        pltpu.VMEM((ch, width), low),
        pltpu.VMEM((ch, width), low),
        pltpu.VMEM((2, nz * ch, step), low),
        pltpu.VMEM((nc, tokens), exact),
        pltpu.VMEM((ch, tokens), low),
        pltpu.VMEM((ch, 128), exact),
        pltpu.VMEM((nz * ch, 128), exact),
        pltpu.VMEM((nz, nc, tokens), exact),
        pltpu.VMEM((nz, nc, tokens), exact),
        pltpu.SemaphoreType.DMA((2 * nz * nc + 8 * nz,)),
        pltpu.SemaphoreType.DMA((2 * nz * nc + 8 * nz,)),
        pltpu.SemaphoreType.DMA((2 * nz * nc + 16 * nz + width // step + 16,)),
    ]
    return pl.pallas_call(
        functools.partial(expert_kernel, cfg),
        out_shape=[o[0] for o in outs],
        in_specs=[any_, any_, vmem, vmem, any_, any_, any_, any_, any_, any_, vmem, vmem],
        out_specs=[o[1] for o in outs],
        scratch_shapes=scratch,
        compiler_params=pltpu.CompilerParams(
            collective_id=1, has_side_effects=True, vmem_limit_bytes=cfg["vmem"]
        ),
        name="experts",
    )(rows, cot_rows, router_t, routes, wg, wu, wd, down_pieces, near, cot_near, r1, gains)


def back_kernel(
    cfg,
    x_ref, dr1_ref, datt_ref, a1_ref, w_ref, raw_ref, stat_ref, rot_ref, ob_ref, wo_ref, gain_ref, fgain_ref,
    gu_ref, cos_ref, sin_ref,
    hidden_out, w_out, wo_out, gains_out, gu_land, pair_land, chip_land, wz_land, oz_land,
    wo, datt, a1, w, raw, rot, ob, dland, aq, ak, av, rq, rk, cq, ck, stat, total, dqkv, gw, go, gsum,
    wtemp, otemp, wsum, wl, xrow, xtemp, small_z, small_c,
    sends, recvs, locals_,
):
    nc, nz, tokens, width = cfg["nc"], cfg["nz"], cfg["tokens"], cfg["width"]
    cols, rows_w, length = cfg["cols"], cfg["rows_w"], cfg["length"]
    hs = 128
    heads = cols // hs
    half = tokens // 2
    block = cfg["block"]
    blocks = length // block
    c, z = lax.axis_index("ctx"), lax.axis_index("fsdp")
    links = Links(sends, recvs, locals_)
    ds = pl.ds
    best = lax.Precision.HIGHEST
    same = [d for d in range(2, nc, 2)]
    own_rows = ds(pl.multiple_of(c * tokens, tokens), tokens)

    wo_in = links.move(wo_ref, wo)
    datt_in = links.move(datt_ref, datt.at[own_rows])
    first = [links.move(rot_ref, rot), links.move(raw_ref.at[:, 0 : 2 * cols], raw), links.move(ob_ref, ob)]
    later = [links.move(w_ref, w), links.move(x_ref, xrow)]
    up_own = links.move(gu_ref.at[z], gu_land.at[z])
    greet(c, z, nc, nz)
    up_sends = [links.send(gu_ref.at[z ^ s], gu_land.at[z], fsdp=z ^ s) for s in range(1, nz)]
    links.left(datt_in)
    links.left(wo_in)

    heads_sent = []
    for d in range(1, nc):
        at = pl.multiple_of((c ^ d) * cols, cols)
        spot = dqkv.at[d * tokens : (d + 1) * tokens, 0:cols]
        spot[...] = kdot(datt[own_rows, :], wo[ds(at, cols), :], ((1,), (1,))).astype(low)
        heads_sent.append(links.send(spot, dland.at[c], ctx=c ^ d))
    at = pl.multiple_of(c * cols, cols)
    dland[c] = kdot(datt[own_rows, :], wo[ds(at, cols), :], ((1,), (1,))).astype(low)
    rows_same = {d: links.send(datt.at[own_rows], datt.at[own_rows], ctx=c ^ d) for d in same}
    rows_side = [links.send(datt.at[own_rows], datt.at[own_rows], ctx=c ^ 1)]
    for copy in first:
        links.left(copy)

    row8 = lax.broadcasted_iota(jnp.int32, (8, hs), 0)

    def columns(src, one, two, finish):
        def step(i, _):
            at = pl.multiple_of(i * block, block)
            part = src[:, ds(at, block)]
            for row, dst in ((0, one), (1, two)):
                sel = jnp.where(row8 == row, 1.0, 0.0)
                dst[ds(at, block), :] = finish(kdot(part, sel, ((0,), (0,)), best) / width)
            return 0

        lax.fori_loop(0, blocks, step, 0)

    columns(stat_ref, rq, rk, lambda v: lax.rsqrt(v + epsilon))
    ak[...] = jnp.zeros_like(ak)
    av[...] = jnp.zeros_like(av)
    gsum[...] = jnp.zeros_like(gsum)
    for copy in heads_sent:
        links.arrived(copy)
    for copy in heads_sent:
        links.left(copy)

    def place(i, _):
        d, side = i // 2, i % 2
        at = pl.multiple_of(side * half, half)
        to = pl.multiple_of(jnp.where(side == 0, d, 2 * nc - 1 - d) * half, half)
        aq[ds(to, half), :] = dland[d, ds(at, half), :].astype(exact)
        return 0

    lax.fori_loop(0, 2 * nc, place, 0)
    for d in same:
        links.arrived(rows_same[d])
        there = datt.at[ds(pl.multiple_of((c ^ d) * tokens, tokens), tokens)]
        rows_side.append(links.send(there, there, ctx=c ^ 1))

    scale = hs ** -0.5
    for h in range(heads):
        lanes = slice(h * hs, (h + 1) * hs)
        for i in range(blocks):
            count = (i + 1) * block
            here = slice(i * block, count)
            q, k, v = rot[0, here, lanes], rot[1, :count, lanes], rot[2, :count, lanes]
            do = aq[here, lanes].astype(low)
            s = kdot(q, k, ((1,), (1,))) * scale
            row = lax.broadcasted_iota(jnp.int32, (block, count), 0) + i * block
            col = lax.broadcasted_iota(jnp.int32, (block, count), 1)
            s = jnp.where(col <= row, s, neg_large)
            p = jnp.exp(s - jnp.max(s, axis=-1, keepdims=True))
            p = p * (1.0 / jnp.sum(p, axis=-1, keepdims=True))
            dp = kdot(do, v, ((1,), (1,)))
            delta = jnp.sum(p * dp, axis=-1, keepdims=True)
            dscore = (p * (dp - delta)).astype(low)
            av[:count, lanes] += kdot(p.astype(low), do, ((0,), (0,)))
            ak[:count, lanes] += kdot(dscore, q, ((0,), (0,))) * scale
            aq[here, lanes] = kdot(dscore, k) * scale

    def unturn(i, _):
        d, side = i // 2, i % 2
        at = pl.multiple_of(d * tokens + side * half, half)
        to = pl.multiple_of(jnp.where(side == 0, d, 2 * nc - 1 - d) * half, half)
        cosine, sine = cos_ref[ds(at, half), :], sin_ref[ds(at, half), :]
        for j, acc, scale_ref, sums in ((0, aq, rq, cq), (1, ak, rk, ck)):
            row_sum = jnp.zeros((half, 1), exact)
            for h in range(heads):
                lanes = slice(h * hs, (h + 1) * hs)
                lane = j * cols + h * hs
                v = acc[ds(to, half), lanes]
                v = v * cosine - pltpu.roll(v, hs // 2, 1) * sine
                acc[ds(to, half), lanes] = v
                normed = raw[ds(at, half), lane : lane + hs] * scale_ref[ds(at, half), :]
                v = v * normed
                gsum[j : j + 1, lanes] += jnp.sum(v, axis=0, keepdims=True)
                gain = gain_ref[1 + j : 2 + j, ds(pl.multiple_of(c * cols + h * hs, hs), hs)]
                row_sum += jnp.sum(v * gain, axis=-1, keepdims=True)
            sums[ds(at, half), :] = jnp.broadcast_to(row_sum, (half, hs))
        return 0

    lax.fori_loop(0, 2 * nc, unturn, 0)
    lane8 = lax.broadcasted_iota(jnp.int32, (8, hs), 1)

    def gather_sums(i, _):
        at = pl.multiple_of(i * block, block)
        part = jnp.zeros((8, block), exact)
        for row, src in ((0, cq), (1, ck)):
            sel = jnp.where((row8 == row) & (lane8 == 0), 1.0, 0.0)
            part += kdot(sel, src[ds(at, block), :], ((1,), (1,)), best)
        stat[c, :, ds(at, block)] = part
        return 0

    lax.fori_loop(0, blocks, gather_sums, 0)
    stats = [links.send(stat.at[c], stat.at[c], ctx=c ^ d) for d in range(1, nc)]

    for copy in rows_side:
        links.arrived(copy)
    tile = width // nc
    tile_base = links.local_count
    links.local_count += nc

    def tile_load(k):
        return pltpu.make_async_copy(
            a1_ref.at[:, ds(k * tile, tile)], a1.at[lax.rem(k, 2)], locals_.at[tile_base + k]
        )

    tile_load(0).start()

    def out_tile(k, _):
        at = pl.multiple_of(k * tile, tile)
        v = kdot(ob[...], datt[:, ds(at, tile)], ((0,), (0,))).astype(low)
        go[:, :, ds(at, tile)] = v.reshape(nz, rows_w, tile)
        return 0

    lax.fori_loop(0, nc, out_tile, 0)
    for copy in stats:
        links.arrived(copy)
    summed = stat[0]
    for k in range(1, nc):
        summed += stat[k]
    total[...] = summed
    columns(total, cq, ck, lambda v: v)

    def finish(i, _):
        d, side = i // 2, i % 2
        at = pl.multiple_of(d * tokens + side * half, half)
        to = pl.multiple_of(jnp.where(side == 0, d, 2 * nc - 1 - d) * half, half)
        for j, acc, scale_ref, sums in ((0, aq, rq, cq), (1, ak, rk, ck)):
            for h in range(heads):
                lanes = slice(h * hs, (h + 1) * hs)
                lane = j * cols + h * hs
                gain = gain_ref[1 + j : 2 + j, ds(pl.multiple_of(c * cols + h * hs, hs), hs)]
                normed = raw[ds(at, half), lane : lane + hs] * scale_ref[ds(at, half), :]
                v = acc[ds(to, half), lanes] * gain - normed * sums[ds(at, half), :]
                dqkv[ds(at, half), lane : lane + hs] = (v * scale_ref[ds(at, half), :]).astype(low)
        dqkv[ds(at, half), 2 * cols : 3 * cols] = av[ds(to, half), :].astype(low)
        return 0

    lax.fori_loop(0, 2 * nc, finish, 0)
    for copy in later:
        links.left(copy)
    for copy in list(rows_same.values()) + rows_side:
        links.left(copy)

    def w_tile(k, _):
        @pl.when(k + 1 < nc)
        def _():
            tile_load(k + 1).start()

        tile_load(k).wait()
        v = kdot(a1[lax.rem(k, 2)], dqkv[...], ((0,), (0,))).astype(low)
        for j in range(3):
            gw[j, k] = v[:, j * cols : (j + 1) * cols].reshape(nz, rows_w, cols)
        return 0

    lax.fori_loop(0, nc, w_tile, 0)
    home = {}

    def send_home(s):
        peer = z ^ (s & -s)
        home[s] = (
            links.send(gw.at[:, :, z ^ s], wz_land.at[s], fsdp=peer),
            links.send(go.at[z ^ s], oz_land.at[s], fsdp=peer),
        )

    def taken(s):
        w_sum = gw[:, :, z ^ s].astype(exact)
        o_sum = go[z ^ s].astype(exact)
        bit = 1
        while bit < nz and (s == 0 or bit < (s & -s)):
            for copy in home[s | bit]:
                links.arrived(copy)
            got = [links.move(wz_land.at[s | bit], wtemp), links.move(oz_land.at[s | bit], otemp)]
            for copy in got:
                links.left(copy)
            w_sum += wtemp[...].astype(exact)
            o_sum += otemp[...].astype(exact)
            bit *= 2
        return w_sum, o_sum

    for s in range(nz - 1, 0, -1):
        if s & 1:
            send_home(s)

    def partial(k):
        at = pl.multiple_of(k * tokens, tokens)
        v = jnp.zeros((tokens, width), exact)
        for j in range(3):
            v += kdot(dqkv[ds(at, tokens), j * cols : (j + 1) * cols], w[j], ((1,), (1,)))
        datt[ds(at, tokens), :] = v.astype(low)

    def rows_of(k):
        return datt.at[ds(pl.multiple_of(k * tokens, tokens), tokens)]

    evens = [0] + same
    pair, chip = {}, {}

    def other_core(m, _):
        partial(2 * m + 1 - lax.rem(c, 2))
        return 0

    def this_core(m, _):
        partial(2 * m + lax.rem(c, 2))
        return 0

    lax.fori_loop(0, nc // 2, other_core, 0)
    for m, d in enumerate(evens):
        pair[d] = links.send(rows_of((c ^ 1) ^ d), pair_land.at[m], ctx=c ^ 1)
    lax.fori_loop(0, nc // 2, this_core, 0)
    for m, d in list(enumerate(evens))[::-1]:
        links.arrived(pair[d])
        got = links.move(pair_land.at[m], xtemp)
        links.left(got)
        mine = rows_of(c ^ d)
        if d:
            mine[...] = (mine[...].astype(exact) + xtemp[...].astype(exact)).astype(low)
            chip[d] = links.send(mine, chip_land.at[m], ctx=c ^ d)
        else:
            grad_in = mine[...].astype(exact) + xtemp[...].astype(exact)
            hidden_out[...] = grad_in

    for s in range(nz - 2, 0, -1):
        if not s & 1:
            w_sum, o_sum = taken(s)
            gw[:, :, z ^ s] = w_sum.astype(low)
            go[z ^ s] = o_sum.astype(low)
            send_home(s)

    for m, d in enumerate(evens):
        if d:
            links.arrived(chip[d])
            got = links.move(chip_land.at[m], xtemp)
            links.left(got)
            hidden_out[...] += xtemp[...].astype(exact)
    x = xrow[...].astype(exact)
    rs = lax.rsqrt(jnp.mean(x * x, axis=-1, keepdims=True) + epsilon)
    n1 = x * rs
    grad_in = hidden_out[...]
    gains_out[...] = jnp.zeros_like(gains_out)
    gains_out[0:1, :] = jnp.sum(grad_in * n1, axis=0, keepdims=True)
    for j in range(2):
        own_lanes = ds(pl.multiple_of(c * cols, cols), cols)
        gains_out[1 + j : 2 + j, own_lanes] = gsum[j : j + 1, :]
    gains_out[3:4, :] = fgain_ref[0:1, :]
    dn = grad_in * gain_ref[0:1, :]
    hidden_out[...] = dr1_ref[...] + rs * (dn - n1 * jnp.mean(dn * n1, axis=-1, keepdims=True))

    small_z[0] = gains_out[...]
    z_sums = [links.send(small_z.at[0], small_z.at[s], fsdp=z ^ s) for s in range(1, nz)]
    for copy in z_sums:
        links.arrived(copy)
    v = small_z[0]
    for s in range(1, nz):
        v += small_z[s]
    small_c[0] = v
    c_sums = [links.send(small_c.at[0], small_c.at[d], ctx=c ^ d) for d in range(1, nc)]
    for copy in c_sums:
        links.arrived(copy)
    v = small_c[0]
    for d in range(1, nc):
        v += small_c[d]
    gains_out[...] = v

    w_sum, o_sum = taken(0)
    wo_out[...] = o_sum
    wsum[...] = w_sum.astype(low)
    w_home = [links.send(wsum.at[:, c ^ d], wl.at[:, c], ctx=c ^ d) for d in range(1, nc)]
    w_own = links.move(wsum.at[:, c], wl.at[:, c])
    for copy in w_home:
        links.arrived(copy)
    links.left(w_own)
    for j in range(3):
        for k in range(nc):
            w_out[j, :, k * cols : (k + 1) * cols] = wl[j, k].astype(exact)
    for copy in up_sends:
        links.arrived(copy)
    links.close()


def run_back(cfg, x, dr1, datt, a1, w, raw, stat, rot, ob, wo, gains, fgain, gu, cosine, sine):
    nc, nz, tokens, width = cfg["nc"], cfg["nz"], cfg["tokens"], cfg["width"]
    cols, rows_w, length = cfg["cols"], cfg["rows_w"], cfg["length"]
    shape = jax.ShapeDtypeStruct
    any_, vmem = pl.BlockSpec(memory_space=pl.ANY), pl.BlockSpec(memory_space=pltpu.VMEM)
    outs = [
        (shape((tokens, width), exact), vmem),
        (shape((3, rows_w, width), exact), vmem),
        (shape((rows_w, width), exact), vmem),
        (shape((8, width), exact), vmem),
        (shape(gu.shape, low), any_),
        (shape((nc // 2, tokens, width), low), any_),
        (shape((nc // 2, tokens, width), low), any_),
        (shape((nz, 3, nc, rows_w, cols), low), any_),
        (shape((nz, rows_w, width), low), any_),
    ]
    scratch = [
        pltpu.VMEM((width, width), low),
        pltpu.VMEM((length, width), low),
        pltpu.VMEM((2, length, width // nc), low),
        pltpu.VMEM((3, width, cols), low),
        pltpu.VMEM((length, 2 * cols), exact),
        pltpu.VMEM((3, length, cols), low),
        pltpu.VMEM((length, cols), low),
        pltpu.VMEM((nc, tokens, cols), low),
        pltpu.VMEM((length, cols), exact),
        pltpu.VMEM((length, cols), exact),
        pltpu.VMEM((length, cols), exact),
        pltpu.VMEM((length, 128), exact),
        pltpu.VMEM((length, 128), exact),
        pltpu.VMEM((length, 128), exact),
        pltpu.VMEM((length, 128), exact),
        pltpu.VMEM((nc, 8, length), exact),
        pltpu.VMEM((8, length), exact),
        pltpu.VMEM((length, 3 * cols), low),
        pltpu.VMEM((3, nc, nz, rows_w, cols), low),
        pltpu.VMEM((nz, rows_w, width), low),
        pltpu.VMEM((8, cols), exact),
        pltpu.VMEM((3, nc, rows_w, cols), low),
        pltpu.VMEM((rows_w, width), low),
        pltpu.VMEM((3, nc, rows_w, cols), low),
        pltpu.VMEM((3, nc, rows_w, cols), low),
        pltpu.VMEM((tokens, width), low),
        pltpu.VMEM((tokens, width), low),
        pltpu.VMEM((nz, 8, width), exact),
        pltpu.VMEM((nc, 8, width), exact),
        pltpu.SemaphoreType.DMA((8 * nc + 8 * nz,)),
        pltpu.SemaphoreType.DMA((8 * nc + 8 * nz,)),
        pltpu.SemaphoreType.DMA((4 * nc + 8 * nz + 16,)),
    ]
    return pl.pallas_call(
        functools.partial(back_kernel, cfg),
        out_shape=[o[0] for o in outs],
        in_specs=[any_, vmem, any_, any_, any_, any_, vmem, any_, any_, any_, vmem, vmem, any_, vmem, vmem],
        out_specs=[o[1] for o in outs],
        scratch_shapes=scratch,
        compiler_params=pltpu.CompilerParams(
            collective_id=2, has_side_effects=True, vmem_limit_bytes=cfg["vmem"]
        ),
        name="back",
    )(x, dr1, datt, a1, w, raw, stat, rot, ob, wo, gains, fgain, gu, cosine, sine)


def tables(nc, tokens, head_size):
    half = tokens // 2
    local = np.arange(tokens)
    device = np.arange(nc)[:, None]
    position = np.where(
        local < half, device * half + local, (2 * nc - 1 - device) * half + local - half
    ).reshape(-1)
    freq = np.float32(10000.0) ** (-np.arange(head_size // 2, dtype=np.float32) * (2.0 / head_size))
    angle = position.astype(np.float32)[:, None] * freq.astype(np.float32)
    cosine = np.concatenate([np.cos(angle), np.cos(angle)], axis=1)
    sine = np.concatenate([-np.sin(angle), np.sin(angle)], axis=1)
    return jnp.asarray(cosine, exact), jnp.asarray(sine, exact)


def body(
    hidden_in,
    cotangent,
    routes,
    attn_gain,
    query_gain,
    key_gain,
    ffn_gain,
    w_query,
    w_key,
    w_value,
    w_out,
    w_router,
    w_gate,
    w_up,
    w_down,
):
    tokens = hidden_in.shape[1]
    width = hidden_in.shape[2]
    head_size = width // HEADS
    ctx_count = lax.axis_size("ctx")
    z_count = lax.axis_size("fsdp")
    both = ("ctx", "fsdp")
    top = routes.shape[2]
    exp_local = w_gate.shape[0]
    split = z_count // exp_local
    hidden = w_gate.shape[2]
    part = hidden // split
    experts = exp_local * ctx_count
    capacity = tokens * top * 4 // (3 * experts)
    cols = HEADS // ctx_count * head_size
    length = tokens * ctx_count
    c_index = lax.axis_index("ctx")
    z_index = lax.axis_index("fsdp")
    rows_w = w_query.shape[0]

    cfg = dict(
        nc=ctx_count,
        nz=z_count,
        tokens=tokens,
        width=width,
        cols=cols,
        rows_w=rows_w,
        length=length,
        cap=capacity,
        top=top,
        exp_local=exp_local,
        split=split,
        block=math.gcd(length, 256 if length <= 2048 else 128),
        chunk=math.gcd(length, 64),
        copies=(ctx_count - 1) * (8 + 2 * z_count) + (z_count - 1) * 12 + 2 * ctx_count + 8,
        part=part,
        vmem=62 * 2**20,
    )
    index = c_index * z_count + z_index
    per = 128 // rows_w
    gains = jnp.stack([attn_gain, query_gain, key_gain, ffn_gain]).astype(exact)
    gains = lax.dynamic_update_slice(
        jnp.zeros((8, 128), exact), gains, (0, jnp.mod(index, per) * rows_w)
    )
    router_tile = jnp.pad(w_router, ((0, 0), (0, 128 - experts)))
    route_tile = jnp.pad(routes[0].T, ((0, 8 - top), (0, 0)), constant_values=-1)

    def pieces_of(weight):
        rows = weight.shape[1]
        weight = weight.reshape(exp_local, rows, z_count, split, part // z_count)
        return weight.transpose(0, 3, 1, 2, 4).reshape(z_count, rows, part)

    down_pieces = w_down.reshape(z_count, -1, width)
    cosine, sine = tables(ctx_count, tokens, head_size)
    (
        attn_all, w_full, raw, squares, rot, out_heads, wo_full, resid_one,
        router_full, gains, routes_all, gate_full, up_full, down_full, cot_rows, cot_near,
        input_rows, input_near, *_,
    ) = front(
        cfg, hidden_in[0], w_query, w_key, w_value, w_out, gains, router_tile, route_tile,
        cotangent[0], pieces_of(w_gate), pieces_of(w_up), down_pieces,
        cosine, sine,
    )
    gate_full = gate_full.reshape(-1, part)
    up_full = up_full.reshape(-1, part)
    ffn_input = input_near[0]
    router_t = router_full.reshape(width, 128).T
    (
        resid_two, grad_one, attn_grad_low, logit_grad, ffn_gain_grad, down_land, gate_land,
        up_grad, *_,
    ) = run_experts(
        cfg, input_rows.reshape(-1, width), cot_rows.reshape(-1, width), router_t, routes_all,
        gate_full, up_full, down_full, down_pieces, input_near, cot_near, resid_one, gains,
    )
    out_hidden = resid_two[None]
    router_grad = lax.dot_general(
        ffn_input, logit_grad[:experts], (((0,), (1,)), ((), ())), preferred_element_type=exact
    )

    def whole_out(grad):
        grad = grad.reshape(exp_local, split, -1, z_count, part // z_count)
        return grad.transpose(0, 2, 3, 1, 4).reshape(exp_local, -1, hidden).astype(exact)

    grad_down = down_land.reshape(exp_local, -1, width).astype(exact)
    grad_gate = whole_out(gate_land)
    grad_hidden, w_grads, grad_out, gain_grads, up_land, *_ = run_back(
        cfg, hidden_in[0], grad_one, attn_grad_low, attn_all, w_full.reshape(3, width, cols), raw,
        squares, rot, out_heads, wo_full.reshape(width, width), gains, ffn_gain_grad,
        up_grad.reshape(z_count, -1, part), cosine, sine,
    )
    grad_up = whole_out(up_land)
    gain_grads = lax.dynamic_slice_in_dim(gain_grads, index * rows_w, rows_w, 1)
    sums = router_grad.reshape(ctx_count * z_count, rows_w * experts)
    sums = jnp.sum(exchange(sums, both), axis=0)
    return (
        out_hidden,
        grad_hidden[None],
        gain_grads[0],
        gain_grads[1],
        gain_grads[2],
        gain_grads[3],
        w_grads[0],
        w_grads[1],
        w_grads[2],
        grad_out,
        sums.reshape(rows_w, experts),
        grad_gate,
        grad_up,
        grad_down,
    )


def solution(mesh):
    in_specs = (
        P("fsdp", "ctx", None),
        P("fsdp", "ctx", None),
        P("fsdp", "ctx", None),
        P(("ctx", "fsdp")),
        P(("ctx", "fsdp")),
        P(("ctx", "fsdp")),
        P(("ctx", "fsdp")),
        P(("ctx", "fsdp"), None),
        P(("ctx", "fsdp"), None),
        P(("ctx", "fsdp"), None),
        P(("ctx", "fsdp"), None),
        P(("ctx", "fsdp"), None),
        P("ctx", "fsdp", None),
        P("ctx", "fsdp", None),
        P("ctx", "fsdp", None),
    )
    out_specs = (
        P("fsdp", "ctx", None),
        P("fsdp", "ctx", None),
        P(("ctx", "fsdp")),
        P(("ctx", "fsdp")),
        P(("ctx", "fsdp")),
        P(("ctx", "fsdp")),
        P(("ctx", "fsdp"), None),
        P(("ctx", "fsdp"), None),
        P(("ctx", "fsdp"), None),
        P(("ctx", "fsdp"), None),
        P(("ctx", "fsdp"), None),
        P("ctx", "fsdp", None),
        P("ctx", "fsdp", None),
        P("ctx", "fsdp", None),
    )
    return jax.shard_map(body, mesh=mesh, in_specs=in_specs, out_specs=out_specs, check_vma=False)
```

```python
import functools
import math

import jax
import jax.numpy as jnp
import numpy as np
from jax import lax
from jax.experimental import pallas as pl
from jax.experimental.pallas import tpu as pltpu
from jax.sharding import PartitionSpec as P

HEADS = 16


epsilon = 1e-05
neg_large = -1e30
low = jnp.bfloat16
exact = jnp.float32


def exchange(x, axis):
    return lax.all_to_all(x, axis, split_axis=0, concat_axis=0, tiled=True)


def bits_down(count):
    return [1 << i for i in range(count.bit_length() - 1)][::-1]


class Links:
    def __init__(self, sends, recvs, locals_):
        self.sends, self.recvs, self.locals = sends, recvs, locals_
        self.count = self.local_count = 0
        self.open = {}
        self.seen = {}

    def send(self, src, dst, **to):
        copy = pltpu.make_async_remote_copy(
            src_ref=src,
            dst_ref=dst,
            send_sem=self.sends.at[self.count],
            recv_sem=self.recvs.at[self.count],
            device_id=to,
            device_id_type=pl.DeviceIdType.MESH,
        )
        self.count += 1
        copy.start()
        self.open[id(copy)] = (copy, True)
        return copy

    def move(self, src, dst):
        copy = pltpu.make_async_copy(src, dst, self.locals.at[self.local_count])
        self.local_count += 1
        copy.start()
        self.open[id(copy)] = (copy, False)
        return copy

    def left(self, copy):
        if id(copy) in self.open:
            copy, remote = self.open.pop(id(copy))
            self.seen[id(copy), "left"] = copy
            copy.wait_send() if remote else copy.wait()

    def arrived(self, copy):
        if (id(copy), "in") not in self.seen:
            self.seen[id(copy), "in"] = copy
            copy.wait_recv()

    def close(self):
        for copy, _ in list(self.open.values()):
            self.left(copy)


def greet(c, z, nc, nz):
    barrier = pltpu.get_barrier_semaphore()
    for d in range(1, nc):
        pl.semaphore_signal(
            barrier, inc=1, device_id={"ctx": c ^ d}, device_id_type=pl.DeviceIdType.MESH
        )
    for s in range(1, nz):
        pl.semaphore_signal(
            barrier, inc=1, device_id={"fsdp": z ^ s}, device_id_type=pl.DeviceIdType.MESH
        )
    pl.semaphore_wait(barrier, nc - 1 + nz - 1)


def kdot(left, right, dims=((1,), (0,)), precision=None):
    return lax.dot_general(
        left, right, (dims, ((), ())), preferred_element_type=exact, precision=precision
    )


def slots_of(cfg, mask_rows, upper):
    rank = kdot(mask_rows.astype(low), upper)
    return jnp.where(mask_rows > 0, rank, 0.0)


def plane_ranks(cfg, routes, z):
    nc, tokens = cfg["nc"], cfg["tokens"]
    expert = lax.broadcasted_iota(jnp.int32, (nc, tokens), 0) * cfg["exp_local"] + z // cfg["split"]
    mask = jnp.zeros((nc, tokens), exact)
    for k in range(cfg["top"]):
        mask = jnp.where(routes[k : k + 1, :] == expert, 1.0, mask)
    upper = jnp.where(
        lax.broadcasted_iota(jnp.int32, (tokens, tokens), 0)
        <= lax.broadcasted_iota(jnp.int32, (tokens, tokens), 1),
        1.0,
        0.0,
    ).astype(low)
    return slots_of(cfg, mask, upper)


def fill_hot(cfg, ranks, hot_ref):
    cap, tokens = cfg["cap"], cfg["tokens"]
    number = lax.broadcasted_iota(jnp.int32, (cap, tokens), 0).astype(exact) + 1.0
    for k in range(cfg["nc"]):
        hit = jnp.where(ranks[k : k + 1, :] == number, 1.0, 0.0)
        hot_ref[k * cap : (k + 1) * cap, :] = hit.astype(low)


def front_kernel(
    cfg,
    x_ref, wq_ref, wk_ref, wv_ref, wo_ref, gt_ref, rt_ref, ro_ref, cot_ref, gp_ref, up_ref, dp_ref, cos_ref, sin_ref,
    a1_out, w_full, raw_out, stat_out, rot_out, ob_out, wo_full, r1_out, r_all, g_all, t_all,
    gate_full, up_full, down_full, cot_rows, cot_near, in_rows, in_near, staged,
    xbuf, wbuf, obw, gbuf, gfull, rbuf, tbuf, raw, stat, total, rq, rk, rot, opos, odev, orecv, r1, xrow, cbuf, abuf, hot, cs,
    sends, recvs, locals_,
):
    nc, nz, tokens, width = cfg["nc"], cfg["nz"], cfg["tokens"], cfg["width"]
    cols, rows_w, length, cap = cfg["cols"], cfg["rows_w"], cfg["length"], cfg["cap"]
    hs = 128
    heads = cols // hs
    half = tokens // 2
    block = cfg["block"]
    blocks = length // block
    c, z = lax.axis_index("ctx"), lax.axis_index("fsdp")
    links = Links(sends, recvs, locals_)
    ds = pl.ds
    same = [d for d in range(2, nc, 2)]
    steps = bits_down(nz)
    last = steps[-1]

    own_wo = links.move(wo_ref, obw.at[c, z])
    own_cot = links.move(cot_ref, cbuf.at[0])
    own_route = links.move(ro_ref, tbuf.at[c, z])
    own = []
    for j, ref in enumerate((wq_ref, wk_ref, wv_ref)):
        at = pl.multiple_of(c * cols, 128)
        own.append(links.move(ref.at[:, ds(at, cols)], wbuf.at[j, c, z]))
    own.append(links.move(gt_ref, gbuf.at[c, z]))
    own.append(links.move(rt_ref, rbuf.at[c, z]))
    own.append(links.move(x_ref, xbuf.at[ds(c * tokens, tokens)]))
    links.move(gp_ref.at[z], gate_full.at[z])
    links.move(up_ref.at[z], up_full.at[z])
    links.move(dp_ref.at[z], down_full.at[z])
    greet(c, z, nc, nz)

    slices = []
    for d in range(1, nc):
        peer = c ^ d
        at = pl.multiple_of(peer * cols, 128)
        for j, ref in enumerate((wq_ref, wk_ref, wv_ref)):
            slices.append(links.send(ref.at[:, ds(at, cols)], wbuf.at[j, c, z], ctx=peer))
    small_z = []
    for s in range(1, nz):
        for src, dst in ((gt_ref, gbuf), (rt_ref, rbuf), (ro_ref, tbuf)):
            small_z.append(links.send(src, dst.at[c, z], fsdp=z ^ s))
    wo_near, cot_copies, w_near = {}, {}, {}

    def wo_send(s, bit):
        place = obw.at[c, z ^ s]
        wo_near[s | bit] = links.send(place, place, fsdp=z ^ bit)

    def cot_send(s, bit):
        cot_copies[s | bit] = links.send(cbuf.at[s], cbuf.at[s | bit], fsdp=z ^ bit)

    def w_send(s, bit):
        place = wbuf.at[:, :, z ^ s]
        w_near[s | bit] = links.send(place, place, fsdp=z ^ bit)

    def forward(waits, send):
        for at, bit in enumerate(steps):
            held = [0]
            for earlier in steps[:at]:
                held += [s | earlier for s in held]
            for s in held[1:]:
                links.arrived(waits[s])
                send(s, bit)

    def all_in(waits):
        for s in range(1, nz):
            links.arrived(waits[s])

    links.left(own_wo)
    links.left(own_route)
    for bit in steps:
        wo_send(0, bit)
    x_at = xbuf.at[ds(c * tokens, tokens)]
    x_same = {d: links.send(x_ref, x_at, ctx=c ^ d) for d in same}
    x_side = [links.send(x_ref, x_at, ctx=c ^ 1)]
    rows_sent = []
    turn_of = [0]

    def dispatch(s, near, landing):
        number = turn_of[0]
        turn_of[0] += 1
        fill_hot(cfg, plane_ranks(cfg, tbuf[c, z ^ s], z), hot)
        cs[...] = kdot(hot[...], near[s]).astype(low)
        off = links.move(cs, staged.at[number])
        links.left(off)
        for d in range(1, nc):
            src = staged.at[number, ds((c ^ d) * cap, cap)]
            rows_sent.append(links.send(src, landing.at[s, c], ctx=c ^ d))
        links.move(cs.at[ds(c * cap, cap)], landing.at[s, c])

    def settle():
        for copy, remote in list(links.open.values()):
            if not remote:
                links.left(copy)

    for copy in own:
        links.left(copy)

    for copy in slices:
        links.arrived(copy)
    for bit in steps:
        w_send(0, bit)
    for copy in small_z:
        links.arrived(copy)
    small_c = []
    for d in range(1, nc):
        for buf in (gbuf, rbuf, tbuf):
            small_c.append(links.send(buf.at[c], buf.at[c], ctx=c ^ d))
    forward(wo_near, wo_send)
    for d in same:
        links.arrived(x_same[d])
        place = xbuf.at[ds((c ^ d) * tokens, tokens)]
        x_side.append(links.send(place, place, ctx=c ^ 1))
    links.left(own_cot)
    dispatch(0, cbuf, cot_rows)
    for copy in small_c:
        links.arrived(copy)
    per = 128 // rows_w
    groups = nz // per
    for k in range(nc):
        for g in range(groups):
            tile = gbuf[k, g * per]
            for p in range(1, per):
                tile = tile + gbuf[k, g * per + p]
            at = (k * groups + g) * 128
            gfull[:, at : at + 128] = tile
    all_in(wo_near)
    wo_same = {d: links.send(obw.at[c], obw.at[c], ctx=c ^ d) for d in same}
    wo_side = [links.send(obw.at[c], obw.at[c], ctx=c ^ 1)]
    for copy in x_side:
        links.arrived(copy)
    for copy in list(x_same.values()) + x_side:
        links.left(copy)

    chunk = cfg["chunk"]

    def norm_rows(i, _):
        at = pl.multiple_of(i * chunk, chunk)
        v = xbuf[ds(at, chunk), :].astype(exact)
        v = v * lax.rsqrt(jnp.mean(v * v, axis=-1, keepdims=True) + epsilon) * gfull[0:1, :]
        xbuf[ds(at, chunk), :] = v.astype(low)
        return 0

    forward(w_near, w_send)
    for bit in steps:
        cot_send(0, bit)
    lax.fori_loop(0, length // chunk, norm_rows, 0)
    links.move(xbuf, a1_out)
    all_in(w_near)
    experts_in = []
    for s in range(1, nz):
        experts_in.append(links.send(gp_ref.at[z ^ s], gate_full.at[z], fsdp=z ^ s))
    links.move(wbuf, w_full)

    one_row = lax.broadcasted_iota(jnp.int32, (8, cols), 0)
    pick_q = jnp.where(one_row == 0, 1.0, 0.0)
    pick_k = jnp.where(one_row == 1, 1.0, 0.0)
    best = lax.Precision.HIGHEST

    def project(i, _):
        at = pl.multiple_of(i * block, block)
        rows = xbuf[ds(at, block), :]
        sums = jnp.zeros((8, block), exact)
        for j in range(3):
            weight = wbuf[j].reshape(width, cols)
            v = kdot(rows, weight)
            raw[ds(at, block), j * cols : (j + 1) * cols] = v
            if j < 2:
                sums += kdot(pick_k if j else pick_q, v * v, ((1,), (1,)), best)
        stat[c, :, ds(at, block)] = sums
        return 0

    lax.fori_loop(0, blocks, project, 0)
    stats = [links.send(stat.at[c], stat.at[c], ctx=c ^ d) for d in range(1, nc)]
    links.move(raw, raw_out)
    for d in same:
        links.arrived(wo_same[d])
        place_at = obw.at[c ^ d]
        wo_side.append(links.send(place_at, place_at, ctx=c ^ 1))
    for copy in stats:
        links.arrived(copy)
    summed = stat[0]
    for k in range(1, nc):
        summed += stat[k]
    total[...] = summed
    row8 = lax.broadcasted_iota(jnp.int32, (8, hs), 0)

    def columns(i, _):
        at = pl.multiple_of(i * block, block)
        part = total[:, ds(at, block)]
        for row, dst in ((0, rq), (1, rk)):
            sel = jnp.where(row8 == row, 1.0, 0.0)
            ms = kdot(part, sel, ((0,), (0,)), best)
            dst[ds(at, block), :] = lax.rsqrt(ms / width + epsilon)
        return 0

    lax.fori_loop(0, blocks, columns, 0)
    links.move(total, stat_out)
    forward(cot_copies, cot_send)
    for s in range(1, nz):
        experts_in.append(links.send(up_ref.at[z ^ s], up_full.at[z], fsdp=z ^ s))

    def turn(i, _):
        d, side = i // 2, i % 2
        at = pl.multiple_of(d * tokens + side * half, half)
        to = pl.multiple_of(jnp.where(side == 0, d, 2 * nc - 1 - d) * half, half)
        cosine, sine = cos_ref[ds(at, half), :], sin_ref[ds(at, half), :]
        for h in range(heads):
            for j, scale in ((0, rq), (1, rk)):
                lane = j * cols + h * hs
                gain = gfull[1 + j : 2 + j, ds(pl.multiple_of(c * cols + h * hs, hs), hs)]
                v = raw[ds(at, half), lane : lane + hs] * scale[ds(at, half), :] * gain
                v = v * cosine + pltpu.roll(v, hs // 2, 1) * sine
                rot[j, ds(to, half), h * hs : (h + 1) * hs] = v.astype(low)
        rot[2, ds(to, half), :] = raw[ds(at, half), 2 * cols : 3 * cols].astype(low)
        return 0

    lax.fori_loop(0, 2 * nc, turn, 0)
    links.move(rot, rot_out)
    settle()
    for bit in steps:
        links.arrived(cot_copies[bit])
        dispatch(bit, cbuf, cot_rows)
        settle()

    scale = hs ** -0.5
    for h in range(heads):
        lanes = slice(h * hs, (h + 1) * hs)
        for i in range(blocks):
            count = (i + 1) * block
            q = rot[0, i * block : count, lanes]
            s = kdot(q, rot[1, :count, lanes], ((1,), (1,))) * scale
            row = lax.broadcasted_iota(jnp.int32, (block, count), 0) + i * block
            col = lax.broadcasted_iota(jnp.int32, (block, count), 1)
            s = jnp.where(col <= row, s, neg_large)
            p = jnp.exp(s - jnp.max(s, axis=-1, keepdims=True))
            p = p * (1.0 / jnp.sum(p, axis=-1, keepdims=True))
            opos[i * block : count, lanes] = kdot(p.astype(low), rot[2, :count, lanes]).astype(low)

    def place(i, _):
        d, side = i // 2, i % 2
        to = pl.multiple_of(d * tokens + side * half, half)
        at = pl.multiple_of(jnp.where(side == 0, d, 2 * nc - 1 - d) * half, half)
        odev[ds(to, half), :] = opos[ds(at, half), :]
        return 0

    lax.fori_loop(0, 2 * nc, place, 0)
    mixed = []
    for d in range(1, nc):
        src = odev.at[ds((c ^ d) * tokens, tokens)]
        mixed.append(links.send(src, orecv.at[c], ctx=c ^ d))
    own_mixed = links.move(odev.at[ds(c * tokens, tokens)], orecv.at[c])
    links.move(odev, ob_out)
    x_in = links.move(x_ref, xrow)
    for copy in wo_side:
        links.arrived(copy)
    links.move(obw, wo_full)
    r1[...] = jnp.zeros_like(r1)
    for copy in mixed:
        links.arrived(copy)
    links.left(own_mixed)

    def mix(k, _):
        r1[...] += kdot(orecv[k], obw[k].reshape(cols, width))
        return 0

    lax.fori_loop(0, nc, mix, 0)
    links.left(x_in)
    v = r1[...] + xrow[...].astype(exact)
    r1[...] = v
    n2 = v * lax.rsqrt(jnp.mean(v * v, axis=-1, keepdims=True) + epsilon)
    abuf[0] = (n2 * gfull[3:4, :]).astype(low)
    in_copies = {}

    def in_send(s, bit):
        in_copies[s | bit] = links.send(abuf.at[s], abuf.at[s | bit], fsdp=z ^ bit)

    for bit in steps:
        in_send(0, bit)
    settle()
    dispatch(0, abuf, in_rows)
    links.move(r1, r1_out)
    links.move(rbuf, r_all)
    links.move(gfull, g_all)
    links.move(tbuf, t_all)
    all_in(cot_copies)
    links.move(cbuf, cot_near)
    for s in range(1, nz):
        if s & (s - 1):
            settle()
            dispatch(s, cbuf, cot_rows)
    forward(in_copies, in_send)
    for s in range(1, nz - 1):
        experts_in.append(links.send(dp_ref.at[z ^ s], down_full.at[z], fsdp=z ^ s))
    for s in list(steps) + [s for s in range(1, nz) if s & (s - 1)]:
        links.arrived(in_copies[s])
        settle()
        dispatch(s, abuf, in_rows)
    links.move(abuf, in_near)
    for copy in experts_in + rows_sent:
        links.arrived(copy)
    links.close()


def front(cfg, x, w_query, w_key, w_value, w_out, gains, router, routes, cot, gate_pieces, up_pieces, down_pieces, cosine, sine):
    nc, nz, tokens, width = cfg["nc"], cfg["nz"], cfg["tokens"], cfg["width"]
    cols, rows_w, length, cap = cfg["cols"], cfg["rows_w"], cfg["length"], cfg["cap"]
    rows, part = gate_pieces.shape[1:]
    shape = jax.ShapeDtypeStruct
    any_, vmem = pl.BlockSpec(memory_space=pl.ANY), pl.BlockSpec(memory_space=pltpu.VMEM)
    top_rows = routes.shape[0]
    outs = [
        shape((length, width), low),
        shape((3, nc, nz, rows_w, cols), low),
        shape((length, 3 * cols), exact),
        shape((8, length), exact),
        shape((3, length, cols), low),
        shape((length, cols), low),
        shape((nc, nz, rows_w, width), low),
        shape((tokens, width), exact),
        shape((nc, nz, rows_w, 128), low),
        shape((8, width), exact),
        shape((nc, nz, top_rows, tokens), jnp.int32),
        shape((nz, rows, part), low),
        shape((nz, rows, part), low),
        shape(down_pieces.shape, low),
        shape((nz, nc, cap, width), low),
        shape((nz, tokens, width), low),
        shape((nz, nc, cap, width), low),
        shape((nz, tokens, width), low),
        shape((2 * nz, nc * cap, width), low),
    ]
    scratch = [
        pltpu.VMEM((length, width), low),
        pltpu.VMEM((3, nc, nz, rows_w, cols), low),
        pltpu.VMEM((nc, nz, rows_w, width), low),
        pltpu.VMEM((nc, nz, 8, 128), exact),
        pltpu.VMEM((8, width), exact),
        pltpu.VMEM((nc, nz, rows_w, 128), low),
        pltpu.VMEM((nc, nz, top_rows, tokens), jnp.int32),
        pltpu.VMEM((length, 3 * cols), exact),
        pltpu.VMEM((nc, 8, length), exact),
        pltpu.VMEM((8, length), exact),
        pltpu.VMEM((length, 128), exact),
        pltpu.VMEM((length, 128), exact),
        pltpu.VMEM((3, length, cols), low),
        pltpu.VMEM((length, cols), low),
        pltpu.VMEM((length, cols), low),
        pltpu.VMEM((nc, tokens, cols), low),
        pltpu.VMEM((tokens, width), exact),
        pltpu.VMEM((tokens, width), low),
        pltpu.VMEM((nz, tokens, width), low),
        pltpu.VMEM((nz, tokens, width), low),
        pltpu.VMEM((nc * cap, tokens), low),
        pltpu.VMEM((nc * cap, width), low),
        pltpu.SemaphoreType.DMA((cfg["copies"],)),
        pltpu.SemaphoreType.DMA((cfg["copies"],)),
        pltpu.SemaphoreType.DMA((32 + 4 * cfg["nz"],)),
    ]
    return pl.pallas_call(
        functools.partial(front_kernel, cfg),
        out_shape=outs,
        in_specs=[any_] * 12 + [vmem] * 2,
        out_specs=[any_] * len(outs),
        scratch_shapes=scratch,
        compiler_params=pltpu.CompilerParams(
            collective_id=0, has_side_effects=True, vmem_limit_bytes=cfg["vmem"]
        ),
        name="front",
    )(x, w_query, w_key, w_value, w_out, gains, router, routes, cot, gate_pieces, up_pieces, down_pieces, cosine, sine)


def expert_kernel(
    cfg,
    rows_ref, cotr_ref, rt_ref, tb_ref, wg_ref, wu_ref, wd_ref, dp_ref, near_ref, cotn_ref, r1_ref, gain_ref,
    hidden_out, dr1_out, datt_out, dlog_out, fgain_out, gd_land, gg_land, gu_out,
    back, in_back, out_land, in_land, ebh, rbh,
    wg, wu, wd, rows, cotb, gin, gdb, du, eb, rb, tile, ranks, hot, metab, gate_rows, dgs, dgl,
    sends, recvs, locals_,
):
    nc, nz, tokens, width = cfg["nc"], cfg["nz"], cfg["tokens"], cfg["width"]
    cap, part, split, exp_local = cfg["cap"], cfg["part"], cfg["split"], cfg["exp_local"]
    ch = nc * cap
    total = nz * ch
    c, z = lax.axis_index("ctx"), lax.axis_index("fsdp")
    links = Links(sends, recvs, locals_)
    ds = pl.ds
    expert = c * exp_local + z // split
    best = lax.Precision.HIGHEST
    peers = list(range(1, nc))

    loads = [links.move(wg_ref, wg), links.move(wu_ref, wu), links.move(rows_ref, rows)]
    rows_d = part // nz

    def down_place(owner):
        return wd.at[ds(pl.multiple_of(owner * rows_d, rows_d), rows_d)]

    down_here = [links.move(wd_ref.at[z ^ s], down_place(z ^ s)) for s in range(nz - 1)]
    cot_base = links.local_count
    links.local_count += nz
    send_base = links.count
    links.count += 2 * nz * (nc - 1)
    keep_base = links.local_count
    links.local_count += 2 * nz
    off_base = links.local_count
    links.local_count += 2 * nz

    def cot_load(s, slot):
        return pltpu.make_async_copy(
            cotr_ref.at[ds(s * ch, ch)], cotb.at[slot], locals_.at[cot_base + s]
        )

    def chunk_copies(s, which):
        buf, landing = ((ebh, back), (rbh, in_back))[which]
        base = send_base + which * nz * (nc - 1) + s * (nc - 1)
        out = []
        for d in peers:
            out.append(
                pltpu.make_async_remote_copy(
                    src_ref=buf.at[s, ds((c ^ d) * cap, cap)],
                    dst_ref=landing.at[s, c],
                    send_sem=sends.at[base + d - 1],
                    recv_sem=recvs.at[base + d - 1],
                    device_id={"ctx": c ^ d},
                    device_id_type=pl.DeviceIdType.MESH,
                )
            )
        return out

    def keep_copy(s, which):
        landing = (back, in_back)[which]
        return pltpu.make_async_copy(
            (ebh, rbh)[which].at[s, ds(c * cap, cap)],
            landing.at[s, c],
            locals_.at[keep_base + which * nz + s],
        )

    def off_copy(s, which):
        return pltpu.make_async_copy(
            (eb, rb)[which], (ebh, rbh)[which].at[s], locals_.at[off_base + which * nz + s]
        )

    cot_load(nz - 1, 0).start()
    greet(c, z, nc, nz)
    far = z ^ (nz - 1)
    down_in = [links.send(dp_ref.at[far], down_place(z), fsdp=far)]
    for copy in loads:
        links.left(copy)

    expert_rows = lax.broadcasted_iota(jnp.int32, (128, tokens), 0)
    upper = jnp.where(
        lax.broadcasted_iota(jnp.int32, (tokens, tokens), 0)
        <= lax.broadcasted_iota(jnp.int32, (tokens, tokens), 1),
        1.0,
        0.0,
    ).astype(low)

    def routed(block):
        chosen = jnp.zeros((128, tokens), exact)
        for k in range(cfg["top"]):
            chosen = jnp.where(block[k : k + 1, :] == expert_rows, 1.0, chosen)
        return chosen

    sub = min(256, ch)
    lane = lax.broadcasted_iota(jnp.int32, (sub, 128), 1)

    def gate_of(block, picked):
        logits = kdot(block, rt_ref[...], ((1,), (1,)))
        logits = jnp.where(picked > 0.5, logits, neg_large)
        weight = jnp.exp(logits - jnp.max(logits, axis=-1, keepdims=True))
        gate = jnp.sum(jnp.where(lane == expert, weight, 0.0), axis=-1, keepdims=True)
        return gate / jnp.sum(weight, axis=-1, keepdims=True)

    def first_work(s, _):
        for k in range(nc):
            block = tb_ref[k, z ^ s]
            found = jnp.where(block == expert, 1.0, 0.0)
            ranks[k : k + 1, :] = jnp.max(found, axis=0, keepdims=True)
        ranks[...] = slots_of(cfg, ranks[...], upper)
        fill_hot(cfg, ranks[...], hot)
        for k in range(nc):
            chosen = routed(tb_ref[k, z ^ s]).astype(low)
            metab[k * cap : (k + 1) * cap, :] = kdot(
                hot[k * cap : (k + 1) * cap, :], chosen, ((1,), (1,))
            )

        def some_rows(j, _):
            here = pl.multiple_of(j * sub, sub)
            at = pl.multiple_of(s * ch + j * sub, sub)
            span, to = ds(here, sub), ds(at, sub)
            block = rows[to, :]
            gate = gate_of(block, metab[span, :])
            g = kdot(block, wg[...])
            u = kdot(block, wu[...])
            inner = (g * (1.0 / (1.0 + jnp.exp(-g))) * u).astype(low)
            gin[to, :] = (inner.astype(exact) * gate).astype(low)
            gate_rows[to, :] = jnp.broadcast_to(gate, (sub, 128))
            return 0

        lax.fori_loop(0, ch // sub, some_rows, 0)
        return 0

    lax.fori_loop(0, nz, first_work, 0)

    step = 256 if nz * ch <= 2048 else 128
    tile_base = links.local_count
    links.local_count += width // step

    def tile_load(k):
        return pltpu.make_async_copy(
            cotr_ref.at[:, ds(k * step, step)], tile.at[lax.rem(k, 2)], locals_.at[tile_base + k]
        )

    tile_load(0).start()

    def down_tile(k, _):
        @pl.when(k + 1 < width // step)
        def _():
            tile_load(k + 1).start()

        tile_load(k).wait()
        at = pl.multiple_of(k * step, step)
        gdb[:, ds(at, step)] = kdot(gin[...], tile[lax.rem(k, 2)], ((0,), (0,))).astype(low)
        return 0

    lax.fori_loop(0, width // step, down_tile, 0)
    grads_out = []
    for s in range(1, nz):
        src = gdb.at[ds(pl.multiple_of((z ^ s) * rows_d, rows_d), rows_d)]
        grads_out.append(links.send(src, gd_land.at[z], fsdp=z ^ s))
    links.move(gdb.at[ds(pl.multiple_of(z * rows_d, rows_d), rows_d)], gd_land.at[z])
    for copy in down_here:
        links.left(copy)
    for copy in down_in:
        links.arrived(copy)

    def work(i, _):
        s = nz - 1 - i
        slot = lax.rem(i, 2)

        @pl.when(i + 1 < nz)
        def _():
            cot_load(s - 1, 1 - slot).start()

        cot_load(s, slot).wait()

        def some_rows(j, _):
            here = pl.multiple_of(j * sub, sub)
            at = pl.multiple_of(s * ch + j * sub, sub)
            span, to = ds(here, sub), ds(at, sub)
            block = rows[to, :]
            gate = gate_rows[to, 0:1]
            g = kdot(block, wg[...])
            u = kdot(block, wu[...])
            sg = 1.0 / (1.0 + jnp.exp(-g))
            act = g * sg
            inner = (act * u).astype(low)
            eb[span, :] = kdot(inner, wd[...]).astype(low)
            dinner = kdot(cotb[slot, span, :], wd[...], ((1,), (1,))) * gate
            dg_low = (dinner * u * sg * (1.0 + g * (1.0 - sg))).astype(low)
            du_low = (dinner * act).astype(low)
            gin[to, :] = dg_low
            du[to, :] = du_low
            rb[span, :] = (
                kdot(dg_low, wg[...], ((1,), (1,))) + kdot(du_low, wu[...], ((1,), (1,)))
            ).astype(low)
            return 0

        lax.fori_loop(0, ch // sub, some_rows, 0)
        for which in (0, 1):
            off_copy(s, which).start()
        for which in (0, 1):
            off_copy(s, which).wait()
            for copy in chunk_copies(s, which):
                copy.start()
            keep_copy(s, which).start()
        return 0

    lax.fori_loop(0, nz, work, 0)

    rows_g = width // nz

    def rows_tile(left, dst):
        def one(k, _):
            at = pl.multiple_of(k * step, step)
            dst[ds(at, step), :] = kdot(rows[:, ds(at, step)], left[...], ((0,), (0,))).astype(low)
            return 0

        lax.fori_loop(0, width // step, one, 0)

    rows_tile(gin, wg)
    for s in range(1, nz):
        src = wg.at[ds(pl.multiple_of((z ^ s) * rows_g, rows_g), rows_g)]
        grads_out.append(links.send(src, gg_land.at[z], fsdp=z ^ s))
    links.move(wg.at[ds(pl.multiple_of(z * rows_g, rows_g), rows_g)], gg_land.at[z])
    rows_tile(du, wu)
    links.move(wu, gu_out)

    spare = {}
    at = 0
    for name, count in (
        ("back", ch), ("in_back", ch), ("near", tokens), ("cot", tokens), ("out0", tokens),
        ("in0", tokens),
    ):
        spare[name] = rows.at[at : at + count]
        at += count
    stage = {0: (spare["out0"], spare["in0"]), 1: (cotb.at[0, 0:tokens], cotb.at[1, 0:tokens])}
    extra = (cotb.at[0, tokens : 2 * tokens], cotb.at[1, tokens : 2 * tokens])
    pick_rows = lax.broadcasted_iota(jnp.int32, (nc, 128), 0)
    pick_lane = lax.broadcasted_iota(jnp.int32, (nc, 128), 1)
    homeward = {}
    gate_home = {}
    busy = {0: [], 1: []}
    gates_own = None
    sums = None
    for s in range(nz - 1, -1, -1):
        for which in (0, 1):
            out = chunk_copies(s, which)
            for copy in out:
                copy.wait_recv()
            keep_copy(s, which).wait()
        fetch = []
        for k in range(nc):
            fetch.append(links.move(back.at[s, k], rows.at[k * cap : (k + 1) * cap]))
            fetch.append(links.move(in_back.at[s, k], rows.at[ch + k * cap : ch + (k + 1) * cap]))
        fetch.append(links.move(near_ref.at[s], spare["near"]))
        fetch.append(links.move(cotn_ref.at[s], spare["cot"]))
        block = tb_ref[c, z ^ s]
        fill_hot(cfg, plane_ranks(cfg, block, z), hot)
        chosen = routed(block)
        for copy in fetch:
            links.left(copy)
        logits = kdot(rt_ref[...], spare["near"][...], ((1,), (1,)))
        logits = jnp.where(chosen > 0.5, logits, neg_large)
        weight = jnp.exp(logits - jnp.max(logits, axis=0, keepdims=True))
        gates = weight / jnp.sum(weight, axis=0, keepdims=True)
        sel = jnp.where(pick_lane == pick_rows * exp_local + z // split, 1.0, 0.0)
        plane = kdot(sel, gates, ((1,), (0,)), best)
        slot_grad = kdot(spare["back"][...], spare["cot"][...], ((1,), (1,)))
        for k in range(nc):
            span = slice(k * cap, (k + 1) * cap)
            hit = hot[span, :].astype(exact)
            dgs[s, k : k + 1, :] = jnp.sum(hit * slot_grad[span, :], axis=0, keepdims=True)
        in_part = kdot(hot[...], spare["in_back"][...], ((0,), (0,)))
        for k in range(nc):
            span = slice(k * cap, (k + 1) * cap)
            hot[span, :] = (hot[span, :].astype(exact) * plane[k : k + 1, :]).astype(low)
        out_part = kdot(hot[...], spare["back"][...], ((0,), (0,)))
        lowest = s & -s
        bit = 1
        while bit < nz and (s == 0 or bit < lowest):
            for copy in homeward[s | bit]:
                links.arrived(copy)
            got = [links.move(out_land.at[s | bit], extra[0]), links.move(in_land.at[s | bit], extra[1])]
            for copy in got:
                links.left(copy)
            out_part += extra[0][...].astype(exact)
            in_part += extra[1][...].astype(exact)
            bit *= 2
        if s:
            slot = s % 2
            for copy in busy[slot]:
                links.left(copy)
            stage[slot][0][...] = out_part.astype(low)
            stage[slot][1][...] = in_part.astype(low)
            homeward[s] = [
                links.send(stage[slot][0], out_land.at[s], fsdp=z ^ lowest),
                links.send(stage[slot][1], in_land.at[s], fsdp=z ^ lowest),
            ]
            busy[slot] = homeward[s]
            gate_home[s] = links.send(dgs.at[s], dgl.at[s], fsdp=z ^ s)
        else:
            gates_own = gates
            sums = (out_part, in_part)

    dgate = jnp.zeros((128, tokens), exact)
    for s in range(nz):
        if s:
            links.arrived(gate_home[s])
        here = dgl[s] if s else dgs[0]
        sel = jnp.where(pick_lane == pick_rows * exp_local + (z ^ s) // split, 1.0, 0.0)
        dgate += kdot(sel, here, ((0,), (0,)), best)
    dchosen = gates_own * (dgate - jnp.sum(gates_own * dgate, axis=0, keepdims=True))
    dlog = dchosen.astype(low)
    hot[0:128, :] = dlog
    dlog_copy = links.move(hot.at[0:128], dlog_out)
    out_part, in_part = sums
    da2 = in_part + kdot(dlog, rt_ref[...], ((0,), (0,)))
    r1 = r1_ref[...]
    for copies in busy.values():
        for copy in copies:
            links.left(copy)
    stage[0][0][...] = (r1 + out_part).astype(low)
    links.move(stage[0][0], hidden_out)
    rs = lax.rsqrt(jnp.mean(r1 * r1, axis=-1, keepdims=True) + epsilon)
    n2 = r1 * rs
    dm = da2 * gain_ref[3:4, :]
    fgain_out[...] = jnp.broadcast_to(jnp.sum(da2 * n2, axis=0, keepdims=True), (8, width))
    inner_mean = jnp.mean(dm * n2, axis=-1, keepdims=True)
    dr1 = spare["cot"][...].astype(exact) + rs * (dm - n2 * inner_mean)
    dr1_out[...] = dr1
    datt_out[...] = dr1.astype(low)
    for s in range(nz):
        for which in (0, 1):
            out = chunk_copies(s, which)
            for copy in out:
                copy.wait_send()
    for copy in grads_out:
        links.arrived(copy)
    links.close()


def run_experts(cfg, rows, cot_rows, router_t, routes, wg, wu, wd, down_pieces, near, cot_near, r1, gains):
    nc, nz, tokens, width = cfg["nc"], cfg["nz"], cfg["tokens"], cfg["width"]
    cap, part = cfg["cap"], cfg["part"]
    ch = nc * cap
    shape = jax.ShapeDtypeStruct
    any_, vmem = pl.BlockSpec(memory_space=pl.ANY), pl.BlockSpec(memory_space=pltpu.VMEM)
    outs = [
        (shape((tokens, width), low), any_),
        (shape((tokens, width), exact), vmem),
        (shape((tokens, width), low), vmem),
        (shape((128, tokens), low), any_),
        (shape((8, width), exact), vmem),
        (shape((nz, part // nz, width), low), any_),
        (shape((nz, width // nz, part), low), any_),
        (shape((width, part), low), any_),
        (shape((nz, nc, cap, width), low), any_),
        (shape((nz, nc, cap, width), low), any_),
        (shape((nz, tokens, width), low), any_),
        (shape((nz, tokens, width), low), any_),
        (shape((nz, ch, width), low), any_),
        (shape((nz, ch, width), low), any_),
    ]
    step = 256 if nz * ch <= 2048 else 128
    scratch = [
        pltpu.VMEM((width, part), low),
        pltpu.VMEM((width, part), low),
        pltpu.VMEM((part, width), low),
        pltpu.VMEM((nz * ch, width), low),
        pltpu.VMEM((2, ch, width), low),
        pltpu.VMEM((nz * ch, part), low),
        pltpu.VMEM((part, width), low),
        pltpu.VMEM((nz * ch, part), low),
        pltpu.VMEM((ch, width), low),
        pltpu.VMEM((ch, width), low),
        pltpu.VMEM((2, nz * ch, step), low),
        pltpu.VMEM((nc, tokens), exact),
        pltpu.VMEM((ch, tokens), low),
        pltpu.VMEM((ch, 128), exact),
        pltpu.VMEM((nz * ch, 128), exact),
        pltpu.VMEM((nz, nc, tokens), exact),
        pltpu.VMEM((nz, nc, tokens), exact),
        pltpu.SemaphoreType.DMA((2 * nz * nc + 8 * nz,)),
        pltpu.SemaphoreType.DMA((2 * nz * nc + 8 * nz,)),
        pltpu.SemaphoreType.DMA((2 * nz * nc + 16 * nz + width // step + 16,)),
    ]
    return pl.pallas_call(
        functools.partial(expert_kernel, cfg),
        out_shape=[o[0] for o in outs],
        in_specs=[any_, any_, vmem, vmem, any_, any_, any_, any_, any_, any_, vmem, vmem],
        out_specs=[o[1] for o in outs],
        scratch_shapes=scratch,
        compiler_params=pltpu.CompilerParams(
            collective_id=1, has_side_effects=True, vmem_limit_bytes=cfg["vmem"]
        ),
        name="experts",
    )(rows, cot_rows, router_t, routes, wg, wu, wd, down_pieces, near, cot_near, r1, gains)


def back_kernel(
    cfg,
    x_ref, dr1_ref, datt_ref, a1_ref, w_ref, raw_ref, stat_ref, rot_ref, ob_ref, wo_ref, gain_ref, fgain_ref,
    gu_ref, cos_ref, sin_ref,
    hidden_out, w_out, wo_out, gains_out, gu_land, pair_land, chip_land, wz_land, oz_land,
    wo, datt, a1, w, raw, rot, ob, dland, aq, ak, av, rq, rk, cq, ck, stat, total, dqkv, gw, go, gsum,
    wtemp, otemp, wsum, wl, xrow, xtemp, small_z, small_c,
    sends, recvs, locals_,
):
    nc, nz, tokens, width = cfg["nc"], cfg["nz"], cfg["tokens"], cfg["width"]
    cols, rows_w, length = cfg["cols"], cfg["rows_w"], cfg["length"]
    hs = 128
    heads = cols // hs
    half = tokens // 2
    block = cfg["block"]
    blocks = length // block
    c, z = lax.axis_index("ctx"), lax.axis_index("fsdp")
    links = Links(sends, recvs, locals_)
    ds = pl.ds
    best = lax.Precision.HIGHEST
    same = [d for d in range(2, nc, 2)]
    own_rows = ds(pl.multiple_of(c * tokens, tokens), tokens)

    wo_in = links.move(wo_ref, wo)
    datt_in = links.move(datt_ref, datt.at[own_rows])
    first = [links.move(rot_ref, rot), links.move(raw_ref.at[:, 0 : 2 * cols], raw), links.move(ob_ref, ob)]
    later = [links.move(w_ref, w), links.move(x_ref, xrow)]
    up_own = links.move(gu_ref.at[z], gu_land.at[z])
    greet(c, z, nc, nz)
    up_sends = [links.send(gu_ref.at[z ^ s], gu_land.at[z], fsdp=z ^ s) for s in range(1, nz)]
    links.left(datt_in)
    links.left(wo_in)

    heads_sent = []
    for d in range(1, nc):
        at = pl.multiple_of((c ^ d) * cols, cols)
        spot = dqkv.at[d * tokens : (d + 1) * tokens, 0:cols]
        spot[...] = kdot(datt[own_rows, :], wo[ds(at, cols), :], ((1,), (1,))).astype(low)
        heads_sent.append(links.send(spot, dland.at[c], ctx=c ^ d))
    at = pl.multiple_of(c * cols, cols)
    dland[c] = kdot(datt[own_rows, :], wo[ds(at, cols), :], ((1,), (1,))).astype(low)
    rows_same = {d: links.send(datt.at[own_rows], datt.at[own_rows], ctx=c ^ d) for d in same}
    rows_side = [links.send(datt.at[own_rows], datt.at[own_rows], ctx=c ^ 1)]
    for copy in first:
        links.left(copy)

    row8 = lax.broadcasted_iota(jnp.int32, (8, hs), 0)

    def columns(src, one, two, finish):
        def step(i, _):
            at = pl.multiple_of(i * block, block)
            part = src[:, ds(at, block)]
            for row, dst in ((0, one), (1, two)):
                sel = jnp.where(row8 == row, 1.0, 0.0)
                dst[ds(at, block), :] = finish(kdot(part, sel, ((0,), (0,)), best) / width)
            return 0

        lax.fori_loop(0, blocks, step, 0)

    columns(stat_ref, rq, rk, lambda v: lax.rsqrt(v + epsilon))
    ak[...] = jnp.zeros_like(ak)
    av[...] = jnp.zeros_like(av)
    gsum[...] = jnp.zeros_like(gsum)
    for copy in heads_sent:
        links.arrived(copy)
    for copy in heads_sent:
        links.left(copy)

    def place(i, _):
        d, side = i // 2, i % 2
        at = pl.multiple_of(side * half, half)
        to = pl.multiple_of(jnp.where(side == 0, d, 2 * nc - 1 - d) * half, half)
        aq[ds(to, half), :] = dland[d, ds(at, half), :].astype(exact)
        return 0

    lax.fori_loop(0, 2 * nc, place, 0)
    for d in same:
        links.arrived(rows_same[d])
        there = datt.at[ds(pl.multiple_of((c ^ d) * tokens, tokens), tokens)]
        rows_side.append(links.send(there, there, ctx=c ^ 1))

    scale = hs ** -0.5
    for h in range(heads):
        lanes = slice(h * hs, (h + 1) * hs)
        for i in range(blocks):
            count = (i + 1) * block
            here = slice(i * block, count)
            q, k, v = rot[0, here, lanes], rot[1, :count, lanes], rot[2, :count, lanes]
            do = aq[here, lanes].astype(low)
            s = kdot(q, k, ((1,), (1,))) * scale
            row = lax.broadcasted_iota(jnp.int32, (block, count), 0) + i * block
            col = lax.broadcasted_iota(jnp.int32, (block, count), 1)
            s = jnp.where(col <= row, s, neg_large)
            p = jnp.exp(s - jnp.max(s, axis=-1, keepdims=True))
            p = p * (1.0 / jnp.sum(p, axis=-1, keepdims=True))
            dp = kdot(do, v, ((1,), (1,)))
            delta = jnp.sum(p * dp, axis=-1, keepdims=True)
            dscore = (p * (dp - delta)).astype(low)
            av[:count, lanes] += kdot(p.astype(low), do, ((0,), (0,)))
            ak[:count, lanes] += kdot(dscore, q, ((0,), (0,))) * scale
            aq[here, lanes] = kdot(dscore, k) * scale

    def unturn(i, _):
        d, side = i // 2, i % 2
        at = pl.multiple_of(d * tokens + side * half, half)
        to = pl.multiple_of(jnp.where(side == 0, d, 2 * nc - 1 - d) * half, half)
        cosine, sine = cos_ref[ds(at, half), :], sin_ref[ds(at, half), :]
        for j, acc, scale_ref, sums in ((0, aq, rq, cq), (1, ak, rk, ck)):
            row_sum = jnp.zeros((half, 1), exact)
            for h in range(heads):
                lanes = slice(h * hs, (h + 1) * hs)
                lane = j * cols + h * hs
                v = acc[ds(to, half), lanes]
                v = v * cosine - pltpu.roll(v, hs // 2, 1) * sine
                acc[ds(to, half), lanes] = v
                normed = raw[ds(at, half), lane : lane + hs] * scale_ref[ds(at, half), :]
                v = v * normed
                gsum[j : j + 1, lanes] += jnp.sum(v, axis=0, keepdims=True)
                gain = gain_ref[1 + j : 2 + j, ds(pl.multiple_of(c * cols + h * hs, hs), hs)]
                row_sum += jnp.sum(v * gain, axis=-1, keepdims=True)
            sums[ds(at, half), :] = jnp.broadcast_to(row_sum, (half, hs))
        return 0

    lax.fori_loop(0, 2 * nc, unturn, 0)
    lane8 = lax.broadcasted_iota(jnp.int32, (8, hs), 1)

    def gather_sums(i, _):
        at = pl.multiple_of(i * block, block)
        part = jnp.zeros((8, block), exact)
        for row, src in ((0, cq), (1, ck)):
            sel = jnp.where((row8 == row) & (lane8 == 0), 1.0, 0.0)
            part += kdot(sel, src[ds(at, block), :], ((1,), (1,)), best)
        stat[c, :, ds(at, block)] = part
        return 0

    lax.fori_loop(0, blocks, gather_sums, 0)
    stats = [links.send(stat.at[c], stat.at[c], ctx=c ^ d) for d in range(1, nc)]

    for copy in rows_side:
        links.arrived(copy)
    tile = width // nc
    tile_base = links.local_count
    links.local_count += nc

    def tile_load(k):
        return pltpu.make_async_copy(
            a1_ref.at[:, ds(k * tile, tile)], a1.at[lax.rem(k, 2)], locals_.at[tile_base + k]
        )

    tile_load(0).start()

    def out_tile(k, _):
        at = pl.multiple_of(k * tile, tile)
        v = kdot(ob[...], datt[:, ds(at, tile)], ((0,), (0,))).astype(low)
        go[:, :, ds(at, tile)] = v.reshape(nz, rows_w, tile)
        return 0

    lax.fori_loop(0, nc, out_tile, 0)
    for copy in stats:
        links.arrived(copy)
    summed = stat[0]
    for k in range(1, nc):
        summed += stat[k]
    total[...] = summed
    columns(total, cq, ck, lambda v: v)

    def finish(i, _):
        d, side = i // 2, i % 2
        at = pl.multiple_of(d * tokens + side * half, half)
        to = pl.multiple_of(jnp.where(side == 0, d, 2 * nc - 1 - d) * half, half)
        for j, acc, scale_ref, sums in ((0, aq, rq, cq), (1, ak, rk, ck)):
            for h in range(heads):
                lanes = slice(h * hs, (h + 1) * hs)
                lane = j * cols + h * hs
                gain = gain_ref[1 + j : 2 + j, ds(pl.multiple_of(c * cols + h * hs, hs), hs)]
                normed = raw[ds(at, half), lane : lane + hs] * scale_ref[ds(at, half), :]
                v = acc[ds(to, half), lanes] * gain - normed * sums[ds(at, half), :]
                dqkv[ds(at, half), lane : lane + hs] = (v * scale_ref[ds(at, half), :]).astype(low)
        dqkv[ds(at, half), 2 * cols : 3 * cols] = av[ds(to, half), :].astype(low)
        return 0

    lax.fori_loop(0, 2 * nc, finish, 0)
    for copy in later:
        links.left(copy)
    for copy in list(rows_same.values()) + rows_side:
        links.left(copy)

    def w_tile(k, _):
        @pl.when(k + 1 < nc)
        def _():
            tile_load(k + 1).start()

        tile_load(k).wait()
        v = kdot(a1[lax.rem(k, 2)], dqkv[...], ((0,), (0,))).astype(low)
        for j in range(3):
            gw[j, k] = v[:, j * cols : (j + 1) * cols].reshape(nz, rows_w, cols)
        return 0

    lax.fori_loop(0, nc, w_tile, 0)
    home = {}

    def send_home(j, s):
        peer = z ^ (s & -s)
        home[j, s] = [links.send(gw.at[j, :, z ^ s], wz_land.at[s, j], fsdp=peer)]
        if j == 2:
            home[j, s].append(links.send(go.at[z ^ s], oz_land.at[s], fsdp=peer))

    def taken(j, s):
        w_sum = gw[j, :, z ^ s].astype(exact)
        o_sum = go[z ^ s].astype(exact) if j == 2 else None
        bit = 1
        while bit < nz and (s == 0 or bit < (s & -s)):
            for copy in home[j, s | bit]:
                links.arrived(copy)
            got = [links.move(wz_land.at[s | bit, j], wtemp.at[j])]
            if j == 2:
                got.append(links.move(oz_land.at[s | bit], otemp))
            for copy in got:
                links.left(copy)
            w_sum += wtemp[j].astype(exact)
            if j == 2:
                o_sum += otemp[...].astype(exact)
            bit *= 2
        return w_sum, o_sum

    for j in range(3):
        for s in range(nz - 1, 0, -1):
            if s & 1:
                send_home(j, s)

    def partial(k):
        at = pl.multiple_of(k * tokens, tokens)
        v = jnp.zeros((tokens, width), exact)
        for j in range(3):
            v += kdot(dqkv[ds(at, tokens), j * cols : (j + 1) * cols], w[j], ((1,), (1,)))
        datt[ds(at, tokens), :] = v.astype(low)

    def rows_of(k):
        return datt.at[ds(pl.multiple_of(k * tokens, tokens), tokens)]

    evens = [0] + same
    pair, chip = {}, {}

    def other_core(m, _):
        partial(2 * m + 1 - lax.rem(c, 2))
        return 0

    def this_core(m, _):
        partial(2 * m + lax.rem(c, 2))
        return 0

    lax.fori_loop(0, nc // 2, other_core, 0)
    for m, d in enumerate(evens):
        pair[d] = links.send(rows_of((c ^ 1) ^ d), pair_land.at[m], ctx=c ^ 1)
    lax.fori_loop(0, nc // 2, this_core, 0)
    for m, d in list(enumerate(evens))[::-1]:
        links.arrived(pair[d])
        got = links.move(pair_land.at[m], xtemp)
        links.left(got)
        mine = rows_of(c ^ d)
        if d:
            mine[...] = (mine[...].astype(exact) + xtemp[...].astype(exact)).astype(low)
            chip[d] = links.send(mine, chip_land.at[m], ctx=c ^ d)
        else:
            grad_in = mine[...].astype(exact) + xtemp[...].astype(exact)
            hidden_out[...] = grad_in

    for j in range(3):
        for s in range(nz - 2, 0, -1):
            if not s & 1:
                w_sum, o_sum = taken(j, s)
                gw[j, :, z ^ s] = w_sum.astype(low)
                if j == 2:
                    go[z ^ s] = o_sum.astype(low)
                send_home(j, s)

    for m, d in enumerate(evens):
        if d:
            links.arrived(chip[d])
            got = links.move(chip_land.at[m], xtemp)
            links.left(got)
            hidden_out[...] += xtemp[...].astype(exact)
    x = xrow[...].astype(exact)
    rs = lax.rsqrt(jnp.mean(x * x, axis=-1, keepdims=True) + epsilon)
    n1 = x * rs
    grad_in = hidden_out[...]
    gains_out[...] = jnp.zeros_like(gains_out)
    gains_out[0:1, :] = jnp.sum(grad_in * n1, axis=0, keepdims=True)
    for j in range(2):
        own_lanes = ds(pl.multiple_of(c * cols, cols), cols)
        gains_out[1 + j : 2 + j, own_lanes] = gsum[j : j + 1, :]
    gains_out[3:4, :] = fgain_ref[0:1, :]
    dn = grad_in * gain_ref[0:1, :]
    hidden_out[...] = dr1_ref[...] + rs * (dn - n1 * jnp.mean(dn * n1, axis=-1, keepdims=True))

    small_z[0] = gains_out[...]
    z_sums = [links.send(small_z.at[0], small_z.at[s], fsdp=z ^ s) for s in range(1, nz)]
    for j in range(3):
        w_sum, o_sum = taken(j, 0)
        if j == 2:
            wo_out[...] = o_sum
        wsum[j] = w_sum.astype(low)
    w_home = [links.send(wsum.at[:, c ^ d], wl.at[:, c], ctx=c ^ d) for d in range(1, nc)]
    w_own = links.move(wsum.at[:, c], wl.at[:, c])
    for copy in z_sums:
        links.arrived(copy)
    v = small_z[0]
    for s in range(1, nz):
        v += small_z[s]
    small_c[0] = v
    c_sums = [links.send(small_c.at[0], small_c.at[d], ctx=c ^ d) for d in range(1, nc)]
    for copy in w_home:
        links.arrived(copy)
    links.left(w_own)
    for j in range(3):
        for k in range(nc):
            w_out[j, :, k * cols : (k + 1) * cols] = wl[j, k].astype(exact)
    for copy in c_sums:
        links.arrived(copy)
    v = small_c[0]
    for d in range(1, nc):
        v += small_c[d]
    gains_out[...] = v
    for copy in up_sends:
        links.arrived(copy)
    links.close()


def run_back(cfg, x, dr1, datt, a1, w, raw, stat, rot, ob, wo, gains, fgain, gu, cosine, sine):
    nc, nz, tokens, width = cfg["nc"], cfg["nz"], cfg["tokens"], cfg["width"]
    cols, rows_w, length = cfg["cols"], cfg["rows_w"], cfg["length"]
    shape = jax.ShapeDtypeStruct
    any_, vmem = pl.BlockSpec(memory_space=pl.ANY), pl.BlockSpec(memory_space=pltpu.VMEM)
    outs = [
        (shape((tokens, width), exact), vmem),
        (shape((3, rows_w, width), exact), vmem),
        (shape((rows_w, width), exact), vmem),
        (shape((8, width), exact), vmem),
        (shape(gu.shape, low), any_),
        (shape((nc // 2, tokens, width), low), any_),
        (shape((nc // 2, tokens, width), low), any_),
        (shape((nz, 3, nc, rows_w, cols), low), any_),
        (shape((nz, rows_w, width), low), any_),
    ]
    scratch = [
        pltpu.VMEM((width, width), low),
        pltpu.VMEM((length, width), low),
        pltpu.VMEM((2, length, width // nc), low),
        pltpu.VMEM((3, width, cols), low),
        pltpu.VMEM((length, 2 * cols), exact),
        pltpu.VMEM((3, length, cols), low),
        pltpu.VMEM((length, cols), low),
        pltpu.VMEM((nc, tokens, cols), low),
        pltpu.VMEM((length, cols), exact),
        pltpu.VMEM((length, cols), exact),
        pltpu.VMEM((length, cols), exact),
        pltpu.VMEM((length, 128), exact),
        pltpu.VMEM((length, 128), exact),
        pltpu.VMEM((length, 128), exact),
        pltpu.VMEM((length, 128), exact),
        pltpu.VMEM((nc, 8, length), exact),
        pltpu.VMEM((8, length), exact),
        pltpu.VMEM((length, 3 * cols), low),
        pltpu.VMEM((3, nc, nz, rows_w, cols), low),
        pltpu.VMEM((nz, rows_w, width), low),
        pltpu.VMEM((8, cols), exact),
        pltpu.VMEM((3, nc, rows_w, cols), low),
        pltpu.VMEM((rows_w, width), low),
        pltpu.VMEM((3, nc, rows_w, cols), low),
        pltpu.VMEM((3, nc, rows_w, cols), low),
        pltpu.VMEM((tokens, width), low),
        pltpu.VMEM((tokens, width), low),
        pltpu.VMEM((nz, 8, width), exact),
        pltpu.VMEM((nc, 8, width), exact),
        pltpu.SemaphoreType.DMA((8 * nc + 8 * nz,)),
        pltpu.SemaphoreType.DMA((8 * nc + 8 * nz,)),
        pltpu.SemaphoreType.DMA((4 * nc + 8 * nz + 16,)),
    ]
    return pl.pallas_call(
        functools.partial(back_kernel, cfg),
        out_shape=[o[0] for o in outs],
        in_specs=[any_, vmem, any_, any_, any_, any_, vmem, any_, any_, any_, vmem, vmem, any_, vmem, vmem],
        out_specs=[o[1] for o in outs],
        scratch_shapes=scratch,
        compiler_params=pltpu.CompilerParams(
            collective_id=2, has_side_effects=True, vmem_limit_bytes=cfg["vmem"]
        ),
        name="back",
    )(x, dr1, datt, a1, w, raw, stat, rot, ob, wo, gains, fgain, gu, cosine, sine)


def tables(nc, tokens, head_size):
    half = tokens // 2
    local = np.arange(tokens)
    device = np.arange(nc)[:, None]
    position = np.where(
        local < half, device * half + local, (2 * nc - 1 - device) * half + local - half
    ).reshape(-1)
    freq = np.float32(10000.0) ** (-np.arange(head_size // 2, dtype=np.float32) * (2.0 / head_size))
    angle = position.astype(np.float32)[:, None] * freq.astype(np.float32)
    cosine = np.concatenate([np.cos(angle), np.cos(angle)], axis=1)
    sine = np.concatenate([-np.sin(angle), np.sin(angle)], axis=1)
    return jnp.asarray(cosine, exact), jnp.asarray(sine, exact)


def body(
    hidden_in,
    cotangent,
    routes,
    attn_gain,
    query_gain,
    key_gain,
    ffn_gain,
    w_query,
    w_key,
    w_value,
    w_out,
    w_router,
    w_gate,
    w_up,
    w_down,
):
    tokens = hidden_in.shape[1]
    width = hidden_in.shape[2]
    head_size = width // HEADS
    ctx_count = lax.axis_size("ctx")
    z_count = lax.axis_size("fsdp")
    both = ("ctx", "fsdp")
    top = routes.shape[2]
    exp_local = w_gate.shape[0]
    split = z_count // exp_local
    hidden = w_gate.shape[2]
    part = hidden // split
    experts = exp_local * ctx_count
    capacity = tokens * top * 4 // (3 * experts)
    cols = HEADS // ctx_count * head_size
    length = tokens * ctx_count
    c_index = lax.axis_index("ctx")
    z_index = lax.axis_index("fsdp")
    rows_w = w_query.shape[0]

    cfg = dict(
        nc=ctx_count,
        nz=z_count,
        tokens=tokens,
        width=width,
        cols=cols,
        rows_w=rows_w,
        length=length,
        cap=capacity,
        top=top,
        exp_local=exp_local,
        split=split,
        block=math.gcd(length, 256 if length <= 2048 else 128),
        chunk=math.gcd(length, 64),
        copies=(ctx_count - 1) * (8 + 2 * z_count) + (z_count - 1) * 12 + 2 * ctx_count + 8,
        part=part,
        vmem=62 * 2**20,
    )
    index = c_index * z_count + z_index
    per = 128 // rows_w
    gains = jnp.stack([attn_gain, query_gain, key_gain, ffn_gain]).astype(exact)
    gains = lax.dynamic_update_slice(
        jnp.zeros((8, 128), exact), gains, (0, jnp.mod(index, per) * rows_w)
    )
    router_tile = jnp.pad(w_router, ((0, 0), (0, 128 - experts)))
    route_tile = jnp.pad(routes[0].T, ((0, 8 - top), (0, 0)), constant_values=-1)

    def pieces_of(weight):
        rows = weight.shape[1]
        weight = weight.reshape(exp_local, rows, z_count, split, part // z_count)
        return weight.transpose(0, 3, 1, 2, 4).reshape(z_count, rows, part)

    down_pieces = w_down.reshape(z_count, -1, width)
    cosine, sine = tables(ctx_count, tokens, head_size)
    (
        attn_all, w_full, raw, squares, rot, out_heads, wo_full, resid_one,
        router_full, gains, routes_all, gate_full, up_full, down_full, cot_rows, cot_near,
        input_rows, input_near, *_,
    ) = front(
        cfg, hidden_in[0], w_query, w_key, w_value, w_out, gains, router_tile, route_tile,
        cotangent[0], pieces_of(w_gate), pieces_of(w_up), down_pieces,
        cosine, sine,
    )
    gate_full = gate_full.reshape(-1, part)
    up_full = up_full.reshape(-1, part)
    ffn_input = input_near[0]
    router_t = router_full.reshape(width, 128).T
    (
        resid_two, grad_one, attn_grad_low, logit_grad, ffn_gain_grad, down_land, gate_land,
        up_grad, *_,
    ) = run_experts(
        cfg, input_rows.reshape(-1, width), cot_rows.reshape(-1, width), router_t, routes_all,
        gate_full, up_full, down_full, down_pieces, input_near, cot_near, resid_one, gains,
    )
    out_hidden = resid_two[None]
    router_grad = lax.dot_general(
        ffn_input, logit_grad[:experts], (((0,), (1,)), ((), ())), preferred_element_type=exact
    )

    def whole_out(grad):
        grad = grad.reshape(exp_local, split, -1, z_count, part // z_count)
        return grad.transpose(0, 2, 3, 1, 4).reshape(exp_local, -1, hidden).astype(exact)

    grad_down = down_land.reshape(exp_local, -1, width).astype(exact)
    grad_gate = whole_out(gate_land)
    grad_hidden, w_grads, grad_out, gain_grads, up_land, *_ = run_back(
        cfg, hidden_in[0], grad_one, attn_grad_low, attn_all, w_full.reshape(3, width, cols), raw,
        squares, rot, out_heads, wo_full.reshape(width, width), gains, ffn_gain_grad,
        up_grad.reshape(z_count, -1, part), cosine, sine,
    )
    grad_up = whole_out(up_land)
    gain_grads = lax.dynamic_slice_in_dim(gain_grads, index * rows_w, rows_w, 1)
    sums = router_grad.reshape(ctx_count * z_count, rows_w * experts)
    sums = jnp.sum(exchange(sums, both), axis=0)
    return (
        out_hidden,
        grad_hidden[None],
        gain_grads[0],
        gain_grads[1],
        gain_grads[2],
        gain_grads[3],
        w_grads[0],
        w_grads[1],
        w_grads[2],
        grad_out,
        sums.reshape(rows_w, experts),
        grad_gate,
        grad_up,
        grad_down,
    )


def solution(mesh):
    in_specs = (
        P("fsdp", "ctx", None),
        P("fsdp", "ctx", None),
        P("fsdp", "ctx", None),
        P(("ctx", "fsdp")),
        P(("ctx", "fsdp")),
        P(("ctx", "fsdp")),
        P(("ctx", "fsdp")),
        P(("ctx", "fsdp"), None),
        P(("ctx", "fsdp"), None),
        P(("ctx", "fsdp"), None),
        P(("ctx", "fsdp"), None),
        P(("ctx", "fsdp"), None),
        P("ctx", "fsdp", None),
        P("ctx", "fsdp", None),
        P("ctx", "fsdp", None),
    )
    out_specs = (
        P("fsdp", "ctx", None),
        P("fsdp", "ctx", None),
        P(("ctx", "fsdp")),
        P(("ctx", "fsdp")),
        P(("ctx", "fsdp")),
        P(("ctx", "fsdp")),
        P(("ctx", "fsdp"), None),
        P(("ctx", "fsdp"), None),
        P(("ctx", "fsdp"), None),
        P(("ctx", "fsdp"), None),
        P(("ctx", "fsdp"), None),
        P("ctx", "fsdp", None),
        P("ctx", "fsdp", None),
        P("ctx", "fsdp", None),
    )
    return jax.shard_map(body, mesh=mesh, in_specs=in_specs, out_specs=out_specs, check_vma=False)
```
